128 devices in a mesh: stream: 8 (over z, core), radial: 4 (over x), azim: 4 (over y).
Axes of the slice: x: 4, y: 4, z: 4, core: 2. Of those that a mesh axis runs over, the one named last changes fastest.
Arguments:
- component_fractions: float32 [53, 64, 32, 512], P(None, 'stream', 'radial', 'azim'), may hold values from 0 to 1
- kilokelvin_field: float32 [64, 32, 512], P('stream', 'radial', 'azim'), may hold values from 1 to 2.5
- axial_courant_number: float32 [64, 32, 512], P('stream', 'radial', 'azim'), may hold values from 0.1 to 0.4
- spreading_number: float32 [54], replicated, may hold values from 0.01 to 0.08
- arrhenius_multiplier_exponent: float32 [325], replicated, may hold values from -1 to 1
- thermal_exponents: float32 [325], replicated, may hold values from -1 to 1
- arrhenius_barrier: float32 [325], replicated, may hold values from 0 to 2
- balance_constant_exponents: float32 [325], replicated, may hold values from -2 to 2
- enthalpy_formation: float32 [53], replicated, may hold values from -0.3 to 0.3
- consumed_stoich_matrix: float32 [53, 325], replicated
- yield_stoich_matrix: float32 [53, 325], replicated
- processor_tiles_burning: int32 [128, 64], P(('stream', 'radial', 'azim')), may hold values from 0 to 63, as said below
- tile_transfer_tally: int32 [128, 128], P(('stream', 'radial', 'azim')), may hold values from 0 to 1, as said below
Outputs:
- species_out: float32 [53, 64, 32, 512], P(None, 'stream', 'radial', 'azim')
- temperature_out: float32 [64, 32, 512], P('stream', 'radial', 'azim')
The draws below stay inside these ranges and needn't reach their ends.
Inputs may be any that keep to these rules, and one draw needn't show every extreme that they name: `processor_tiles_burning`: each row is a permutation of 0 to 63; the first c entries of row d are device d's flame blocks, c the sum of row d of tile_transfer_tally. Row sums lie in 0 to 64, one row sums to exactly 64; an entry is at most 1, reached in every draw; every column sums to exactly 24. Device d's flame blocks go to devices in increasing order: the first tile_transfer_tally[d, 0] of them to device 0, the next tile_transfer_tally[d, 1] to device 1, and so on.
All inputs are finite; a program needn't handle non-finite values.
Results may differ from the reference program's by a relative error of at most 0.0001.
Values sent between devices are 32-bit elements; how exact they have to be, the bound alone decides.
A program may use at most 128 MiB of HBM per device.

```python
import math
import jax
import jax.numpy as jnp
from jax import lax

S = 53
RXN_TOTAL = 325
CX = 8
CY = 8
CZ = 128
NCYC = 4
SUBSTEPS = 2
BLK_DEV = 64
FLAME_DEV = 24
AXIAL_ZONES = 64
SPOKE_ZONES = 32
ANGULAR_ZONES = 512
N_STREAM = 8
N_RADIAL = 4
N_AZIM = 4
DEVICES = 128


def flame_layout(key):
    key = jax.random.fold_in(key, 5)
    first, second, third, fourth = jax.random.split(key, 4)
    half = (DEVICES - 4) // 2
    swing = jax.random.randint(first, (half,), 0, FLAME_DEV + 1).astype(jnp.int32)
    excess = BLK_DEV - FLAME_DEV
    special = jnp.array([BLK_DEV, FLAME_DEV - excess // 2, FLAME_DEV - excess + excess // 2, FLAME_DEV], jnp.int32)
    ordered = jnp.concatenate([special, FLAME_DEV + swing, FLAME_DEV - swing])
    placed = jax.random.permutation(second, DEVICES)
    counts = jnp.zeros((DEVICES,), jnp.int32).at[placed].set(ordered)
    lists = jax.vmap(lambda sub: jax.random.permutation(sub, BLK_DEV))(jax.random.split(third, DEVICES)).astype(jnp.int32)
    offsets = jnp.cumsum(counts) - counts
    order = jax.random.permutation(fourth, DEVICES).astype(jnp.int32)
    position = (offsets[:, None] + jnp.arange(BLK_DEV, dtype=jnp.int32)[None, :]) % DEVICES
    target = order[position]
    live = jnp.arange(BLK_DEV, dtype=jnp.int32)[None, :] < counts[:, None]
    hits = (target[:, :, None] == jnp.arange(DEVICES, dtype=jnp.int32)[None, None, :]) & live[:, :, None]
    per_peer = jnp.sum(hits.astype(jnp.int32), 1)
    return (lists, per_peer)


def stoich_table(key):
    first, second, third = jax.random.split(key, 3)
    chosen = jax.random.randint(first, (RXN_TOTAL,), 0, S)
    primary = (jnp.arange(S)[:, None] == chosen[None, :]).astype(jnp.float32)
    extra = (jax.random.randint(second, (S, RXN_TOTAL), 0, 100) < 3).astype(jnp.float32)
    double = (jax.random.randint(third, (S, RXN_TOTAL), 0, 5) == 0).astype(jnp.float32)
    return primary + extra * (1.0 + double)


def draw_consumed_stoich_matrix(key, part):
    key = jax.random.fold_in(key, 11)
    return stoich_table(key)


def draw_yield_stoich_matrix(key, part):
    key = jax.random.fold_in(key, 23)
    return stoich_table(key)


def draw_processor_tiles_burning(key, part):
    return flame_layout(key)[0]


def draw_tile_transfer_tally(key, part):
    return flame_layout(key)[1]


def block_scale(rng, extent, pieces, least, largest):
    level, own = 1.0, jax.random.fold_in(rng, 6)
    for dim, blocks in pieces:
        heights = jnp.exp(jax.random.uniform(jax.random.fold_in(own, dim), (blocks,), jnp.float32, least / len(pieces), largest / len(pieces)))
        level = level * jnp.repeat(heights, extent[dim] // blocks).reshape([-1 if axis == dim else 1 for axis in range(len(extent))])
    return level


def bell_draw(stream_key, extent, scale, reach, held_as=jnp.bfloat16):
    entries = scale * jax.random.normal(stream_key, extent, jnp.float32)
    return jnp.clip(entries, min=-reach, max=reach).astype(held_as)


def setup_inputs(seed: int = 0) -> dict:
    splits = jax.random.split(jax.random.key(seed), 14)
    component_fractions = jnp.clip(1.0 * jax.random.uniform(splits[0], (S, AXIAL_ZONES, SPOKE_ZONES, ANGULAR_ZONES), jnp.float32) ** block_scale(splits[0], (S, AXIAL_ZONES, SPOKE_ZONES, ANGULAR_ZONES), ((1, 8), (2, 4), (3, 4)), -0.2, 0.2), 0.0, 1.0)
    kilokelvin_field = jnp.clip(1.0 + 1.5 * jax.random.uniform(splits[1], (AXIAL_ZONES, SPOKE_ZONES, ANGULAR_ZONES), jnp.float32) ** block_scale(splits[1], (AXIAL_ZONES, SPOKE_ZONES, ANGULAR_ZONES), ((0, 8), (1, 4), (2, 4)), -0.2, 0.2), 1.0, 2.5)
    axial_courant_number = jnp.clip(0.1 + 0.3 * jax.random.uniform(splits[2], (AXIAL_ZONES, SPOKE_ZONES, ANGULAR_ZONES), jnp.float32) ** block_scale(splits[2], (AXIAL_ZONES, SPOKE_ZONES, ANGULAR_ZONES), ((0, 8), (1, 4), (2, 4)), -0.2, 0.2), 0.1, 0.4)
    spreading_number = jnp.clip(jnp.exp(jax.random.uniform(splits[3], (S + 1,), jnp.float32, math.log(0.01), math.log(0.08))), 0.01, 0.08)
    arrhenius_multiplier_exponent = jnp.clip(jax.random.uniform(splits[4], (RXN_TOTAL,), jnp.float32, -1.0, 1.0), -1.0, 1.0)
    thermal_exponents = jnp.clip(jax.random.uniform(splits[5], (RXN_TOTAL,), jnp.float32, -1.0, 1.0), -1.0, 1.0)
    arrhenius_barrier = jnp.clip(jax.random.uniform(splits[6], (RXN_TOTAL,), jnp.float32, 0.0, 2.0), 0.0, 2.0)
    balance_constant_exponents = jnp.clip(jax.random.uniform(splits[7], (RXN_TOTAL,), jnp.float32, -2.0, 2.0), -2.0, 2.0)
    enthalpy_formation = bell_draw(splits[8], (S,), 0.05, 0.3, jnp.float32)
    consumed_stoich_matrix = draw_consumed_stoich_matrix(jax.random.fold_in(splits[13], 71), 0)
    yield_stoich_matrix = draw_yield_stoich_matrix(jax.random.fold_in(splits[13], 71), 0)
    processor_tiles_burning = draw_processor_tiles_burning(jax.random.fold_in(splits[13], 71), 0)
    tile_transfer_tally = draw_tile_transfer_tally(jax.random.fold_in(splits[13], 71), 0)
    return {"component_fractions": component_fractions, "kilokelvin_field": kilokelvin_field, "axial_courant_number": axial_courant_number, "spreading_number": spreading_number, "arrhenius_multiplier_exponent": arrhenius_multiplier_exponent, "thermal_exponents": thermal_exponents, "arrhenius_barrier": arrhenius_barrier, "balance_constant_exponents": balance_constant_exponents, "enthalpy_formation": enthalpy_formation, "consumed_stoich_matrix": consumed_stoich_matrix, "yield_stoich_matrix": yield_stoich_matrix, "processor_tiles_burning": processor_tiles_burning, "tile_transfer_tally": tile_transfer_tally}


chem_step = 0.02
mass_offset = 0.05


def chemistry(rows, kinetic_settings):
    consumed_stoich_matrix, yield_stoich_matrix, arrhenius_multiplier_exponent, thermal_exponents, arrhenius_barrier, balance_constant_exponents, enthalpy_formation = kinetic_settings
    fine = lax.Precision.HIGHEST
    nspec = consumed_stoich_matrix.shape[0]
    mass = rows[:, :nspec]
    thermal_scratch = rows[:, nspec]
    for cycle in range(NCYC):
        logc = jnp.log(mass + mass_offset)
        natural_log_kilokelvin = jnp.log(thermal_scratch)
        starting_point = arrhenius_multiplier_exponent[None, :, None] + thermal_exponents[None, :, None] * natural_log_kilokelvin[:, None, :] - arrhenius_barrier[None, :, None] / thermal_scratch[:, None, :]
        forward = jnp.exp(starting_point + jnp.einsum("sr,ksw->krw", consumed_stoich_matrix, logc, precision=fine))
        backward = jnp.exp(starting_point - balance_constant_exponents[None, :, None] + jnp.einsum("sr,ksw->krw", yield_stoich_matrix, logc, precision=fine))
        made = jnp.einsum("sr,krw->ksw", yield_stoich_matrix, forward, precision=fine) + jnp.einsum("sr,krw->ksw", consumed_stoich_matrix, backward, precision=fine)
        lost = jnp.einsum("sr,krw->ksw", consumed_stoich_matrix, forward, precision=fine) + jnp.einsum("sr,krw->ksw", yield_stoich_matrix, backward, precision=fine)
        mass = (mass + chem_step * made) / (1.0 + chem_step * lost / (mass + mass_offset))
        thermal_scratch = thermal_scratch * jnp.exp(chem_step * jnp.einsum("s,ksw->kw", enthalpy_formation, made - lost, precision=fine))
    return jnp.concatenate([mass, thermal_scratch[:, None, :]], 1)


def transport(fluid_fields, axial_courant_number, spreading_number):
    padded = jnp.pad(fluid_fields, ((0, 0), (1, 1), (1, 1), (0, 0)))
    padded = jnp.concatenate([padded[..., -1:], padded, padded[..., :1]], -1)
    centre = padded[:, 1:-1, 1:-1, 1:-1]
    beside_all = padded[:, 2:, 1:-1, 1:-1] + padded[:, :-2, 1:-1, 1:-1]
    beside_all = beside_all + padded[:, 1:-1, 2:, 1:-1] + padded[:, 1:-1, :-2, 1:-1]
    beside_all = beside_all + padded[:, 1:-1, 1:-1, 2:] + padded[:, 1:-1, 1:-1, :-2]
    rate = spreading_number[:, None, None, None]
    return (1.0 - 6.0 * rate - axial_courant_number) * centre + rate * beside_all + axial_courant_number * padded[:, :-2, 1:-1, 1:-1]


def to_devices(fluid_fields):
    nvar = fluid_fields.shape[0]
    shaped = fluid_fields.reshape(nvar, N_STREAM, CX, N_RADIAL, CY, N_AZIM, CZ)
    return shaped.transpose(1, 3, 5, 0, 2, 4, 6).reshape(N_STREAM * N_RADIAL * N_AZIM, nvar, CX * CY, CZ)


def from_devices(local):
    nvar = local.shape[1]
    shaped = local.reshape(N_STREAM, N_RADIAL, N_AZIM, nvar, CX, CY, CZ)
    return shaped.transpose(3, 0, 4, 1, 5, 2, 6).reshape(nvar, CX * N_STREAM, CY * N_RADIAL, CZ * N_AZIM)


def reference(component_fractions, kilokelvin_field, axial_courant_number, spreading_number, arrhenius_multiplier_exponent, thermal_exponents, arrhenius_barrier, balance_constant_exponents, enthalpy_formation, consumed_stoich_matrix, yield_stoich_matrix, processor_tiles_burning, tile_transfer_tally):
    nspec = component_fractions.shape[0]
    kinetic_settings = (consumed_stoich_matrix, yield_stoich_matrix, arrhenius_multiplier_exponent, thermal_exponents, arrhenius_barrier, balance_constant_exponents, enthalpy_formation)
    fluid_fields = jnp.concatenate([component_fractions, kilokelvin_field[None]], 0)
    counts = jnp.sum(tile_transfer_tally, 1)
    alive = jnp.arange(processor_tiles_burning.shape[1])[None, :] < counts[:, None]

    def one_device(item):
        flat, blocks, live = item
        rows = jnp.moveaxis(jnp.take(flat, blocks, axis=1), 1, 0)
        done = chemistry(rows, kinetic_settings)
        updated = jnp.where(live[:, None, None], done, rows)
        return flat.at[:, blocks].set(jnp.moveaxis(updated, 0, 1))

    for substep in range(SUBSTEPS):
        fluid_fields = transport(fluid_fields, axial_courant_number, spreading_number)
        local = lax.map(one_device, (to_devices(fluid_fields), processor_tiles_burning, alive))
        fluid_fields = from_devices(local)
    return fluid_fields[:nspec], fluid_fields[nspec]
```

```python
import functools

import jax
import jax.numpy as jnp
from jax import lax
from jax.experimental import pallas as pl
from jax.experimental.pallas import tpu as pltpu
from jax.sharding import PartitionSpec as P

NCYC = 4
ROWS = 56
GROUP = 8
chem_step = 0.02
mass_offset = 0.05
LOG2E = 1.4426950408889634
F32 = jnp.float32
BF16 = jnp.bfloat16
MESH = pl.DeviceIdType.MESH
AXES = ("stream", "radial", "azim")
LIMIT = 50 * 2**20


def halves(value):
    high = lax.reduce_precision(value, 8, 7)
    low = lax.reduce_precision(value - high, 8, 7)
    return high.astype(BF16), low.astype(BF16)


def weights(consumed, made, exponent, thermal, barrier, balance, enthalpy):
    nspec, nrxn = consumed.shape
    padded = -(-nrxn // 8) * 8

    def columns(table, constant):
        rows = [table, thermal[None], -LOG2E * barrier[None], LOG2E * constant[None]]
        return jnp.pad(jnp.concatenate(rows, 0), ((0, 0), (0, padded - nrxn)))

    ahead = columns(consumed, exponent)
    back = columns(made, exponent - balance)
    high, low = halves(jnp.concatenate([ahead, back], 1).T)
    rates = jnp.concatenate([high, high, low, high], 1)
    heat = LOG2E * jnp.sum(enthalpy[:, None] * (made - consumed), 0, keepdims=True)

    def stack(gain, loss, warm):
        rows = [gain, warm, jnp.zeros((2, nrxn), F32), loss, jnp.zeros((3, nrxn), F32)]
        return jnp.pad(jnp.concatenate(rows, 0), ((0, 0), (0, padded - nrxn)))

    both = jnp.concatenate([stack(made, consumed, heat), stack(consumed, made, -heat)], 1)
    high, low = halves(chem_step * both)
    return rates, jnp.concatenate([high, low], 0)


def parted(value):
    high = value.astype(BF16)
    return high, value - high.astype(F32)


def product(a, b):
    return lax.dot_general(a, b, (((1,), (0,)), ((), ())), preferred_element_type=F32)


def cycle(state, rates, sums):
    row = lax.broadcasted_iota(jnp.int32, state.shape, 0)
    moved = state + jnp.where(row < 53, mass_offset, jnp.where(row == 53, 0.0, 1.0))
    heat = state[53:54]
    logs = jnp.log2(moved)
    logs = jnp.where(row == 54, 1.0 / heat, jnp.where(row == 55, 1.0, logs))
    first, rest = parted(logs)
    second, third = parted(rest)
    first, second = first.astype(F32), second.astype(F32)
    stacked = jnp.concatenate([first, second, first, third], 0).astype(BF16)
    flux = jnp.exp2(product(rates, stacked))
    high, low = parted(flux)
    half = sums.shape[0] // 2
    both = product(sums, high)
    total = both[:half] + both[half:] + product(sums[:half], low.astype(BF16))
    gain, loss = total[:ROWS], total[ROWS:]
    species = (state + gain) * moved / (moved + loss)
    return jnp.where(row == 53, heat * jnp.exp2(gain[53:54]), species)


def chem_kernel(last, blocks_ref, tally_ref, state_ref, rates_ref, sums_ref, *outs):
    count = jnp.sum(tally_ref[...])
    work = outs[-1]
    work[...] = state_ref[...]

    def group(g, carry):
        at = [blocks_ref[0, g * GROUP + k] for k in range(GROUP)]
        state = jnp.concatenate([work[at[k]] for k in range(GROUP)], 1)
        state = lax.fori_loop(
            0, NCYC, lambda c, s: cycle(s, rates_ref[...], sums_ref[...]), state
        )
        for k in range(GROUP):

            @pl.when(g * GROUP + k < count)
            def _():
                work[at[k]] = state[:, k * 128 : (k + 1) * 128]

        return carry

    lax.fori_loop(0, (count + GROUP - 1) // GROUP, group, 0)
    if last:
        species_ref, heat_ref = outs[:2]

        def put(b, carry):
            species_ref[pl.ds(b, 53, stride=64), :] = work[b, pl.ds(0, 53), :]
            heat_ref[pl.ds(b, 1), :] = work[b, pl.ds(53, 1), :]
            return carry

        lax.fori_loop(0, 64, put, 0)


def react(last, blocks, tally, state, rates, sums):
    vmem = pl.BlockSpec(memory_space=pltpu.VMEM)
    if last:
        shape = [jax.ShapeDtypeStruct((53 * 64, 128), F32), jax.ShapeDtypeStruct((64, 128), F32)]
        scratch = [pltpu.VMEM(state.shape, F32)]
    else:
        shape = [jax.ShapeDtypeStruct(state.shape, F32)]
        scratch = []
    return pl.pallas_call(
        functools.partial(chem_kernel, last),
        out_shape=shape,
        in_specs=[pl.BlockSpec(memory_space=pltpu.SMEM)] + [vmem] * 4,
        out_specs=[vmem] * len(shape),
        scratch_shapes=scratch,
        compiler_params=pltpu.CompilerParams(vmem_limit_bytes=LIMIT),
    )(blocks, tally, state, rates, sums)


def neighbours():
    found = []
    for axis in AXES:
        n, me = lax.axis_size(axis), lax.axis_index(axis)
        found += [{axis: lax.rem(me + n - 1, n)}, {axis: lax.rem(me + 1, n)}]
    return found


def move_kernel(first, *refs):
    if first:
        species_ref, heat_ref, courant_ref, spread_ref, out_ref = refs[:5]
    else:
        state_ref, courant_ref, spread_ref, out_ref = refs[:4]
    grid, edge, halo, send_sem, recv_sem = refs[-5:]
    peers = neighbours()
    barrier = pltpu.get_barrier_semaphore()
    for peer in peers:
        pl.semaphore_signal(barrier, inc=1, device_id=peer, device_id_type=MESH)
    edge[...] = jnp.zeros_like(edge)
    lane = lax.broadcasted_iota(jnp.int32, (ROWS, 128), 1)

    def load(b, carry):
        i, j = b // 8 + 1, b % 8 + 1
        if first:
            grid[i, j, pl.ds(0, 53), :] = species_ref[pl.ds(b, 53, stride=64), :]
            grid[i, j, pl.ds(53, 1), :] = heat_ref[pl.ds(b, 1), :]
            grid[i, j, pl.ds(54, 2), :] = jnp.zeros((2, 128), F32)
            here = grid[i, j]
        else:
            here = state_ref[b]
            grid[i, j] = here
        low, high = carry
        low = jnp.where(lane == b, pltpu.roll(here, b, 1), low)
        high = jnp.where(lane == b, pltpu.roll(here, b + 1, 1), high)
        return low, high

    low, high = lax.fori_loop(0, 64, load, (jnp.zeros((ROWS, 128), F32),) * 2)
    edge[0] = low
    edge[1] = high
    pl.semaphore_wait(barrier, 6)
    inner = pl.ds(1, 8)
    plans = [
        (grid.at[1, inner], grid.at[9, inner]),
        (grid.at[8, inner], grid.at[0, inner]),
        (grid.at[inner, 1], grid.at[inner, 9]),
        (grid.at[inner, 8], grid.at[inner, 0]),
        (edge.at[0], halo.at[1]),
        (edge.at[1], halo.at[0]),
    ]
    copies = [
        pltpu.make_async_remote_copy(
            src_ref=src,
            dst_ref=dst,
            send_sem=send_sem.at[k],
            recv_sem=recv_sem.at[k],
            device_id=peers[k],
            device_id_type=MESH,
        )
        for k, (src, dst) in enumerate(plans)
    ]
    for copy in copies:
        copy.start()
    for copy in copies:
        copy.wait()
    blank = jnp.zeros((8, ROWS, 128), F32)
    stream, radial = lax.axis_index("stream"), lax.axis_index("radial")

    @pl.when(stream == 0)
    def _():
        grid[0, inner] = blank

    @pl.when(stream == lax.axis_size("stream") - 1)
    def _():
        grid[9, inner] = blank

    @pl.when(radial == 0)
    def _():
        grid[inner, 0] = blank

    @pl.when(radial == lax.axis_size("radial") - 1)
    def _():
        grid[inner, 9] = blank

    rate = spread_ref[...]
    keep = 1.0 - 6.0 * rate

    def step(b, carry):
        i, j = b // 8 + 1, b % 8 + 1
        here = grid[i, j]
        behind = grid[i - 1, j]
        left = jnp.where(lane == 0, pltpu.roll(halo[0], lax.rem(128 - b, 128), 1), pltpu.roll(here, 1, 1))
        right = jnp.where(lane == 127, pltpu.roll(halo[1], 127 - b, 1), pltpu.roll(here, 127, 1))
        beside = (behind + grid[i + 1, j]) + (grid[i, j - 1] + grid[i, j + 1]) + (left + right)
        speed = courant_ref[pl.ds(b, 1), :]
        out_ref[b] = (keep - speed) * here + rate * beside + speed * behind
        return carry

    lax.fori_loop(0, 64, step, 0)


def move(first, args):
    vmem = pl.BlockSpec(memory_space=pltpu.VMEM)
    return pl.pallas_call(
        functools.partial(move_kernel, first),
        out_shape=jax.ShapeDtypeStruct((64, ROWS, 128), F32),
        in_specs=[vmem] * len(args),
        out_specs=vmem,
        scratch_shapes=[
            pltpu.VMEM((10, 10, ROWS, 128), F32),
            pltpu.VMEM((2, ROWS, 128), F32),
            pltpu.VMEM((2, ROWS, 128), F32),
            pltpu.SemaphoreType.DMA((6,)),
            pltpu.SemaphoreType.DMA((6,)),
        ],
        compiler_params=pltpu.CompilerParams(
            collective_id=0 if first else 1, has_side_effects=True, vmem_limit_bytes=LIMIT
        ),
    )(*args)


def shards(
    component_fractions,
    kilokelvin_field,
    axial_courant_number,
    spreading_number,
    arrhenius_multiplier_exponent,
    thermal_exponents,
    arrhenius_barrier,
    balance_constant_exponents,
    enthalpy_formation,
    consumed_stoich_matrix,
    yield_stoich_matrix,
    processor_tiles_burning,
    tile_transfer_tally,
):
    shape = component_fractions.shape
    rates, sums = weights(
        consumed_stoich_matrix,
        yield_stoich_matrix,
        arrhenius_multiplier_exponent,
        thermal_exponents,
        arrhenius_barrier,
        balance_constant_exponents,
        enthalpy_formation,
    )
    species = component_fractions.reshape(53 * 64, 128)
    heat = kilokelvin_field.reshape(64, 128)
    courant = axial_courant_number.reshape(64, 128)
    spread = jnp.broadcast_to(jnp.pad(spreading_number, (0, 2))[:, None], (ROWS, 128))
    blocks, tally = processor_tiles_burning, tile_transfer_tally
    state = move(True, (species, heat, courant, spread))
    (state,) = react(False, blocks, tally, state, rates, sums)
    state = move(False, (state, courant, spread))
    species, heat = react(True, blocks, tally, state, rates, sums)
    return species.reshape(shape), heat.reshape(shape[1:])


def solution(mesh):
    in_specs = (
        P(None, "stream", "radial", "azim"),
        P("stream", "radial", "azim"),
        P("stream", "radial", "azim"),
        P(),
        P(),
        P(),
        P(),
        P(),
        P(),
        P(),
        P(),
        P(AXES, None),
        P(AXES, None),
    )
    out_specs = (P(None, "stream", "radial", "azim"), P("stream", "radial", "azim"))
    return jax.shard_map(shards, mesh=mesh, in_specs=in_specs, out_specs=out_specs, check_vma=False)
```

```python
import functools

import jax
import jax.numpy as jnp
from jax import lax
from jax.experimental import pallas as pl
from jax.experimental.pallas import tpu as pltpu
from jax.sharding import PartitionSpec as P

NCYC = 4
ROWS = 56
GROUP = 8
chem_step = 0.02
mass_offset = 0.05
LOG2E = 1.4426950408889634
F32 = jnp.float32
BF16 = jnp.bfloat16
MESH = pl.DeviceIdType.MESH
AXES = ("stream", "radial", "azim")
LIMIT = 50 * 2**20
WORK = 32
EARLY = 8
LATE = 8
SPAN = WORK - EARLY - LATE
FLOOR = 24
SWEEPS = 3
PAIR = 16
SIDE = 6
SIZES = (PAIR,) + (SIDE,) * 6
BASES = tuple(sum(SIZES[:k]) for k in range(7))
SLOTS = sum(SIZES)
OPPOSITE = (0, 2, 1, 4, 3, 6, 5)
SEND_AT, WORK_AT, REPLY_AT, FINAL_AT, REST_AT = 0, 64, 96, 160, 224


def halves(value):
    high = lax.reduce_precision(value, 8, 7)
    low = lax.reduce_precision(value - high, 8, 7)
    return high.astype(BF16), low.astype(BF16)


def weights(consumed, made, exponent, thermal, barrier, balance, enthalpy):
    nspec, nrxn = consumed.shape
    padded = -(-nrxn // 8) * 8

    def columns(table, constant):
        rows = [table, thermal[None], -LOG2E * barrier[None], LOG2E * constant[None]]
        return jnp.pad(jnp.concatenate(rows, 0), ((0, 0), (0, padded - nrxn)))

    ahead = columns(consumed, exponent)
    back = columns(made, exponent - balance)
    high, low = halves(jnp.concatenate([ahead, back], 1).T)
    rates = jnp.concatenate([high, high, low, high], 1)
    heat = LOG2E * jnp.sum(enthalpy[:, None] * (made - consumed), 0, keepdims=True)

    def stack(gain, loss, warm):
        rows = [gain, warm, jnp.zeros((2, nrxn), F32), loss, jnp.zeros((3, nrxn), F32)]
        return jnp.pad(jnp.concatenate(rows, 0), ((0, 0), (0, padded - nrxn)))

    both = jnp.concatenate([stack(made, consumed, heat), stack(consumed, made, -heat)], 1)
    high, low = halves(chem_step * both)
    return rates, jnp.concatenate([high, low], 0)


def parted(value):
    high = value.astype(BF16)
    return high, value - high.astype(F32)


def product(a, b):
    return lax.dot_general(a, b, (((1,), (0,)), ((), ())), preferred_element_type=F32)


def cycle(state, rates, sums):
    row = lax.broadcasted_iota(jnp.int32, state.shape, 0)
    moved = state + jnp.where(row < 53, mass_offset, jnp.where(row == 53, 0.0, 1.0))
    heat = state[53:54]
    logs = jnp.log2(moved)
    logs = jnp.where(row == 54, 1.0 / heat, jnp.where(row == 55, 1.0, logs))
    first, rest = parted(logs)
    second, third = parted(rest)
    first, second = first.astype(F32), second.astype(F32)
    stacked = jnp.concatenate([first, second, first, third], 0).astype(BF16)
    flux = jnp.exp2(product(rates, stacked))
    high, low = parted(flux)
    half = sums.shape[0] // 2
    both = product(sums, high)
    total = both[:half] + both[half:] + product(sums[:half], low.astype(BF16))
    gain, loss = total[:ROWS], total[ROWS:]
    species = (state + gain) * moved / (moved + loss)
    return jnp.where(row == 53, heat * jnp.exp2(gain[53:54]), species)


def toward(value, k):
    lane = lax.broadcasted_iota(jnp.int32, value.shape, 1)
    azim, radial, core = lane & 3, (lane >> 2) & 3, (lane >> 4) & 1

    def ahead(step):
        return pltpu.roll(value, (128 - step) % 128, 1)

    return (
        lambda: jnp.where(core == 0, ahead(16), ahead(-16)),
        lambda: ahead(32),
        lambda: ahead(-32),
        lambda: jnp.where(radial < 3, ahead(4), ahead(-12)),
        lambda: jnp.where(radial > 0, ahead(-4), ahead(12)),
        lambda: jnp.where(azim < 3, ahead(1), ahead(-3)),
        lambda: jnp.where(azim > 0, ahead(-1), ahead(3)),
    )[k]()


def flows(counts):
    load, own = jnp.maximum(counts, EARLY + LATE), counts
    given = [jnp.zeros_like(counts) for _ in SIZES]
    taken = [jnp.zeros_like(counts) for _ in SIZES]
    for sweep in range(SWEEPS):
        for k, size in enumerate(SIZES):
            other = toward(load, k)
            gap = load - other + (1 if sweep == SWEEPS - 1 else 0)
            spare = jnp.maximum(own - (EARLY + LATE), 0)
            give = jnp.minimum(jnp.minimum(size - given[k], spare), jnp.maximum(gap, 0) >> 1)
            give = jnp.minimum(give, jnp.maximum(load - FLOOR, 0))
            give = jnp.minimum(give, jnp.maximum(WORK - other, 0))
            take = toward(give, OPPOSITE[k])
            given[k], taken[k] = given[k] + give, taken[k] + take
            own, load = own - give, load - give + take
    return own, given, taken


def plan_kernel(me_ref, blocks_ref, counts_ref, out_ref):
    counts = jnp.broadcast_to(counts_ref[...], (8, 128))
    own, given, taken = flows(counts)
    place = lax.broadcasted_iota(jnp.int32, (8, 128), 0) * 128
    place = place + lax.broadcasted_iota(jnp.int32, (8, 128), 1)
    mine = place == me_ref[0]

    def pick(value):
        return jnp.sum(jnp.where(mine, value, 0))

    own, total = pick(own), pick(counts)
    given, taken = [pick(v) for v in given], [pick(v) for v in taken]
    received = sum(taken)
    kept = jnp.minimum(own, WORK - received)

    def clear(k, carry):
        out_ref[k] = 0
        return carry

    def clear_final(k, carry):
        out_ref[FINAL_AT + k] = k
        return carry

    lax.fori_loop(0, FINAL_AT, clear, 0)
    lax.fori_loop(0, 64, clear_final, 0)

    def keep(o, carry):
        block = blocks_ref[0, o]
        late = WORK - LATE + o - EARLY
        middle = EARLY + received + o - EARLY - LATE
        slot = jnp.where(o < EARLY, o, jnp.where(o < EARLY + LATE, late, middle))
        out_ref[WORK_AT + slot] = block
        out_ref[FINAL_AT + block] = 128 + slot
        return carry

    lax.fori_loop(0, kept, keep, 0)
    start, reached = kept, jnp.int32(EARLY)
    for p, base in enumerate(BASES):

        def give(k, carry):
            block = blocks_ref[0, start + k]
            out_ref[SEND_AT + base + k] = block
            out_ref[FINAL_AT + block] = 64 + base + k
            return carry

        def take(k, carry):
            out_ref[WORK_AT + reached + k] = 64 + base + k
            out_ref[REPLY_AT + base + k] = reached + k
            return carry

        lax.fori_loop(0, given[p], give, 0)
        lax.fori_loop(0, taken[p], take, 0)
        start, reached = start + given[p], reached + taken[p]
    out_ref[REST_AT] = start
    out_ref[REST_AT + 1] = total


def plan(me, blocks, counts):
    smem = pl.BlockSpec(memory_space=pltpu.SMEM)
    return pl.pallas_call(
        plan_kernel,
        out_shape=jax.ShapeDtypeStruct((256,), jnp.int32),
        in_specs=[smem, smem, pl.BlockSpec(memory_space=pltpu.VMEM)],
        out_specs=smem,
    )(me, blocks, counts)


def subcycles(state, rates_ref, sums_ref):
    return lax.fori_loop(0, NCYC, lambda c, s: cycle(s, rates_ref[...], sums_ref[...]), state)


def rest_kernel(lists_ref, blocks_ref, state_ref, rates_any, sums_any, out_ref, rates, sums, held, sem):
    start, count = lists_ref[REST_AT], lists_ref[REST_AT + 1]

    def bring(source, target):
        copy = pltpu.make_async_copy(source, target, sem)
        copy.start()
        copy.wait()

    @pl.when(start < count)
    def _():
        bring(rates_any, rates)
        bring(sums_any, sums)

        def group(g, carry):
            first = start + g * GROUP
            for k in range(GROUP):
                bring(out_ref.at[blocks_ref[0, jnp.minimum(first + k, 63)]], held.at[k])
            state = jnp.concatenate([held[k] for k in range(GROUP)], 1)
            state = subcycles(state, rates, sums)
            for k in range(GROUP):
                held[k] = state[:, k * 128 : (k + 1) * 128]

                @pl.when(first + k < count)
                def _():
                    bring(held.at[k], out_ref.at[blocks_ref[0, jnp.minimum(first + k, 63)]])

            return carry

        lax.fori_loop(0, (count - start + GROUP - 1) // GROUP, group, 0)


def react_rest(lists, blocks, state, rates, sums):
    smem, anywhere = pl.BlockSpec(memory_space=pltpu.SMEM), pl.BlockSpec(memory_space=pl.ANY)
    return pl.pallas_call(
        rest_kernel,
        out_shape=jax.ShapeDtypeStruct(state.shape, F32),
        in_specs=[smem, smem] + [anywhere] * 3,
        out_specs=anywhere,
        scratch_shapes=[
            pltpu.VMEM(rates.shape, BF16),
            pltpu.VMEM(sums.shape, BF16),
            pltpu.VMEM((GROUP, ROWS, 128), F32),
            pltpu.SemaphoreType.DMA(()),
        ],
        input_output_aliases={2: 0},
        compiler_params=pltpu.CompilerParams(vmem_limit_bytes=LIMIT),
    )(lists, blocks, state, rates, sums)


def last_kernel(lists_ref, blocks_ref, state_ref, rates_ref, sums_ref, species_ref, heat_ref, work):
    start, count = lists_ref[REST_AT], lists_ref[REST_AT + 1]

    def put(source, b):
        species_ref[pl.ds(b, 53, stride=64), :] = source[b, pl.ds(0, 53), :]
        heat_ref[pl.ds(b, 1), :] = source[b, pl.ds(53, 1), :]

    def put_row(i, carry):
        for j in range(8):
            put(state_ref, i * 8 + j)
        return carry

    lax.fori_loop(0, 8, put_row, 0)

    def group(g, carry):
        first = start + g * GROUP
        at = [blocks_ref[0, jnp.minimum(first + k, 63)] for k in range(GROUP)]
        state = jnp.concatenate([state_ref[at[k]] for k in range(GROUP)], 1)
        state = subcycles(state, rates_ref, sums_ref)
        for k in range(GROUP):

            @pl.when(first + k < count)
            def _():
                work[at[k]] = state[:, k * 128 : (k + 1) * 128]
                put(work, at[k])

        return carry

    lax.fori_loop(0, (count - start + GROUP - 1) // GROUP, group, 0)


def finish(lists, blocks, state, rates, sums):
    smem, vmem = pl.BlockSpec(memory_space=pltpu.SMEM), pl.BlockSpec(memory_space=pltpu.VMEM)
    return pl.pallas_call(
        last_kernel,
        out_shape=[jax.ShapeDtypeStruct((53 * 64, 128), F32), jax.ShapeDtypeStruct((64, 128), F32)],
        in_specs=[smem, smem] + [vmem] * 3,
        out_specs=[vmem] * 2,
        scratch_shapes=[pltpu.VMEM(state.shape, F32)],
        compiler_params=pltpu.CompilerParams(vmem_limit_bytes=LIMIT),
    )(lists, blocks, state, rates, sums)


def shifted(axis, step):
    n, me = lax.axis_size(axis), lax.axis_index(axis)
    return {axis: lax.rem(me + (n + step), n)}


def faces():
    return [shifted(axis, step) for axis in AXES for step in (-1, 1)]


def partners():
    me = lax.axis_index("stream")
    sides = [("stream", 2), ("stream", -2), ("radial", 1), ("radial", -1), ("azim", 1), ("azim", -1)]
    return [{"stream": me + 1 - 2 * lax.rem(me, 2)}] + [shifted(*side) for side in sides]


def greet(peers):
    barrier = pltpu.get_barrier_semaphore()
    for peer in peers:
        pl.semaphore_signal(barrier, inc=1, device_id=peer, device_id_type=MESH)
    return lambda: pl.semaphore_wait(barrier, len(peers))


def remote(source, target, sems, k, peer):
    return pltpu.make_async_remote_copy(
        src_ref=source,
        dst_ref=target,
        send_sem=sems[0].at[k],
        recv_sem=sems[1].at[k],
        device_id=peer,
        device_id_type=MESH,
    )


def transport(fill, met, courant_ref, spread_ref, out, grid, edge, halo, sems):
    lane = lax.broadcasted_iota(jnp.int32, (ROWS, 128), 1)

    def load(i, carry):
        low, high = carry
        for j in range(8):
            b = i * 8 + j
            fill(b, grid.at[i + 1, j + 1])
            here = grid[i + 1, j + 1]
            low = jnp.where(lane == b, pltpu.roll(here, b, 1), low)
            high = jnp.where(lane == b, pltpu.roll(here, b + 1, 1), high)
        return low, high

    low, high = lax.fori_loop(0, 8, load, (jnp.zeros((ROWS, 128), F32),) * 2)
    edge[0] = low
    edge[1] = high
    met()
    peers = faces()
    inner = pl.ds(1, 8)
    plans = [
        (grid.at[1, inner], grid.at[9, inner]),
        (grid.at[8, inner], grid.at[0, inner]),
        (grid.at[inner, 1], grid.at[inner, 9]),
        (grid.at[inner, 8], grid.at[inner, 0]),
        (edge.at[0], halo.at[1]),
        (edge.at[1], halo.at[0]),
    ]
    copies = [remote(*plans[k], sems, k, peers[k]) for k in range(6)]
    for copy in copies:
        copy.start()
    for copy in copies:
        copy.wait()
    blank = jnp.zeros((8, ROWS, 128), F32)
    stream, radial = lax.axis_index("stream"), lax.axis_index("radial")

    @pl.when(stream == 0)
    def _():
        grid[0, inner] = blank

    @pl.when(stream == lax.axis_size("stream") - 1)
    def _():
        grid[9, inner] = blank

    @pl.when(radial == 0)
    def _():
        grid[inner, 0] = blank

    @pl.when(radial == lax.axis_size("radial") - 1)
    def _():
        grid[inner, 9] = blank

    rate = spread_ref[...]
    keep = 1.0 - 6.0 * rate

    def step(i, carry):
        for j in range(8):
            b = i * 8 + j
            here = grid[i + 1, j + 1]
            behind = grid[i, j + 1]
            low = pltpu.roll(halo[0], lax.rem(128 - b, 128), 1)
            high = pltpu.roll(halo[1], 127 - b, 1)
            left = jnp.where(lane == 0, low, pltpu.roll(here, 1, 1))
            right = jnp.where(lane == 127, high, pltpu.roll(here, 127, 1))
            beside = (behind + grid[i + 2, j + 1]) + (grid[i + 1, j] + grid[i + 1, j + 2])
            beside = beside + (left + right)
            speed = courant_ref[pl.ds(b, 1), :]
            out[b] = (keep - speed) * here + rate * beside + speed * behind
        return carry

    lax.fori_loop(0, 8, step, 0)


def chemistry(lists_ref, state, rates_ref, sums_ref, out, send, recv, reply, back, result, sems, met):
    def pack(s, carry):
        send[s] = state[lists_ref[SEND_AT + s]]
        return carry

    lax.fori_loop(0, SLOTS, pack, 0)
    met()
    peers = partners()

    def exchange(source, target, first, turned):
        found = []
        for k, (base, size) in enumerate(zip(BASES, SIZES)):
            area = pl.ds(base, size)
            peer = peers[OPPOSITE[k] if turned else k]
            found.append(remote(source.at[area], target.at[area], sems, first + k, peer))
            found[-1].start()
        return found

    def run(first, items):
        whole = subcycles(jnp.concatenate(items, 1), rates_ref, sums_ref)
        for k in range(len(items)):
            result[first + k] = whole[:, k * 128 : (k + 1) * 128]

    def own(first):
        run(first, [state[lists_ref[WORK_AT + first + k]] for k in range(GROUP)])

    def any_item(slot):
        code = lists_ref[WORK_AT + slot]
        there = recv[jnp.maximum(code - 64, 0)]
        return jnp.where(code < 64, state[jnp.minimum(code, 63)], there)

    def middle(g, carry):
        first = EARLY + g * GROUP
        run(first, [any_item(first + k) for k in range(GROUP)])
        return carry

    copies = exchange(send, recv, 0, False)
    own(0)
    for copy in copies:
        copy.wait()
    lax.fori_loop(0, SPAN // GROUP, middle, 0)

    def answer(s, carry):
        reply[s] = result[lists_ref[REPLY_AT + s]]
        return carry

    lax.fori_loop(0, SLOTS, answer, 0)
    copies = exchange(reply, back, 7, True)
    own(WORK - LATE)
    for copy in copies:
        copy.wait()

    def settle(b, carry):
        code = lists_ref[FINAL_AT + b]
        here = state[jnp.minimum(code, 63)]
        there = back[jnp.clip(code - 64, 0, SLOTS - 1)]
        done = result[jnp.clip(code - 128, 0, WORK - 1)]
        out[b] = jnp.where(code < 64, here, jnp.where(code < 128, there, done))
        return carry

    lax.fori_loop(0, 64, settle, 0)


STATE = (64, ROWS, 128)
MOVE_SCRATCH = [
    pltpu.VMEM((10, 10, ROWS, 128), F32),
    pltpu.VMEM((2, ROWS, 128), F32),
    pltpu.VMEM((2, ROWS, 128), F32),
    pltpu.SemaphoreType.DMA((6,)),
    pltpu.SemaphoreType.DMA((6,)),
]
CHEM_SCRATCH = [pltpu.VMEM((SLOTS, ROWS, 128), F32)] * 4 + [
    pltpu.VMEM((WORK, ROWS, 128), F32),
    pltpu.SemaphoreType.DMA((14,)),
    pltpu.SemaphoreType.DMA((14,)),
]


def communicating(kernel, name, smem, args, scratch):
    vmem = pl.BlockSpec(memory_space=pltpu.VMEM)
    specs = [pl.BlockSpec(memory_space=pltpu.SMEM)] * smem + [vmem] * (len(args) - smem)
    return pl.pallas_call(
        kernel,
        out_shape=jax.ShapeDtypeStruct(STATE, F32),
        in_specs=specs,
        out_specs=vmem,
        scratch_shapes=scratch,
        compiler_params=pltpu.CompilerParams(
            collective_id=name, has_side_effects=True, vmem_limit_bytes=LIMIT
        ),
    )(*args)


def first_move(species, heat, courant, spread):
    def kernel(species_ref, heat_ref, courant_ref, spread_ref, out, grid, edge, halo, *sems):
        def fill(b, cell):
            cell[pl.ds(0, 53), :] = species_ref[pl.ds(b, 53, stride=64), :]
            cell[pl.ds(53, 1), :] = heat_ref[pl.ds(b, 1), :]
            cell[pl.ds(54, 2), :] = jnp.zeros((2, 128), F32)

        met = greet(faces())
        transport(fill, met, courant_ref, spread_ref, out, grid, edge, halo, sems)

    return communicating(kernel, 0, 0, (species, heat, courant, spread), MOVE_SCRATCH)


def first_chem(lists, state, rates, sums):
    def kernel(lists_ref, state_ref, rates_ref, sums_ref, out, *scratch):
        met = greet(partners())
        chemistry(lists_ref, state_ref, rates_ref, sums_ref, out, *scratch[:5], scratch[5:], met)

    return communicating(kernel, 1, 1, (lists, state, rates, sums), CHEM_SCRATCH)


def second_step(lists, state, courant, spread, rates, sums):
    def kernel(lists_ref, state_ref, courant_ref, spread_ref, rates_ref, sums_ref, out, *scratch):
        grid, edge, halo, *sems = scratch[: len(MOVE_SCRATCH)]
        moved, *others = scratch[len(MOVE_SCRATCH) :]

        def fill(b, cell):
            cell[...] = state_ref[b]

        met = greet(faces() + [shifted("stream", 2), shifted("stream", -2)])
        transport(fill, met, courant_ref, spread_ref, moved, grid, edge, halo, sems)
        chemistry(
            lists_ref, moved, rates_ref, sums_ref, out, *others[:5], others[5:], lambda: None
        )

    scratch = MOVE_SCRATCH + [pltpu.VMEM(STATE, F32)] + CHEM_SCRATCH
    return communicating(kernel, 2, 1, (lists, state, courant, spread, rates, sums), scratch)


def shards(
    component_fractions,
    kilokelvin_field,
    axial_courant_number,
    spreading_number,
    arrhenius_multiplier_exponent,
    thermal_exponents,
    arrhenius_barrier,
    balance_constant_exponents,
    enthalpy_formation,
    consumed_stoich_matrix,
    yield_stoich_matrix,
    processor_tiles_burning,
    tile_transfer_tally,
):
    shape = component_fractions.shape
    rates, sums = weights(
        consumed_stoich_matrix,
        yield_stoich_matrix,
        arrhenius_multiplier_exponent,
        thermal_exponents,
        arrhenius_barrier,
        balance_constant_exponents,
        enthalpy_formation,
    )
    species = component_fractions.reshape(53 * 64, 128)
    heat = kilokelvin_field.reshape(64, 128)
    courant = axial_courant_number.reshape(64, 128)
    spread = jnp.broadcast_to(jnp.pad(spreading_number, (0, 2))[:, None], (ROWS, 128))
    blocks, tally = processor_tiles_burning, tile_transfer_tally
    count = jnp.sum(tally, 1)
    counts = lax.all_gather(count, AXES, tiled=True)[None]
    me = jnp.int32(0)
    for axis in AXES:
        me = me * lax.axis_size(axis) + lax.axis_index(axis)
    lists = plan(me[None], blocks, counts)
    state = first_move(species, heat, courant, spread)
    state = first_chem(lists, state, rates, sums)
    state = react_rest(lists, blocks, state, rates, sums)
    state = second_step(lists, state, courant, spread, rates, sums)
    species, heat = finish(lists, blocks, state, rates, sums)
    return species.reshape(shape), heat.reshape(shape[1:])


def solution(mesh):
    in_specs = (
        P(None, "stream", "radial", "azim"),
        P("stream", "radial", "azim"),
        P("stream", "radial", "azim"),
        P(),
        P(),
        P(),
        P(),
        P(),
        P(),
        P(),
        P(),
        P(AXES, None),
        P(AXES, None),
    )
    out_specs = (P(None, "stream", "radial", "azim"), P("stream", "radial", "azim"))
    return jax.shard_map(shards, mesh=mesh, in_specs=in_specs, out_specs=out_specs, check_vma=False)
```

```python
import functools

import jax
import jax.numpy as jnp
from jax import lax
from jax.experimental import pallas as pl
from jax.experimental.pallas import tpu as pltpu
from jax.sharding import PartitionSpec as P

NCYC = 4
ROWS = 56
GROUP = 8
chem_step = 0.02
mass_offset = 0.05
LOG2E = 1.4426950408889634
F32 = jnp.float32
BF16 = jnp.bfloat16
MESH = pl.DeviceIdType.MESH
AXES = ("stream", "radial", "azim")
LIMIT = 50 * 2**20
WORK = 32
EARLY = 8
LATE = 8
SPAN = WORK - EARLY - LATE
FLOOR = 24
SWEEPS = 3
PAIR = 16
SIDE = 6
SIZES = (PAIR,) + (SIDE,) * 6
BASES = tuple(sum(SIZES[:k]) for k in range(7))
SLOTS = sum(SIZES)
OPPOSITE = (0, 2, 1, 4, 3, 6, 5)
SEND_AT, WORK_AT, REPLY_AT, FINAL_AT, REST_AT = 0, 64, 96, 160, 224


def prepare(consumed, made, exponent, thermal, barrier, balance, enthalpy, rates, sums, table):
    half = rates.shape[0] // 2

    def put(side, row, value):
        rows, lanes = value.shape
        table[pl.ds(row, rows), pl.ds(side * half, lanes)] = value

    def halves(value):
        high = value.astype(BF16).astype(F32)
        return high, value - high

    table[...] = jnp.zeros_like(table)
    for side, change in enumerate((0.0, balance[...])):
        put(side, 0, (consumed, made)[side][...])
        put(side, 53, thermal[...])
        put(side, 54, -LOG2E * barrier[...])
        put(side, 55, LOG2E * (exponent[...] - change))
    high, low = halves(table[:ROWS])
    stacked = jnp.concatenate([high, high, low, high], 0).T
    rates[...] = stacked[: 2 * half].astype(BF16)
    heat = LOG2E * lax.dot_general(
        enthalpy[...],
        made[...] - consumed[...],
        (((1,), (0,)), ((), ())),
        preferred_element_type=F32,
        precision=lax.Precision.HIGHEST,
    )
    table[...] = jnp.zeros_like(table)
    for side, (gain, loss, warm) in enumerate(((made, consumed, heat), (consumed, made, -heat))):
        put(side, 0, gain[...])
        put(side, 53, warm)
        put(side, ROWS, loss[...])
    high, low = halves(chem_step * table[...])
    sums[...] = jnp.concatenate([high, low], 0)[:, : 2 * half].astype(BF16)


def parted(value):
    high = value.astype(BF16)
    return high, value - high.astype(F32)


def product(a, b):
    return lax.dot_general(a, b, (((1,), (0,)), ((), ())), preferred_element_type=F32)


def cycle(state, rates, sums):
    row = lax.broadcasted_iota(jnp.int32, state.shape, 0)
    moved = state + jnp.where(row < 53, mass_offset, jnp.where(row == 53, 0.0, 1.0))
    heat = state[53:54]
    logs = jnp.log2(moved)
    logs = jnp.where(row == 54, 1.0 / heat, jnp.where(row == 55, 1.0, logs))
    first, rest = parted(logs)
    second, third = parted(rest)
    first, second = first.astype(F32), second.astype(F32)
    stacked = jnp.concatenate([first, second, first, third], 0).astype(BF16)
    flux = jnp.exp2(product(rates, stacked))
    high, low = parted(flux)
    half = sums.shape[0] // 2
    both = product(sums, high)
    total = both[:half] + both[half:] + product(sums[:half], low.astype(BF16))
    gain, loss = total[:ROWS], total[ROWS:]
    species = (state + gain) * moved / (moved + loss)
    return jnp.where(row == 53, heat * jnp.exp2(gain[53:54]), species)


def toward(value, k):
    lane = lax.broadcasted_iota(jnp.int32, value.shape, 1)
    azim, radial, core = lane & 3, (lane >> 2) & 3, (lane >> 4) & 1

    def ahead(step):
        return pltpu.roll(value, (128 - step) % 128, 1)

    return (
        lambda: jnp.where(core == 0, ahead(16), ahead(-16)),
        lambda: ahead(32),
        lambda: ahead(-32),
        lambda: jnp.where(radial < 3, ahead(4), ahead(-12)),
        lambda: jnp.where(radial > 0, ahead(-4), ahead(12)),
        lambda: jnp.where(azim < 3, ahead(1), ahead(-3)),
        lambda: jnp.where(azim > 0, ahead(-1), ahead(3)),
    )[k]()


def flows(counts):
    load, own = jnp.maximum(counts, EARLY + LATE), counts
    given = [jnp.zeros_like(counts) for _ in SIZES]
    taken = [jnp.zeros_like(counts) for _ in SIZES]
    for sweep in range(SWEEPS):
        for k, size in enumerate(SIZES):
            other = toward(load, k)
            gap = load - other + (1 if sweep == SWEEPS - 1 else 0)
            spare = jnp.maximum(own - (EARLY + LATE), 0)
            give = jnp.minimum(jnp.minimum(size - given[k], spare), jnp.maximum(gap, 0) >> 1)
            give = jnp.minimum(give, jnp.maximum(load - FLOOR, 0))
            give = jnp.minimum(give, jnp.maximum(WORK - other, 0))
            take = toward(give, OPPOSITE[k])
            given[k], taken[k] = given[k] + give, taken[k] + take
            own, load = own - give, load - give + take
    return own, given, taken


def plan(me, counts, blocks_ref, lists, codes, codes_smem, sem):
    own, given, taken = flows(counts)
    place = lax.broadcasted_iota(jnp.int32, (8, 128), 0) * 128
    lane = lax.broadcasted_iota(jnp.int32, (8, 128), 1)
    mine = place + lane == me

    def pick(value):
        return jnp.sum(jnp.where(mine, value, 0))

    own, total = pick(own), pick(counts)
    given, taken = [pick(v) for v in given], [pick(v) for v in taken]
    received = sum(taken)
    kept = jnp.minimum(own, WORK - received)
    sent_before, taken_before = [kept], [jnp.int32(0)]
    for p in range(len(SIZES)):
        sent_before.append(sent_before[p] + given[p])
        taken_before.append(taken_before[p] + taken[p])

    position = jnp.zeros((8, 128), jnp.int32)
    for n in range(64):
        position = jnp.where(lane == blocks_ref[0, n], n, position)
    late = WORK - LATE - EARLY + position
    middle = received + position - LATE
    slot = jnp.where(position < EARLY, position, jnp.where(position < EARLY + LATE, late, middle))
    code = jnp.where(position < kept, 128 + slot, lane)
    for p, base in enumerate(BASES):
        inside = (position >= sent_before[p]) & (position < sent_before[p + 1])
        code = jnp.where(inside, 64 + base + position - sent_before[p], code)
    codes[...] = code
    copy = pltpu.make_async_copy(codes, codes_smem, sem)
    copy.start()

    for p, (base, size) in enumerate(zip(BASES, SIZES)):

        def per_slot(k, carry):
            at = jnp.clip(sent_before[p] + k, 0, 63)
            lists[SEND_AT + base + k] = blocks_ref[0, at]
            lists[REPLY_AT + base + k] = jnp.clip(EARLY + taken_before[p] + k, 0, WORK - 1)
            return carry

        lax.fori_loop(0, size, per_slot, 0)

    def per_early(w, carry):
        lists[WORK_AT + w] = blocks_ref[0, w]
        lists[WORK_AT + WORK - LATE + w] = blocks_ref[0, EARLY + w]
        return carry

    lax.fori_loop(0, EARLY, per_early, 0)

    def per_middle(j, carry):
        at = jnp.clip(EARLY + LATE + j - received, 0, 63)
        value = blocks_ref[0, at]
        for p, base in enumerate(BASES):
            inside = (j >= taken_before[p]) & (j < taken_before[p + 1])
            value = jnp.where(inside, 64 + base + j - taken_before[p], value)
        lists[WORK_AT + EARLY + j] = value
        return carry

    lax.fori_loop(0, SPAN, per_middle, 0)
    lists[REST_AT] = sent_before[-1]
    lists[REST_AT + 1] = total
    copy.wait()

    def per_block(b, carry):
        lists[FINAL_AT + b] = codes_smem[0, b]
        return carry

    lax.fori_loop(0, 64, per_block, 0)


def subcycles(state, rates_ref, sums_ref):
    return lax.fori_loop(0, NCYC, lambda c, s: cycle(s, rates_ref[...], sums_ref[...]), state)


def rest_kernel(lists_ref, blocks_ref, state_ref, rates_any, sums_any, out_ref, rates, sums, held, sem):
    start, count = lists_ref[REST_AT], lists_ref[REST_AT + 1]

    def bring(source, target):
        copy = pltpu.make_async_copy(source, target, sem)
        copy.start()
        copy.wait()

    @pl.when(start < count)
    def _():
        bring(rates_any, rates)
        bring(sums_any, sums)

        def group(g, carry):
            first = start + g * GROUP
            for k in range(GROUP):
                bring(out_ref.at[blocks_ref[0, jnp.minimum(first + k, 63)]], held.at[k])
            state = jnp.concatenate([held[k] for k in range(GROUP)], 1)
            state = subcycles(state, rates, sums)
            for k in range(GROUP):
                held[k] = state[:, k * 128 : (k + 1) * 128]

                @pl.when(first + k < count)
                def _():
                    bring(held.at[k], out_ref.at[blocks_ref[0, jnp.minimum(first + k, 63)]])

            return carry

        lax.fori_loop(0, (count - start + GROUP - 1) // GROUP, group, 0)


def react_rest(lists, blocks, state, rates, sums):
    smem, anywhere = pl.BlockSpec(memory_space=pltpu.SMEM), pl.BlockSpec(memory_space=pl.ANY)
    return pl.pallas_call(
        rest_kernel,
        out_shape=jax.ShapeDtypeStruct(state.shape, F32),
        in_specs=[smem, smem] + [anywhere] * 3,
        out_specs=anywhere,
        scratch_shapes=[
            pltpu.VMEM(rates.shape, BF16),
            pltpu.VMEM(sums.shape, BF16),
            pltpu.VMEM((GROUP, ROWS, 128), F32),
            pltpu.SemaphoreType.DMA(()),
        ],
        input_output_aliases={2: 0},
        compiler_params=pltpu.CompilerParams(vmem_limit_bytes=LIMIT),
    )(lists, blocks, state, rates, sums)


def last_kernel(lists_ref, blocks_ref, state_ref, rates_ref, sums_ref, species_ref, heat_ref, work):
    start, count = lists_ref[REST_AT], lists_ref[REST_AT + 1]

    def put(source, b):
        species_ref[pl.ds(b, 53, stride=64), :] = source[b, pl.ds(0, 53), :]
        heat_ref[pl.ds(b, 1), :] = source[b, pl.ds(53, 1), :]

    def put_row(i, carry):
        for j in range(8):
            put(state_ref, i * 8 + j)
        return carry

    lax.fori_loop(0, 8, put_row, 0)

    def group(g, carry):
        first = start + g * GROUP
        at = [blocks_ref[0, jnp.minimum(first + k, 63)] for k in range(GROUP)]
        state = jnp.concatenate([state_ref[at[k]] for k in range(GROUP)], 1)
        state = subcycles(state, rates_ref, sums_ref)
        for k in range(GROUP):

            @pl.when(first + k < count)
            def _():
                work[at[k]] = state[:, k * 128 : (k + 1) * 128]
                put(work, at[k])

        return carry

    lax.fori_loop(0, (count - start + GROUP - 1) // GROUP, group, 0)


def finish(lists, blocks, state, rates, sums):
    smem, vmem = pl.BlockSpec(memory_space=pltpu.SMEM), pl.BlockSpec(memory_space=pltpu.VMEM)
    return pl.pallas_call(
        last_kernel,
        out_shape=[jax.ShapeDtypeStruct((53 * 64, 128), F32), jax.ShapeDtypeStruct((64, 128), F32)],
        in_specs=[smem, smem] + [vmem] * 3,
        out_specs=[vmem] * 2,
        scratch_shapes=[pltpu.VMEM(state.shape, F32)],
        compiler_params=pltpu.CompilerParams(vmem_limit_bytes=LIMIT),
    )(lists, blocks, state, rates, sums)


def shifted(axis, step):
    n, me = lax.axis_size(axis), lax.axis_index(axis)
    return {axis: lax.rem(me + (n + step), n)}


def faces():
    return [shifted(axis, step) for axis in AXES for step in (-1, 1)]


def partners():
    me = lax.axis_index("stream")
    sides = [("stream", 2), ("stream", -2), ("radial", 1), ("radial", -1), ("azim", 1), ("azim", -1)]
    return [{"stream": me + 1 - 2 * lax.rem(me, 2)}] + [shifted(*side) for side in sides]


def greet(peers):
    barrier = pltpu.get_barrier_semaphore()
    for peer in peers:
        pl.semaphore_signal(barrier, inc=1, device_id=peer, device_id_type=MESH)
    return lambda: pl.semaphore_wait(barrier, len(peers))


def remote(source, target, sems, k, peer):
    return pltpu.make_async_remote_copy(
        src_ref=source,
        dst_ref=target,
        send_sem=sems[0].at[k],
        recv_sem=sems[1].at[k],
        device_id=peer,
        device_id_type=MESH,
    )


def transport(fill, met, beside, courant_ref, spread_ref, out, grid, edge, halo, sems):
    lane = lax.broadcasted_iota(jnp.int32, (ROWS, 128), 1)

    def load(i, carry):
        low, high = carry
        for j in range(8):
            b = i * 8 + j
            fill(b, grid.at[i + 1, j + 1])
            here = grid[i + 1, j + 1]
            low = jnp.where(lane == b, pltpu.roll(here, b, 1), low)
            high = jnp.where(lane == b, pltpu.roll(here, b + 1, 1), high)
        return low, high

    low, high = lax.fori_loop(0, 8, load, (jnp.zeros((ROWS, 128), F32),) * 2)
    edge[0] = low
    edge[1] = high
    met()
    peers = faces()
    inner = pl.ds(1, 8)
    plans = [
        (grid.at[1, inner], grid.at[9, inner]),
        (grid.at[8, inner], grid.at[0, inner]),
        (grid.at[inner, 1], grid.at[inner, 9]),
        (grid.at[inner, 8], grid.at[inner, 0]),
        (edge.at[0], halo.at[1]),
        (edge.at[1], halo.at[0]),
    ]
    copies = [remote(*plans[k], sems, k, peers[k]) for k in range(6)]
    for copy in copies:
        copy.start()
    beside()
    for copy in copies:
        copy.wait()
    blank = jnp.zeros((8, ROWS, 128), F32)
    stream, radial = lax.axis_index("stream"), lax.axis_index("radial")

    @pl.when(stream == 0)
    def _():
        grid[0, inner] = blank

    @pl.when(stream == lax.axis_size("stream") - 1)
    def _():
        grid[9, inner] = blank

    @pl.when(radial == 0)
    def _():
        grid[inner, 0] = blank

    @pl.when(radial == lax.axis_size("radial") - 1)
    def _():
        grid[inner, 9] = blank

    rate = spread_ref[...]
    keep = 1.0 - 6.0 * rate

    def step(i, carry):
        for j in range(8):
            b = i * 8 + j
            here = grid[i + 1, j + 1]
            behind = grid[i, j + 1]
            low = pltpu.roll(halo[0], lax.rem(128 - b, 128), 1)
            high = pltpu.roll(halo[1], 127 - b, 1)
            left = jnp.where(lane == 0, low, pltpu.roll(here, 1, 1))
            right = jnp.where(lane == 127, high, pltpu.roll(here, 127, 1))
            around = (behind + grid[i + 2, j + 1]) + (grid[i + 1, j] + grid[i + 1, j + 2])
            around = around + (left + right)
            speed = courant_ref[pl.ds(b, 1), :]
            out[b] = (keep - speed) * here + rate * around + speed * behind
        return carry

    lax.fori_loop(0, 8, step, 0)


def chemistry(lists_ref, state, rates_ref, sums_ref, out, send, recv, reply, back, result, sems, met):
    def pack(s, carry):
        send[s] = state[lists_ref[SEND_AT + s]]
        return carry

    lax.fori_loop(0, SLOTS, pack, 0)
    met()
    peers = partners()

    def exchange(source, target, first, turned):
        found = []
        for k, (base, size) in enumerate(zip(BASES, SIZES)):
            area = pl.ds(base, size)
            peer = peers[OPPOSITE[k] if turned else k]
            found.append(remote(source.at[area], target.at[area], sems, first + k, peer))
            found[-1].start()
        return found

    def run(first, items):
        whole = subcycles(jnp.concatenate(items, 1), rates_ref, sums_ref)
        for k in range(len(items)):
            result[first + k] = whole[:, k * 128 : (k + 1) * 128]

    def own(first):
        run(first, [state[lists_ref[WORK_AT + first + k]] for k in range(GROUP)])

    def any_item(slot):
        code = lists_ref[WORK_AT + slot]
        there = recv[jnp.maximum(code - 64, 0)]
        return jnp.where(code < 64, state[jnp.minimum(code, 63)], there)

    def middle(g, carry):
        first = EARLY + g * GROUP
        run(first, [any_item(first + k) for k in range(GROUP)])
        return carry

    copies = exchange(send, recv, 0, False)
    own(0)
    for copy in copies:
        copy.wait()
    lax.fori_loop(0, SPAN // GROUP, middle, 0)

    def answer(s, carry):
        reply[s] = result[lists_ref[REPLY_AT + s]]
        return carry

    lax.fori_loop(0, SLOTS, answer, 0)
    copies = exchange(reply, back, 7, True)
    own(WORK - LATE)
    for copy in copies:
        copy.wait()

    def settle(b, carry):
        code = lists_ref[FINAL_AT + b]
        here = state[jnp.minimum(code, 63)]
        there = back[jnp.clip(code - 64, 0, SLOTS - 1)]
        done = result[jnp.clip(code - 128, 0, WORK - 1)]
        out[b] = jnp.where(code < 64, here, jnp.where(code < 128, there, done))
        return carry

    lax.fori_loop(0, 64, settle, 0)


STATE = (64, ROWS, 128)
MOVE_SCRATCH = [
    pltpu.VMEM((10, 10, ROWS, 128), F32),
    pltpu.VMEM((2, ROWS, 128), F32),
    pltpu.VMEM((2, ROWS, 128), F32),
    pltpu.SemaphoreType.DMA((6,)),
    pltpu.SemaphoreType.DMA((6,)),
]
CHEM_SCRATCH = [pltpu.VMEM((SLOTS, ROWS, 128), F32)] * 4 + [
    pltpu.VMEM((WORK, ROWS, 128), F32),
    pltpu.SemaphoreType.DMA((14,)),
    pltpu.SemaphoreType.DMA((14,)),
]


COUNT_SCRATCH = [
    pltpu.VMEM((8, 8, 128), jnp.int32),
    pltpu.VMEM((4, 8, 128), jnp.int32),
    pltpu.VMEM((4, 4, 8, 128), jnp.int32),
    pltpu.SemaphoreType.DMA((13,)),
    pltpu.SemaphoreType.DMA((13,)),
    pltpu.VMEM((8, 128), jnp.int32),
    pltpu.SMEM((8, 128), jnp.int32),
    pltpu.SemaphoreType.DMA(()),
    pltpu.VMEM((2 * ROWS, 768), F32),
]


def others(axis):
    return [shifted(axis, step) for step in range(1, lax.axis_size(axis))]


def spread_counts(first, second, third, sems):
    stream, radial, azim = (lax.axis_index(axis) for axis in AXES)

    def stage(source, target, axis, start):
        copies = [remote(source, target, sems, start + k, p) for k, p in enumerate(others(axis))]
        for copy in copies:
            copy.start()

        def wait():
            for copy in copies:
                copy.wait()

        return wait

    def along_stream():
        return stage(first.at[stream], first.at[stream], "stream", 0)

    def along_radial():
        row = lax.broadcasted_iota(jnp.int32, (8, 128), 0)
        joined = first[0]
        for s in range(1, 8):
            joined = jnp.where(row == s, first[s], joined)
        second[radial] = joined
        return stage(second.at[radial], second.at[radial], "radial", 7)

    def along_azim():
        third[azim] = second[...]
        return stage(third.at[azim], third.at[azim], "azim", 10)

    def whole():
        row = lax.broadcasted_iota(jnp.int32, (8, 128), 0)
        lane = lax.broadcasted_iota(jnp.int32, (8, 128), 1)
        total = jnp.zeros((8, 128), jnp.int32)
        for a in range(4):
            for r in range(4):
                here = (lane & 15 == r * 4 + a) & (lane >> 4 == row)
                total = jnp.where(here, third[a, r], total)
        return jnp.broadcast_to(jnp.sum(total, 0, keepdims=True), (8, 128))

    return along_stream, along_radial, along_azim, whole


def communicating(kernel, name, out_shape, out_specs, specs, args, scratch):
    return pl.pallas_call(
        kernel,
        out_shape=out_shape,
        in_specs=specs,
        out_specs=out_specs,
        scratch_shapes=scratch,
        compiler_params=pltpu.CompilerParams(
            collective_id=name, has_side_effects=True, vmem_limit_bytes=LIMIT
        ),
    )(*args)


def first_step(blocks, tally, species, heat, courant, spread, settings):
    nrxn = settings[0].shape[1]
    padded = -(-nrxn // 8) * 8

    def kernel(blocks_ref, tally_ref, species_ref, heat_ref, courant_ref, spread_ref, *refs):
        settings_refs, refs = refs[: len(settings)], refs[len(settings) :]
        out, lists, rates, sums = refs[:4]
        scratch = refs[4:]
        grid, edge, halo, *sems = scratch[: len(MOVE_SCRATCH)]
        scratch = scratch[len(MOVE_SCRATCH) :]
        first, second, third, *count_sems = scratch[:5]
        codes, codes_smem, code_sem, table = scratch[5:9]
        moved, *chem = scratch[9:]

        def fill(b, cell):
            cell[pl.ds(0, 53), :] = species_ref[pl.ds(b, 53, stride=64), :]
            cell[pl.ds(53, 1), :] = heat_ref[pl.ds(b, 1), :]
            cell[pl.ds(54, 2), :] = jnp.zeros((2, 128), F32)

        met = greet(others("stream") + others("radial") + others("azim"))
        stream, radial, azim = (lax.axis_index(axis) for axis in AXES)
        me = (stream * 4 + radial) * 4 + azim
        own = jnp.sum(tally_ref[...], 1, keepdims=True)
        first[stream] = jnp.broadcast_to(own, (8, 128))
        stages = spread_counts(first, second, third, count_sems)
        waiting = []

        def ready():
            met()
            waiting.append(stages[0]())

        def beside():
            waiting[0]()
            wait = stages[1]()
            prepare(*settings_refs, rates, sums, table)
            wait()
            stages[2]()()
            plan(me, stages[3](), blocks_ref, lists, codes, codes_smem, code_sem)

        transport(fill, ready, beside, courant_ref, spread_ref, moved, grid, edge, halo, sems)
        chemistry(lists, moved, rates, sums, out, *chem[:5], chem[5:], lambda: None)

    smem, vmem = pl.BlockSpec(memory_space=pltpu.SMEM), pl.BlockSpec(memory_space=pltpu.VMEM)
    args = (blocks, tally, species, heat, courant, spread, *settings)
    return communicating(
        kernel,
        0,
        [
            jax.ShapeDtypeStruct(STATE, F32),
            jax.ShapeDtypeStruct((256,), jnp.int32),
            jax.ShapeDtypeStruct((2 * padded, 4 * ROWS), BF16),
            jax.ShapeDtypeStruct((4 * ROWS, 2 * padded), BF16),
        ],
        [vmem, smem, vmem, vmem],
        [smem] + [vmem] * (len(args) - 1),
        args,
        MOVE_SCRATCH + COUNT_SCRATCH + [pltpu.VMEM(STATE, F32)] + CHEM_SCRATCH,
    )


def second_step(lists, state, courant, spread, rates, sums):
    def kernel(lists_ref, state_ref, courant_ref, spread_ref, rates_ref, sums_ref, out, *scratch):
        grid, edge, halo, *sems = scratch[: len(MOVE_SCRATCH)]
        moved, *chem = scratch[len(MOVE_SCRATCH) :]

        def fill(b, cell):
            cell[...] = state_ref[b]

        met = greet(faces() + [shifted("stream", 2), shifted("stream", -2)])
        nothing = lambda: None
        transport(fill, met, nothing, courant_ref, spread_ref, moved, grid, edge, halo, sems)
        chemistry(lists_ref, moved, rates_ref, sums_ref, out, *chem[:5], chem[5:], nothing)

    smem, vmem = pl.BlockSpec(memory_space=pltpu.SMEM), pl.BlockSpec(memory_space=pltpu.VMEM)
    return communicating(
        kernel,
        1,
        jax.ShapeDtypeStruct(STATE, F32),
        vmem,
        [smem] + [vmem] * 5,
        (lists, state, courant, spread, rates, sums),
        MOVE_SCRATCH + [pltpu.VMEM(STATE, F32)] + CHEM_SCRATCH,
    )


def shards(
    component_fractions,
    kilokelvin_field,
    axial_courant_number,
    spreading_number,
    arrhenius_multiplier_exponent,
    thermal_exponents,
    arrhenius_barrier,
    balance_constant_exponents,
    enthalpy_formation,
    consumed_stoich_matrix,
    yield_stoich_matrix,
    processor_tiles_burning,
    tile_transfer_tally,
):
    shape = component_fractions.shape
    settings = (
        consumed_stoich_matrix,
        yield_stoich_matrix,
        arrhenius_multiplier_exponent[None],
        thermal_exponents[None],
        arrhenius_barrier[None],
        balance_constant_exponents[None],
        enthalpy_formation[None],
    )
    species = component_fractions.reshape(53 * 64, 128)
    heat = kilokelvin_field.reshape(64, 128)
    courant = axial_courant_number.reshape(64, 128)
    spread = jnp.broadcast_to(jnp.pad(spreading_number, (0, 2))[:, None], (ROWS, 128))
    blocks, tally = processor_tiles_burning, tile_transfer_tally
    state, lists, rates, sums = first_step(blocks, tally, species, heat, courant, spread, settings)
    state = react_rest(lists, blocks, state, rates, sums)
    state = second_step(lists, state, courant, spread, rates, sums)
    species, heat = finish(lists, blocks, state, rates, sums)
    return species.reshape(shape), heat.reshape(shape[1:])


def solution(mesh):
    in_specs = (
        P(None, "stream", "radial", "azim"),
        P("stream", "radial", "azim"),
        P("stream", "radial", "azim"),
        P(),
        P(),
        P(),
        P(),
        P(),
        P(),
        P(),
        P(),
        P(AXES, None),
        P(AXES, None),
    )
    out_specs = (P(None, "stream", "radial", "azim"), P("stream", "radial", "azim"))
    return jax.shard_map(shards, mesh=mesh, in_specs=in_specs, out_specs=out_specs, check_vma=False)
```

```python
import functools

import jax
import jax.numpy as jnp
from jax import lax
from jax.experimental import pallas as pl
from jax.experimental.pallas import tpu as pltpu
from jax.sharding import PartitionSpec as P

NCYC = 4
ROWS = 56
GROUP = 8
chem_step = 0.02
mass_offset = 0.05
LOG2E = 1.4426950408889634
F32 = jnp.float32
BF16 = jnp.bfloat16
MESH = pl.DeviceIdType.MESH
AXES = ("stream", "radial", "azim")
LIMIT = 63 * 2**20
WORK = 32
EARLY = 8
LATE = 8
SPAN = WORK - EARLY - LATE
FLOOR = 24
SWEEPS = 3
PAIR = 16
SIDE = 6
SIZES = (PAIR,) + (SIDE,) * 6
BASES = tuple(sum(SIZES[:k]) for k in range(7))
SLOTS = sum(SIZES)
OPPOSITE = (0, 2, 1, 4, 3, 6, 5)
SEND_AT, WORK_AT, REPLY_AT, FINAL_AT, REST_AT = 0, 64, 96, 160, 224


def prepare(consumed, made, exponent, thermal, barrier, balance, enthalpy, rates, sums, table):
    half = rates.shape[0] // 2
    exponent, thermal, barrier, balance, enthalpy = (
        vector[...].reshape(1, -1) for vector in (exponent, thermal, barrier, balance, enthalpy)
    )

    def put(side, row, value):
        rows, lanes = value.shape
        table[pl.ds(row, rows), pl.ds(side * half, lanes)] = value

    def halves(value):
        high = value.astype(BF16).astype(F32)
        return high, value - high

    table[...] = jnp.zeros_like(table)
    for side, change in enumerate((0.0, balance)):
        put(side, 0, (consumed, made)[side][...])
        put(side, 53, thermal)
        put(side, 54, -LOG2E * barrier)
        put(side, 55, LOG2E * (exponent - change))
    high, low = halves(table[:ROWS])
    stacked = jnp.concatenate([high, high, low, high], 0).T
    rates[...] = stacked[: 2 * half].astype(BF16)
    heat = LOG2E * lax.dot_general(
        enthalpy,
        made[...] - consumed[...],
        (((1,), (0,)), ((), ())),
        preferred_element_type=F32,
        precision=lax.Precision.HIGHEST,
    )
    table[...] = jnp.zeros_like(table)
    for side, (gain, loss, warm) in enumerate(((made, consumed, heat), (consumed, made, -heat))):
        put(side, 0, gain[...])
        put(side, 53, warm)
        put(side, ROWS, loss[...])
    high, low = halves(chem_step * table[...])
    sums[...] = jnp.concatenate([high, low], 0)[:, : 2 * half].astype(BF16)


def parted(value):
    high = value.astype(BF16)
    return high, value - high.astype(F32)


def product(a, b):
    return lax.dot_general(a, b, (((1,), (0,)), ((), ())), preferred_element_type=F32)


def cycle(state, rates, sums):
    row = lax.broadcasted_iota(jnp.int32, state.shape, 0)
    moved = state + jnp.where(row < 53, mass_offset, jnp.where(row == 53, 0.0, 1.0))
    heat = state[53:54]
    logs = jnp.log2(moved)
    logs = jnp.where(row == 54, 1.0 / heat, jnp.where(row == 55, 1.0, logs))
    first, rest = parted(logs)
    second, third = parted(rest)
    first, second = first.astype(F32), second.astype(F32)
    stacked = jnp.concatenate([first, second, first, third], 0).astype(BF16)
    flux = jnp.exp2(product(rates, stacked))
    high, low = parted(flux)
    half = sums.shape[0] // 2
    both = product(sums, high)
    total = both[:half] + both[half:] + product(sums[:half], low.astype(BF16))
    gain, loss = total[:ROWS], total[ROWS:]
    species = (state + gain) * moved / (moved + loss)
    return jnp.where(row == 53, heat * jnp.exp2(gain[53:54]), species)


def toward(value, k):
    lane = lax.broadcasted_iota(jnp.int32, value.shape, 1)
    azim, radial, core = lane & 3, (lane >> 2) & 3, (lane >> 4) & 1

    def ahead(step):
        return pltpu.roll(value, (128 - step) % 128, 1)

    return (
        lambda: jnp.where(core == 0, ahead(16), ahead(-16)),
        lambda: ahead(32),
        lambda: ahead(-32),
        lambda: jnp.where(radial < 3, ahead(4), ahead(-12)),
        lambda: jnp.where(radial > 0, ahead(-4), ahead(12)),
        lambda: jnp.where(azim < 3, ahead(1), ahead(-3)),
        lambda: jnp.where(azim > 0, ahead(-1), ahead(3)),
    )[k]()


def flows(counts):
    load, own = jnp.maximum(counts, EARLY + LATE), counts
    given = [jnp.zeros_like(counts) for _ in SIZES]
    taken = [jnp.zeros_like(counts) for _ in SIZES]
    for sweep in range(SWEEPS):
        for k, size in enumerate(SIZES):
            other = toward(load, k)
            gap = load - other + (1 if sweep == SWEEPS - 1 else 0)
            spare = jnp.maximum(own - (EARLY + LATE), 0)
            give = jnp.minimum(jnp.minimum(size - given[k], spare), jnp.maximum(gap, 0) >> 1)
            give = jnp.minimum(give, jnp.maximum(load - FLOOR, 0))
            give = jnp.minimum(give, jnp.maximum(WORK - other, 0))
            take = toward(give, OPPOSITE[k])
            given[k], taken[k] = given[k] + give, taken[k] + take
            own, load = own - give, load - give + take
    return own, given, taken


def plan(me, counts, blocks_ref, lists, codes, codes_smem, sem):
    own, given, taken = flows(counts)
    place = lax.broadcasted_iota(jnp.int32, (8, 128), 0) * 128
    lane = lax.broadcasted_iota(jnp.int32, (8, 128), 1)
    mine = place + lane == me

    def pick(value):
        return jnp.sum(jnp.where(mine, value, 0))

    own, total = pick(own), pick(counts)
    given, taken = [pick(v) for v in given], [pick(v) for v in taken]
    received = sum(taken)
    kept = jnp.minimum(own, WORK - received)
    sent_before, taken_before = [kept], [jnp.int32(0)]
    for p in range(len(SIZES)):
        sent_before.append(sent_before[p] + given[p])
        taken_before.append(taken_before[p] + taken[p])

    position = jnp.zeros((8, 128), jnp.int32)
    for n in range(64):
        position = jnp.where(lane == blocks_ref[0, n], n, position)
    late = WORK - LATE - EARLY + position
    middle = received + position - LATE
    slot = jnp.where(position < EARLY, position, jnp.where(position < EARLY + LATE, late, middle))
    code = jnp.where(position < kept, 128 + slot, lane)
    for p, base in enumerate(BASES):
        inside = (position >= sent_before[p]) & (position < sent_before[p + 1])
        code = jnp.where(inside, 64 + base + position - sent_before[p], code)
    codes[...] = code
    copy = pltpu.make_async_copy(codes, codes_smem, sem)
    copy.start()

    for p, (base, size) in enumerate(zip(BASES, SIZES)):

        def per_slot(k, carry):
            at = jnp.clip(sent_before[p] + k, 0, 63)
            lists[SEND_AT + base + k] = blocks_ref[0, at]
            lists[REPLY_AT + base + k] = jnp.clip(EARLY + taken_before[p] + k, 0, WORK - 1)
            return carry

        lax.fori_loop(0, size, per_slot, 0)

    def per_early(w, carry):
        lists[WORK_AT + w] = blocks_ref[0, w]
        lists[WORK_AT + WORK - LATE + w] = blocks_ref[0, EARLY + w]
        return carry

    lax.fori_loop(0, EARLY, per_early, 0)

    def per_middle(j, carry):
        at = jnp.clip(EARLY + LATE + j - received, 0, 63)
        value = blocks_ref[0, at]
        for p, base in enumerate(BASES):
            inside = (j >= taken_before[p]) & (j < taken_before[p + 1])
            value = jnp.where(inside, 64 + base + j - taken_before[p], value)
        lists[WORK_AT + EARLY + j] = value
        return carry

    lax.fori_loop(0, SPAN, per_middle, 0)
    lists[REST_AT] = sent_before[-1]
    lists[REST_AT + 1] = total
    copy.wait()

    def per_block(b, carry):
        lists[FINAL_AT + b] = codes_smem[0, b]
        return carry

    lax.fori_loop(0, 64, per_block, 0)


def fetch(pairs, sem):
    copies = [pltpu.make_async_copy(*pair, sem.at[k]) for k, pair in enumerate(pairs)]
    for copy in copies:
        copy.start()
    return [copy.wait for copy in copies]


def subcycles(state, rates_ref, sums_ref):
    return lax.fori_loop(0, NCYC, lambda c, s: cycle(s, rates_ref[...], sums_ref[...]), state)


def rest_kernel(lists_ref, blocks_ref, state_ref, rates_any, sums_any, out_ref, rates, sums, held, sem):
    start, count = lists_ref[REST_AT], lists_ref[REST_AT + 1]

    def bring(source, target):
        copy = pltpu.make_async_copy(source, target, sem)
        copy.start()
        copy.wait()

    @pl.when(start < count)
    def _():
        bring(rates_any, rates)
        bring(sums_any, sums)

        def group(g, carry):
            first = start + g * GROUP
            for k in range(GROUP):
                bring(out_ref.at[blocks_ref[0, jnp.minimum(first + k, 63)]], held.at[k])
            state = jnp.concatenate([held[k] for k in range(GROUP)], 1)
            state = subcycles(state, rates, sums)
            for k in range(GROUP):
                held[k] = state[:, k * 128 : (k + 1) * 128]

                @pl.when(first + k < count)
                def _():
                    bring(held.at[k], out_ref.at[blocks_ref[0, jnp.minimum(first + k, 63)]])

            return carry

        lax.fori_loop(0, (count - start + GROUP - 1) // GROUP, group, 0)


def react_rest(lists, blocks, state, rates, sums):
    smem, anywhere = pl.BlockSpec(memory_space=pltpu.SMEM), pl.BlockSpec(memory_space=pl.ANY)
    return pl.pallas_call(
        rest_kernel,
        out_shape=jax.ShapeDtypeStruct(state.shape, F32),
        in_specs=[smem, smem] + [anywhere] * 3,
        out_specs=anywhere,
        scratch_shapes=[
            pltpu.VMEM(rates.shape, BF16),
            pltpu.VMEM(sums.shape, BF16),
            pltpu.VMEM((GROUP, ROWS, 128), F32),
            pltpu.SemaphoreType.DMA(()),
        ],
        input_output_aliases={2: 0},
        compiler_params=pltpu.CompilerParams(vmem_limit_bytes=LIMIT),
    )(lists, blocks, state, rates, sums)


def last_kernel(
    lists_ref, blocks_ref, state_any, rates_any, sums_any, species_any, heat_any, *scratch
):
    state, work, species, heat, rates, sums, in_sem, out_sem, sem = scratch
    start, count = lists_ref[REST_AT], lists_ref[REST_AT + 1]
    rows = [pl.ds(8 * i, 8) for i in range(8)]
    waits = fetch([(state_any.at[row], state.at[row]) for row in rows], in_sem)

    def put(source, b):
        species[pl.ds(b, 53, stride=64), :] = source[b, pl.ds(0, 53), :]
        heat[pl.ds(b, 1), :] = source[b, pl.ds(53, 1), :]

    copies = []
    for i, row in enumerate(rows):
        waits[i]()
        for j in range(8):
            put(state, 8 * i + j)
        view = species.reshape(53, 64, 128).at[:, row]
        copies.append(pltpu.make_async_copy(view, species_any.at[:, row], out_sem.at[i]))
        copies[-1].start()
    copies.append(pltpu.make_async_copy(heat, heat_any, out_sem.at[8]))
    copies[-1].start()
    for copy in copies:
        copy.wait()

    def bring(source, target):
        copy = pltpu.make_async_copy(source, target, sem)
        copy.start()
        copy.wait()

    @pl.when(start < count)
    def _():
        bring(rates_any, rates)
        bring(sums_any, sums)

        def group(g, carry):
            first = start + g * GROUP
            at = [blocks_ref[0, jnp.minimum(first + k, 63)] for k in range(GROUP)]
            value = jnp.concatenate([state[at[k]] for k in range(GROUP)], 1)
            value = subcycles(value, rates, sums)
            for k in range(GROUP):

                @pl.when(first + k < count)
                def _():
                    work[at[k]] = value[:, k * 128 : (k + 1) * 128]
                    put(work, at[k])

            return carry

        lax.fori_loop(0, (count - start + GROUP - 1) // GROUP, group, 0)
        bring(species.reshape(53, 64, 128), species_any)
        bring(heat, heat_any)


def finish(lists, blocks, state, rates, sums):
    smem, anywhere = pl.BlockSpec(memory_space=pltpu.SMEM), pl.BlockSpec(memory_space=pl.ANY)
    return pl.pallas_call(
        last_kernel,
        out_shape=[jax.ShapeDtypeStruct((53, 64, 128), F32), jax.ShapeDtypeStruct((64, 128), F32)],
        in_specs=[smem, smem] + [anywhere] * 3,
        out_specs=[anywhere] * 2,
        scratch_shapes=[
            pltpu.VMEM(state.shape, F32),
            pltpu.VMEM(state.shape, F32),
            pltpu.VMEM((53 * 64, 128), F32),
            pltpu.VMEM((64, 128), F32),
            pltpu.VMEM(rates.shape, BF16),
            pltpu.VMEM(sums.shape, BF16),
            pltpu.SemaphoreType.DMA((8,)),
            pltpu.SemaphoreType.DMA((9,)),
            pltpu.SemaphoreType.DMA(()),
        ],
        compiler_params=pltpu.CompilerParams(vmem_limit_bytes=LIMIT),
    )(lists, blocks, state, rates, sums)


def shifted(axis, step):
    n, me = lax.axis_size(axis), lax.axis_index(axis)
    return {axis: lax.rem(me + (n + step), n)}


def faces():
    return [shifted(axis, step) for axis in AXES for step in (-1, 1)]


def partners():
    me = lax.axis_index("stream")
    sides = [("stream", 2), ("stream", -2), ("radial", 1), ("radial", -1), ("azim", 1), ("azim", -1)]
    return [{"stream": me + 1 - 2 * lax.rem(me, 2)}] + [shifted(*side) for side in sides]


def greet(peers):
    barrier = pltpu.get_barrier_semaphore()
    for peer in peers:
        pl.semaphore_signal(barrier, inc=1, device_id=peer, device_id_type=MESH)
    return lambda: pl.semaphore_wait(barrier, len(peers))


def remote(source, target, sems, k, peer):
    return pltpu.make_async_remote_copy(
        src_ref=source,
        dst_ref=target,
        send_sem=sems[0].at[k],
        recv_sem=sems[1].at[k],
        device_id=peer,
        device_id_type=MESH,
    )


def transport(met, courant_ref, spread_ref, out, grid, edge, halo, sems, hooks):
    lane = lax.broadcasted_iota(jnp.int32, (ROWS, 128), 1)
    peers = faces()
    inner = pl.ds(1, 8)
    plans = [
        (grid.at[1, inner], grid.at[9, inner]),
        (grid.at[8, inner], grid.at[0, inner]),
        (grid.at[inner, 1], grid.at[inner, 9]),
        (grid.at[inner, 8], grid.at[inner, 0]),
        (edge.at[0], halo.at[1]),
        (edge.at[1], halo.at[0]),
    ]
    copies = [remote(*plans[k], sems, k, peers[k]) for k in range(6)]
    met()
    for k in (2, 3, 0, 1):
        copies[k].start()

    def ends(i, carry):
        low, high = carry
        for j in range(8):
            b = i * 8 + j
            here = grid[i + 1, j + 1]
            low = jnp.where(lane == b, pltpu.roll(here, b, 1), low)
            high = jnp.where(lane == b, pltpu.roll(here, b + 1, 1), high)
        return low, high

    low, high = lax.fori_loop(0, 8, ends, (jnp.zeros((ROWS, 128), F32),) * 2)
    edge[0] = low
    edge[1] = high
    copies[4].start()
    copies[5].start()
    hooks[0]()
    copies[4].wait()
    copies[5].wait()
    rate = spread_ref[...]
    keep = 1.0 - 6.0 * rate

    def cells(i, columns):
        for j in columns:
            b = i * 8 + j
            here = grid[i + 1, j + 1]
            behind = grid[i, j + 1]
            low = pltpu.roll(halo[0], lax.rem(128 - b, 128), 1)
            high = pltpu.roll(halo[1], 127 - b, 1)
            left = jnp.where(lane == 0, low, pltpu.roll(here, 1, 1))
            right = jnp.where(lane == 127, high, pltpu.roll(here, 127, 1))
            around = (behind + grid[i + 2, j + 1]) + (grid[i + 1, j] + grid[i + 1, j + 2])
            around = around + (left + right)
            speed = courant_ref[pl.ds(b, 1), :]
            out[b] = (keep - speed) * here + rate * around + speed * behind

    def middle(i, carry):
        cells(i, range(1, 7))
        return carry

    lax.fori_loop(1, 7, middle, 0)
    hooks[1]()
    for k in range(4):
        copies[k].wait()
    blank = jnp.zeros((8, ROWS, 128), F32)
    stream, radial = lax.axis_index("stream"), lax.axis_index("radial")

    @pl.when(stream == 0)
    def _():
        grid[0, inner] = blank

    @pl.when(stream == lax.axis_size("stream") - 1)
    def _():
        grid[9, inner] = blank

    @pl.when(radial == 0)
    def _():
        grid[inner, 0] = blank

    @pl.when(radial == lax.axis_size("radial") - 1)
    def _():
        grid[inner, 9] = blank

    def sides(i, carry):
        cells(i, (0, 7))
        return carry

    def first_last(i, carry):
        cells(i * 7, range(1, 7))
        return carry

    lax.fori_loop(0, 8, sides, 0)
    lax.fori_loop(0, 2, first_last, 0)
    hooks[2]()


def chemistry(lists_ref, state, rates_ref, sums_ref, out, send, recv, reply, back, result, sems, met):
    def pack(s, carry):
        send[s] = state[lists_ref[SEND_AT + s]]
        return carry

    lax.fori_loop(0, SLOTS, pack, 0)
    met()
    peers = partners()

    def exchange(source, target, first, turned):
        found = []
        for k, (base, size) in enumerate(zip(BASES, SIZES)):
            area = pl.ds(base, size)
            peer = peers[OPPOSITE[k] if turned else k]
            found.append(remote(source.at[area], target.at[area], sems, first + k, peer))
            found[-1].start()
        return found

    def run(first, items):
        whole = subcycles(jnp.concatenate(items, 1), rates_ref, sums_ref)
        for k in range(len(items)):
            result[first + k] = whole[:, k * 128 : (k + 1) * 128]

    def own(first):
        run(first, [state[lists_ref[WORK_AT + first + k]] for k in range(GROUP)])

    def any_item(slot):
        code = lists_ref[WORK_AT + slot]
        there = recv[jnp.maximum(code - 64, 0)]
        return jnp.where(code < 64, state[jnp.minimum(code, 63)], there)

    def middle(g, carry):
        first = EARLY + g * GROUP
        run(first, [any_item(first + k) for k in range(GROUP)])
        return carry

    copies = exchange(send, recv, 0, False)
    own(0)
    for copy in copies:
        copy.wait()
    lax.fori_loop(0, SPAN // GROUP, middle, 0)

    def answer(s, carry):
        reply[s] = result[lists_ref[REPLY_AT + s]]
        return carry

    lax.fori_loop(0, SLOTS, answer, 0)
    copies = exchange(reply, back, 7, True)
    own(WORK - LATE)
    for copy in copies:
        copy.wait()

    def settle(b, carry):
        code = lists_ref[FINAL_AT + b]
        here = state[jnp.minimum(code, 63)]
        there = back[jnp.clip(code - 64, 0, SLOTS - 1)]
        done = result[jnp.clip(code - 128, 0, WORK - 1)]
        out[b] = jnp.where(code < 64, here, jnp.where(code < 128, there, done))
        return carry

    lax.fori_loop(0, 64, settle, 0)


STATE = (64, ROWS, 128)
MOVE_SCRATCH = [
    pltpu.VMEM((10, 10, ROWS, 128), F32),
    pltpu.VMEM((2, ROWS, 128), F32),
    pltpu.VMEM((2, ROWS, 128), F32),
    pltpu.SemaphoreType.DMA((6,)),
    pltpu.SemaphoreType.DMA((6,)),
]
CHEM_SCRATCH = [pltpu.VMEM((SLOTS, ROWS, 128), F32)] * 4 + [
    pltpu.VMEM((WORK, ROWS, 128), F32),
    pltpu.SemaphoreType.DMA((14,)),
    pltpu.SemaphoreType.DMA((14,)),
]


COUNT_SCRATCH = [
    pltpu.VMEM((8, 8, 128), jnp.int32),
    pltpu.VMEM((4, 8, 128), jnp.int32),
    pltpu.VMEM((4, 4, 8, 128), jnp.int32),
    pltpu.SemaphoreType.DMA((13,)),
    pltpu.SemaphoreType.DMA((13,)),
    pltpu.VMEM((8, 128), jnp.int32),
    pltpu.SMEM((8, 128), jnp.int32),
    pltpu.SemaphoreType.DMA(()),
    pltpu.VMEM((2 * ROWS, 768), F32),
]


def others(axis):
    return [shifted(axis, step) for step in range(1, lax.axis_size(axis))]


def spread_counts(first, second, third, sems):
    stream, radial, azim = (lax.axis_index(axis) for axis in AXES)

    def stage(source, target, axis, start):
        copies = [remote(source, target, sems, start + k, p) for k, p in enumerate(others(axis))]
        for copy in copies:
            copy.start()

        def wait():
            for copy in copies:
                copy.wait()

        return wait

    def along_stream():
        return stage(first.at[stream], first.at[stream], "stream", 0)

    def along_radial():
        row = lax.broadcasted_iota(jnp.int32, (8, 128), 0)
        joined = first[0]
        for s in range(1, 8):
            joined = jnp.where(row == s, first[s], joined)
        second[radial] = joined
        return stage(second.at[radial], second.at[radial], "radial", 7)

    def along_azim():
        third[azim] = second[...]
        return stage(third.at[azim], third.at[azim], "azim", 10)

    def whole():
        row = lax.broadcasted_iota(jnp.int32, (8, 128), 0)
        lane = lax.broadcasted_iota(jnp.int32, (8, 128), 1)
        total = jnp.zeros((8, 128), jnp.int32)
        for a in range(4):
            for r in range(4):
                here = (lane & 15 == r * 4 + a) & (lane >> 4 == row)
                total = jnp.where(here, third[a, r], total)
        return jnp.broadcast_to(jnp.sum(total, 0, keepdims=True), (8, 128))

    return along_stream, along_radial, along_azim, whole


def communicating(kernel, name, out_shape, out_specs, specs, args, scratch):
    return pl.pallas_call(
        kernel,
        out_shape=out_shape,
        in_specs=specs,
        out_specs=out_specs,
        scratch_shapes=scratch,
        compiler_params=pltpu.CompilerParams(
            collective_id=name, has_side_effects=True, vmem_limit_bytes=LIMIT
        ),
    )(*args)


def first_step(blocks, tally, species, heat, courant, spread, settings):
    nrxn = settings[0].shape[1]
    padded = -(-nrxn // 8) * 8
    brought = (tally, species, heat, courant, spread, *settings)

    def kernel(blocks_ref, *refs):
        anywhere, refs = refs[: len(brought)], refs[len(brought) :]
        out, lists, rates, sums, spread_out = refs[:5]
        near, refs = refs[5 : 5 + len(brought)], refs[5 + len(brought) :]
        fetch_sem, refs = refs[0], refs[1:]
        tally_ref, species_ref, heat_ref, courant_ref, spread_ref, *settings_refs = near
        grid, edge, halo, *sems = refs[: len(MOVE_SCRATCH)]
        refs = refs[len(MOVE_SCRATCH) :]
        first, second, third, *count_sems = refs[:5]
        codes, codes_smem, code_sem, table = refs[5:9]
        moved, *chem = refs[9:]

        met = greet(others("stream") + others("radial") + others("azim"))
        waits = fetch(list(zip(anywhere, near)), fetch_sem)
        stream, radial, azim = (lax.axis_index(axis) for axis in AXES)
        me = (stream * 4 + radial) * 4 + azim
        waits[0]()
        own = jnp.sum(tally_ref[...], 1, keepdims=True)
        first[stream] = jnp.broadcast_to(own, (8, 128))
        stages = spread_counts(first, second, third, count_sems)
        waits[1]()
        waits[2]()

        def load(i, carry):
            for j in range(8):
                b = i * 8 + j
                cell = grid.at[i + 1, j + 1]
                cell[pl.ds(0, 53), :] = species_ref[pl.ds(b, 53, stride=64), :]
                cell[pl.ds(53, 1), :] = heat_ref[pl.ds(b, 1), :]
                cell[pl.ds(54, 2), :] = jnp.zeros((2, 128), F32)
            return carry

        lax.fori_loop(0, 8, load, 0)
        waiting = []

        def ready():
            met()
            waiting.append(stages[0]())

        def at_once():
            for wait in waits[3:]:
                wait()
            table[pl.ds(0, 1), pl.ds(0, 128)] = jnp.zeros((1, 128), F32)
            table[pl.ds(0, 1), pl.ds(0, 54)] = spread_ref[...].reshape(1, 54)
            row = lax.broadcasted_iota(jnp.int32, (ROWS, 128), 0)
            lane = lax.broadcasted_iota(jnp.int32, (ROWS, 128), 1)
            diagonal = jnp.where(row == lane, table[pl.ds(0, 1), pl.ds(0, 128)], 0.0)
            column = jnp.sum(diagonal, 1, keepdims=True)
            spread_out[...] = jnp.broadcast_to(column, (ROWS, 128))
            waiting[0]()
            waiting.append(stages[1]())
            prepare(*settings_refs, rates, sums, table)
            waiting[1]()
            waiting.append(stages[2]())

        def at_end():
            waiting[2]()
            plan(me, stages[3](), blocks_ref, lists, codes, codes_smem, code_sem)

        hooks = (at_once, lambda: None, at_end)
        transport(ready, courant_ref, spread_out, moved, grid, edge, halo, sems, hooks)
        chemistry(lists, moved, rates, sums, out, *chem[:5], chem[5:], lambda: None)

    smem, vmem = pl.BlockSpec(memory_space=pltpu.SMEM), pl.BlockSpec(memory_space=pltpu.VMEM)
    return communicating(
        kernel,
        0,
        [
            jax.ShapeDtypeStruct(STATE, F32),
            jax.ShapeDtypeStruct((256,), jnp.int32),
            jax.ShapeDtypeStruct((2 * padded, 4 * ROWS), BF16),
            jax.ShapeDtypeStruct((4 * ROWS, 2 * padded), BF16),
            jax.ShapeDtypeStruct((ROWS, 128), F32),
        ],
        [vmem, smem, vmem, vmem, vmem],
        [smem] + [pl.BlockSpec(memory_space=pl.ANY)] * len(brought),
        (blocks, *brought),
        [pltpu.VMEM(x.shape, x.dtype) for x in brought]
        + [pltpu.SemaphoreType.DMA((len(brought),))]
        + MOVE_SCRATCH
        + COUNT_SCRATCH
        + [pltpu.VMEM(STATE, F32)]
        + CHEM_SCRATCH,
    )


def second_step(lists, state, courant, spread, rates, sums):
    brought = (courant, spread, rates, sums)

    def kernel(lists_ref, state_any, *refs):
        anywhere, refs = refs[: len(brought)], refs[len(brought) :]
        out, near, refs = refs[0], refs[1 : 1 + len(brought)], refs[1 + len(brought) :]
        fetch_sem, refs = refs[0], refs[1:]
        courant_ref, spread_ref, rates_ref, sums_ref = near
        grid, edge, halo, *sems = refs[: len(MOVE_SCRATCH)]
        moved, *chem = refs[len(MOVE_SCRATCH) :]
        met = greet(faces() + [shifted("stream", 2), shifted("stream", -2)])
        pairs = [
            (state_any.at[pl.ds(8 * i, 8)], grid.at[i + 1, pl.ds(1, 8)]) for i in range(8)
        ]
        waits = fetch(pairs + list(zip(anywhere, near)), fetch_sem)
        for wait in waits:
            wait()
        nothing = lambda: None
        hooks = (nothing, nothing, nothing)
        transport(met, courant_ref, spread_ref, moved, grid, edge, halo, sems, hooks)
        chemistry(lists_ref, moved, rates_ref, sums_ref, out, *chem[:5], chem[5:], nothing)

    smem, vmem = pl.BlockSpec(memory_space=pltpu.SMEM), pl.BlockSpec(memory_space=pltpu.VMEM)
    return communicating(
        kernel,
        1,
        jax.ShapeDtypeStruct(STATE, F32),
        vmem,
        [smem] + [pl.BlockSpec(memory_space=pl.ANY)] * 5,
        (lists, state, *brought),
        [pltpu.VMEM(x.shape, x.dtype) for x in brought]
        + [pltpu.SemaphoreType.DMA((8 + len(brought),))]
        + MOVE_SCRATCH
        + [pltpu.VMEM(STATE, F32)]
        + CHEM_SCRATCH,
    )


def shards(
    component_fractions,
    kilokelvin_field,
    axial_courant_number,
    spreading_number,
    arrhenius_multiplier_exponent,
    thermal_exponents,
    arrhenius_barrier,
    balance_constant_exponents,
    enthalpy_formation,
    consumed_stoich_matrix,
    yield_stoich_matrix,
    processor_tiles_burning,
    tile_transfer_tally,
):
    shape = component_fractions.shape
    settings = (
        consumed_stoich_matrix,
        yield_stoich_matrix,
        arrhenius_multiplier_exponent,
        thermal_exponents,
        arrhenius_barrier,
        balance_constant_exponents,
        enthalpy_formation,
    )
    species = component_fractions.reshape(53 * 64, 128)
    heat = kilokelvin_field.reshape(64, 128)
    courant = axial_courant_number.reshape(64, 128)
    blocks, tally = processor_tiles_burning, tile_transfer_tally
    state, lists, rates, sums, spread = first_step(
        blocks, tally, species, heat, courant, spreading_number, settings
    )
    state = react_rest(lists, blocks, state, rates, sums)
    state = second_step(lists, state, courant, spread, rates, sums)
    species, heat = finish(lists, blocks, state, rates, sums)
    return species.reshape(shape), heat.reshape(shape[1:])


def solution(mesh):
    in_specs = (
        P(None, "stream", "radial", "azim"),
        P("stream", "radial", "azim"),
        P("stream", "radial", "azim"),
        P(),
        P(),
        P(),
        P(),
        P(),
        P(),
        P(),
        P(),
        P(AXES, None),
        P(AXES, None),
    )
    out_specs = (P(None, "stream", "radial", "azim"), P("stream", "radial", "azim"))
    return jax.shard_map(shards, mesh=mesh, in_specs=in_specs, out_specs=out_specs, check_vma=False)
```

```python
import functools

import jax
import jax.numpy as jnp
from jax import lax
from jax.experimental import pallas as pl
from jax.experimental.pallas import tpu as pltpu
from jax.sharding import PartitionSpec as P

NCYC = 4
ROWS = 56
GROUP = 8
chem_step = 0.02
mass_offset = 0.05
LOG2E = 1.4426950408889634
F32 = jnp.float32
BF16 = jnp.bfloat16
MESH = pl.DeviceIdType.MESH
AXES = ("stream", "radial", "azim")
LIMIT = 63 * 2**20
WORK = 32
EARLY = 8
LATE = 8
SPAN = WORK - EARLY - LATE
FLOOR = 24
SWEEPS = 2
PAIR = 16
SIDE = 6
SIZES = (PAIR,) + (SIDE,) * 6
BASES = tuple(sum(SIZES[:k]) for k in range(7))
SLOTS = sum(SIZES)
OPPOSITE = (0, 2, 1, 4, 3, 6, 5)
SEND, WORK_ROW, REPLY, FINAL, REST = range(5)


def prepare(consumed, made, exponent, thermal, barrier, balance, enthalpy, rates, sums, table):
    half = rates.shape[0] // 2
    exponent, thermal, barrier, balance, enthalpy = (
        vector[...].reshape(1, -1) for vector in (exponent, thermal, barrier, balance, enthalpy)
    )

    def put(side, row, value):
        rows, lanes = value.shape
        table[pl.ds(row, rows), pl.ds(side * half, lanes)] = value

    def halves(value):
        high = value.astype(BF16).astype(F32)
        return high, value - high

    table[...] = jnp.zeros_like(table)
    for side, change in enumerate((0.0, balance)):
        put(side, 0, (consumed, made)[side][...])
        put(side, 53, thermal)
        put(side, 54, -LOG2E * barrier)
        put(side, 55, LOG2E * (exponent - change))
    high, low = halves(table[:ROWS])
    stacked = jnp.concatenate([high, high, low, high], 0).T
    rates[...] = stacked[: 2 * half].astype(BF16)
    heat = LOG2E * lax.dot_general(
        enthalpy,
        made[...] - consumed[...],
        (((1,), (0,)), ((), ())),
        preferred_element_type=F32,
        precision=lax.Precision.HIGHEST,
    )
    table[...] = jnp.zeros_like(table)
    for side, (gain, loss, warm) in enumerate(((made, consumed, heat), (consumed, made, -heat))):
        put(side, 0, gain[...])
        put(side, 53, warm)
        put(side, ROWS, loss[...])
    high, low = halves(chem_step * table[...])
    sums[...] = jnp.concatenate([high, low], 0)[:, : 2 * half].astype(BF16)


def parted(value):
    high = value.astype(BF16)
    return high, value - high.astype(F32)


def product(a, b):
    return lax.dot_general(a, b, (((1,), (0,)), ((), ())), preferred_element_type=F32)


def cycle(state, rates, sums):
    row = lax.broadcasted_iota(jnp.int32, state.shape, 0)
    moved = state + jnp.where(row < 53, mass_offset, jnp.where(row == 53, 0.0, 1.0))
    heat = state[53:54]
    logs = jnp.log2(moved)
    logs = jnp.where(row == 54, 1.0 / heat, jnp.where(row == 55, 1.0, logs))
    first, rest = parted(logs)
    second, third = parted(rest)
    first, second = first.astype(F32), second.astype(F32)
    stacked = jnp.concatenate([first, second, first, third], 0).astype(BF16)
    flux = jnp.exp2(product(rates, stacked))
    high, low = parted(flux)
    half = sums.shape[0] // 2
    both = product(sums, high)
    total = both[:half] + both[half:] + product(sums[:half], low.astype(BF16))
    gain, loss = total[:ROWS], total[ROWS:]
    species = (state + gain) * moved / (moved + loss)
    return jnp.where(row == 53, heat * jnp.exp2(gain[53:54]), species)


def toward(value, k):
    lane = lax.broadcasted_iota(jnp.int32, value.shape, 1)
    azim, radial, core = lane & 3, (lane >> 2) & 3, (lane >> 4) & 1

    def ahead(step):
        return pltpu.roll(value, (128 - step) % 128, 1)

    return (
        lambda: jnp.where(core == 0, ahead(16), ahead(-16)),
        lambda: ahead(32),
        lambda: ahead(-32),
        lambda: jnp.where(radial < 3, ahead(4), ahead(-12)),
        lambda: jnp.where(radial > 0, ahead(-4), ahead(12)),
        lambda: jnp.where(azim < 3, ahead(1), ahead(-3)),
        lambda: jnp.where(azim > 0, ahead(-1), ahead(3)),
    )[k]()


def flows(counts):
    load, own = jnp.maximum(counts, EARLY + LATE), counts
    given = [jnp.zeros_like(counts) for _ in SIZES]
    taken = [jnp.zeros_like(counts) for _ in SIZES]
    for sweep in range(SWEEPS):
        for k, size in enumerate(SIZES):
            other = toward(load, k)
            gap = load - other + (1 if sweep == SWEEPS - 1 else 0)
            spare = jnp.maximum(own - (EARLY + LATE), 0)
            give = jnp.minimum(jnp.minimum(size - given[k], spare), jnp.maximum(gap, 0) >> 1)
            give = jnp.minimum(give, jnp.maximum(load - FLOOR, 0))
            give = jnp.minimum(give, jnp.maximum(WORK - other, 0))
            take = toward(give, OPPOSITE[k])
            given[k], taken[k] = given[k] + give, taken[k] + take
            own, load = own - give, load - give + take
    return own, given, taken


def positions(blocks_ref):
    lane = lax.broadcasted_iota(jnp.int32, (8, 128), 1)
    found = jnp.zeros((8, 128), jnp.int32)
    for n in range(64):
        found = jnp.where(lane == blocks_ref[0, n], n, found)
    return found


def plan(me, counts, position, blocks_ref, codes, lists, sem):
    own, given, taken = flows(counts)
    row = lax.broadcasted_iota(jnp.int32, (8, 128), 0)
    lane = lax.broadcasted_iota(jnp.int32, (8, 128), 1)

    def mine(value):
        return jnp.sum(jnp.where(lane == me, value, 0), 1, keepdims=True)

    own, total = mine(own), mine(counts)
    given, taken = [mine(v) for v in given], [mine(v) for v in taken]
    received = sum(taken)
    kept = jnp.minimum(own, WORK - received)
    sent_before, taken_before = [kept], [jnp.zeros_like(kept)]
    for p in range(len(SIZES)):
        sent_before.append(sent_before[p] + given[p])
        taken_before.append(taken_before[p] + taken[p])

    late = WORK - LATE - EARLY + position
    middle = received + position - LATE
    slot = jnp.where(position < EARLY, position, jnp.where(position < EARLY + LATE, late, middle))
    final = jnp.where(position < kept, 128 + slot, lane)
    send, reply = jnp.zeros((8, 128), jnp.int32), jnp.zeros((8, 128), jnp.int32)
    step = lane - EARLY
    arrived = jnp.zeros((8, 128), jnp.int32)
    for p, (base, size) in enumerate(zip(BASES, SIZES)):
        inside = (position >= sent_before[p]) & (position < sent_before[p + 1])
        final = jnp.where(inside, 64 + base + position - sent_before[p], final)
        here = (lane >= base) & (lane < base + size)
        send = jnp.where(here, sent_before[p] + lane - base, send)
        reply = jnp.where(here, EARLY + taken_before[p] + lane - base, reply)
        inside = (step >= taken_before[p]) & (step < taken_before[p + 1])
        arrived = jnp.where(inside, 64 + base + step - taken_before[p], arrived)
    place = jnp.where(lane < EARLY, lane, EARLY + LATE + step - received)
    place = jnp.where(lane >= WORK - LATE, lane - (WORK - LATE - EARLY), place)
    wanted = jnp.clip(jnp.where(row == SEND, send, place), 0, 63)
    value = jnp.zeros((8, 128), jnp.int32)
    for n in range(64):
        value = jnp.where(wanted == n, blocks_ref[0, n], value)
    value = jnp.where((row == WORK_ROW) & (arrived > 0), arrived, value)
    value = jnp.where(row == REPLY, jnp.clip(reply, 0, WORK - 1), value)
    value = jnp.where(row == FINAL, final, value)
    value = jnp.where(row == REST, jnp.where(lane == 0, sent_before[-1], total), value)
    codes[...] = value
    copy = pltpu.make_async_copy(codes, lists, sem)
    copy.start()
    copy.wait()


def fetch(pairs, sem):
    copies = [pltpu.make_async_copy(*pair, sem.at[k]) for k, pair in enumerate(pairs)]
    for copy in copies:
        copy.start()
    return [copy.wait for copy in copies]


def subcycles(state, rates_ref, sums_ref):
    return lax.fori_loop(0, NCYC, lambda c, s: cycle(s, rates_ref[...], sums_ref[...]), state)


def rest_kernel(lists_ref, blocks_ref, state_ref, rates_any, sums_any, out_ref, rates, sums, held, sem):
    start, count = lists_ref[REST, 0], lists_ref[REST, 1]

    def bring(source, target):
        copy = pltpu.make_async_copy(source, target, sem)
        copy.start()
        copy.wait()

    @pl.when(start < count)
    def _():
        bring(rates_any, rates)
        bring(sums_any, sums)

        def group(g, carry):
            first = start + g * GROUP
            for k in range(GROUP):
                bring(out_ref.at[blocks_ref[0, jnp.minimum(first + k, 63)]], held.at[k])
            state = jnp.concatenate([held[k] for k in range(GROUP)], 1)
            state = subcycles(state, rates, sums)
            for k in range(GROUP):
                held[k] = state[:, k * 128 : (k + 1) * 128]

                @pl.when(first + k < count)
                def _():
                    bring(held.at[k], out_ref.at[blocks_ref[0, jnp.minimum(first + k, 63)]])

            return carry

        lax.fori_loop(0, (count - start + GROUP - 1) // GROUP, group, 0)


def react_rest(lists, blocks, state, rates, sums):
    smem, anywhere = pl.BlockSpec(memory_space=pltpu.SMEM), pl.BlockSpec(memory_space=pl.ANY)
    return pl.pallas_call(
        rest_kernel,
        out_shape=jax.ShapeDtypeStruct(state.shape, F32),
        in_specs=[smem, smem] + [anywhere] * 3,
        out_specs=anywhere,
        scratch_shapes=[
            pltpu.VMEM(rates.shape, BF16),
            pltpu.VMEM(sums.shape, BF16),
            pltpu.VMEM((GROUP, ROWS, 128), F32),
            pltpu.SemaphoreType.DMA(()),
        ],
        input_output_aliases={2: 0},
        compiler_params=pltpu.CompilerParams(vmem_limit_bytes=LIMIT),
    )(lists, blocks, state, rates, sums)


def last_kernel(
    lists_ref, blocks_ref, state_any, rates_any, sums_any, species_any, heat_any, *scratch
):
    state, species, heat, rates, sums, in_sem, out_sem, sem = scratch
    start, count = lists_ref[REST, 0], lists_ref[REST, 1]
    rows = [pl.ds(8 * i, 8) for i in range(8)]
    waits = fetch([(state_any.at[row], state.at[row]) for row in rows], in_sem)
    copies = []
    for i, row in enumerate(rows):
        waits[i]()
        turned = jnp.swapaxes(state[row], 0, 1)
        species[:, row] = turned[:53]
        heat[row] = turned[53]
        copies.append(
            pltpu.make_async_copy(species.at[:, row], species_any.at[:, row], out_sem.at[i])
        )
        copies[-1].start()
    copies.append(pltpu.make_async_copy(heat, heat_any, out_sem.at[8]))
    copies[-1].start()
    for copy in copies:
        copy.wait()

    def bring(source, target):
        copy = pltpu.make_async_copy(source, target, sem)
        copy.start()
        copy.wait()

    @pl.when(start < count)
    def _():
        bring(rates_any, rates)
        bring(sums_any, sums)

        def group(g, carry):
            first = start + g * GROUP
            at = [blocks_ref[0, jnp.minimum(first + k, 63)] for k in range(GROUP)]
            value = jnp.concatenate([state[at[k]] for k in range(GROUP)], 1)
            value = subcycles(value, rates, sums)
            for k in range(GROUP):

                @pl.when(first + k < count)
                def _():
                    state[at[k]] = value[:, k * 128 : (k + 1) * 128]

            return carry

        lax.fori_loop(0, (count - start + GROUP - 1) // GROUP, group, 0)
        for row in rows:
            turned = jnp.swapaxes(state[row], 0, 1)
            species[:, row] = turned[:53]
            heat[row] = turned[53]
        bring(species, species_any)
        bring(heat, heat_any)


def finish(lists, blocks, state, rates, sums):
    smem, anywhere = pl.BlockSpec(memory_space=pltpu.SMEM), pl.BlockSpec(memory_space=pl.ANY)
    return pl.pallas_call(
        last_kernel,
        out_shape=[jax.ShapeDtypeStruct((53, 64, 128), F32), jax.ShapeDtypeStruct((64, 128), F32)],
        in_specs=[smem, smem] + [anywhere] * 3,
        out_specs=[anywhere] * 2,
        scratch_shapes=[
            pltpu.VMEM(state.shape, F32),
            pltpu.VMEM((53, 64, 128), F32),
            pltpu.VMEM((64, 128), F32),
            pltpu.VMEM(rates.shape, BF16),
            pltpu.VMEM(sums.shape, BF16),
            pltpu.SemaphoreType.DMA((8,)),
            pltpu.SemaphoreType.DMA((9,)),
            pltpu.SemaphoreType.DMA(()),
        ],
        compiler_params=pltpu.CompilerParams(vmem_limit_bytes=LIMIT),
    )(lists, blocks, state, rates, sums)


def shifted(axis, step):
    n, me = lax.axis_size(axis), lax.axis_index(axis)
    return {axis: lax.rem(me + (n + step), n)}


def faces():
    return [shifted(axis, step) for axis in AXES for step in (-1, 1)]


def partners():
    me = lax.axis_index("stream")
    sides = [("stream", 2), ("stream", -2), ("radial", 1), ("radial", -1), ("azim", 1), ("azim", -1)]
    return [{"stream": me + 1 - 2 * lax.rem(me, 2)}] + [shifted(*side) for side in sides]


def greet(peers):
    barrier = pltpu.get_barrier_semaphore()
    for peer in peers:
        pl.semaphore_signal(barrier, inc=1, device_id=peer, device_id_type=MESH)
    return lambda: pl.semaphore_wait(barrier, len(peers))


def remote(source, target, sems, k, peer):
    return pltpu.make_async_remote_copy(
        src_ref=source,
        dst_ref=target,
        send_sem=sems[0].at[k],
        recv_sem=sems[1].at[k],
        device_id=peer,
        device_id_type=MESH,
    )


def transport(met, courant_ref, spread_ref, out, grid, edge, halo, sems, hooks):
    lane = lax.broadcasted_iota(jnp.int32, (ROWS, 128), 1)
    peers = faces()
    inner = pl.ds(1, 8)
    plans = [
        (grid.at[1, inner], grid.at[9, inner]),
        (grid.at[8, inner], grid.at[0, inner]),
        (grid.at[inner, 1], grid.at[inner, 9]),
        (grid.at[inner, 8], grid.at[inner, 0]),
        (edge, halo.at[1]),
        (edge, halo.at[0]),
    ]
    copies = [remote(*plans[k], sems, k, peers[k]) for k in range(6)]
    met()
    for k in (2, 3, 0, 1):
        copies[k].start()

    def ends(i, packed):
        for j in range(8):
            b = i * 8 + j
            turned = pltpu.roll(grid[i + 1, j + 1], 2 * b + 1, 1)
            packed = jnp.where((lane >> 1) == b, turned, packed)
        return packed

    edge[...] = lax.fori_loop(0, 8, ends, jnp.zeros((ROWS, 128), F32))
    copies[4].start()
    copies[5].start()
    hooks[0]()
    copies[4].wait()
    copies[5].wait()
    edge[...] = jnp.where((lane & 1) == 0, halo[0], halo[1])
    rate = spread_ref[...]
    keep = 1.0 - 6.0 * rate

    def cells(i, columns):
        for j in columns:
            b = i * 8 + j
            here = grid[i + 1, j + 1]
            behind = grid[i, j + 1]
            ends = pltpu.roll(edge[...], 127 - 2 * b, 1)
            left = pltpu.roll(jnp.where(lane == 127, ends, here), 1, 1)
            right = pltpu.roll(jnp.where(lane == 0, ends, here), 127, 1)
            around = (behind + grid[i + 2, j + 1]) + (grid[i + 1, j] + grid[i + 1, j + 2])
            around = around + (left + right)
            speed = courant_ref[pl.ds(b, 1), :]
            out[b] = (keep - speed) * here + rate * around + speed * behind

    def middle(i, carry):
        cells(i, range(1, 7))
        return carry

    lax.fori_loop(1, 7, middle, 0)
    hooks[1]()
    for k in range(4):
        copies[k].wait()
    blank = jnp.zeros((8, ROWS, 128), F32)
    stream, radial = lax.axis_index("stream"), lax.axis_index("radial")

    @pl.when(stream == 0)
    def _():
        grid[0, inner] = blank

    @pl.when(stream == lax.axis_size("stream") - 1)
    def _():
        grid[9, inner] = blank

    @pl.when(radial == 0)
    def _():
        grid[inner, 0] = blank

    @pl.when(radial == lax.axis_size("radial") - 1)
    def _():
        grid[inner, 9] = blank

    def sides(i, carry):
        cells(i, (0, 7))
        return carry

    def first_last(i, carry):
        cells(i * 7, range(1, 7))
        return carry

    lax.fori_loop(0, 8, sides, 0)
    lax.fori_loop(0, 2, first_last, 0)


def chemistry(lists_ref, state, rates_ref, sums_ref, out, send, recv, reply, back, result, sems, met):
    def each(count, body):
        def four(g, carry):
            for k in range(4):
                body(4 * g + k)
            return carry

        lax.fori_loop(0, count // 4, four, 0)

    def pack(s):
        send[s] = state[lists_ref[SEND, s]]

    each(SLOTS, pack)
    met()
    peers = partners()

    def exchange(source, target, first, turned):
        found = []
        for k, (base, size) in enumerate(zip(BASES, SIZES)):
            area = pl.ds(base, size)
            peer = peers[OPPOSITE[k] if turned else k]
            found.append(remote(source.at[area], target.at[area], sems, first + k, peer))
            found[-1].start()
        return found

    def run(first, items):
        whole = subcycles(jnp.concatenate(items, 1), rates_ref, sums_ref)
        for k in range(len(items)):
            result[first + k] = whole[:, k * 128 : (k + 1) * 128]

    def own(first):
        run(first, [state[lists_ref[WORK_ROW, first + k]] for k in range(GROUP)])

    def any_item(slot):
        code = lists_ref[WORK_ROW, slot]
        there = recv[jnp.maximum(code - 64, 0)]
        return jnp.where(code < 64, state[jnp.minimum(code, 63)], there)

    def middle(g, carry):
        first = EARLY + g * GROUP
        run(first, [any_item(first + k) for k in range(GROUP)])
        return carry

    copies = exchange(send, recv, 0, False)
    own(0)
    for copy in copies:
        copy.wait()
    lax.fori_loop(0, SPAN // GROUP, middle, 0)

    def answer(s):
        reply[s] = result[lists_ref[REPLY, s]]

    each(SLOTS, answer)
    copies = exchange(reply, back, 7, True)
    own(WORK - LATE)
    for copy in copies:
        copy.wait()

    def settle(b):
        code = lists_ref[FINAL, b]
        here = state[jnp.minimum(code, 63)]
        there = back[jnp.clip(code - 64, 0, SLOTS - 1)]
        done = result[jnp.clip(code - 128, 0, WORK - 1)]
        out[b] = jnp.where(code < 64, here, jnp.where(code < 128, there, done))

    each(64, settle)


STATE = (64, ROWS, 128)
MOVE_SCRATCH = [
    pltpu.VMEM((10, 10, ROWS, 128), F32),
    pltpu.VMEM((ROWS, 128), F32),
    pltpu.VMEM((2, ROWS, 128), F32),
    pltpu.SemaphoreType.DMA((6,)),
    pltpu.SemaphoreType.DMA((6,)),
]
CHEM_SCRATCH = [pltpu.VMEM((SLOTS, ROWS, 128), F32)] * 4 + [
    pltpu.VMEM((WORK, ROWS, 128), F32),
    pltpu.SemaphoreType.DMA((14,)),
    pltpu.SemaphoreType.DMA((14,)),
]


COUNT_SCRATCH = [
    pltpu.VMEM((8, 8, 128), jnp.int32),
    pltpu.VMEM((4, 8, 128), jnp.int32),
    pltpu.VMEM((4, 4, 8, 128), jnp.int32),
    pltpu.SemaphoreType.DMA((13,)),
    pltpu.SemaphoreType.DMA((13,)),
    pltpu.VMEM((8, 128), jnp.int32),
    pltpu.SemaphoreType.DMA(()),
    pltpu.VMEM((2 * ROWS, 768), F32),
]


def others(axis):
    return [shifted(axis, step) for step in range(1, lax.axis_size(axis))]


def spread_counts(first, second, third, sems):
    stream, radial, azim = (lax.axis_index(axis) for axis in AXES)

    def stage(source, target, axis, start):
        copies = [remote(source, target, sems, start + k, p) for k, p in enumerate(others(axis))]
        for copy in copies:
            copy.start()

        def wait():
            for copy in copies:
                copy.wait()

        return wait

    def along_stream():
        return stage(first.at[stream], first.at[stream], "stream", 0)

    def along_radial():
        row = lax.broadcasted_iota(jnp.int32, (8, 128), 0)
        joined = first[0]
        for s in range(1, 8):
            joined = jnp.where(row == s, first[s], joined)
        second[radial] = joined
        return stage(second.at[radial], second.at[radial], "radial", 7)

    def along_azim():
        third[azim] = second[...]
        return stage(third.at[azim], third.at[azim], "azim", 10)

    def whole():
        row = lax.broadcasted_iota(jnp.int32, (8, 128), 0)
        lane = lax.broadcasted_iota(jnp.int32, (8, 128), 1)
        total = jnp.zeros((8, 128), jnp.int32)
        for a in range(4):
            for r in range(4):
                here = (lane & 15 == r * 4 + a) & (lane >> 4 == row)
                total = jnp.where(here, third[a, r], total)
        return jnp.broadcast_to(jnp.sum(total, 0, keepdims=True), (8, 128))

    return along_stream, along_radial, along_azim, whole


def communicating(kernel, name, out_shape, out_specs, specs, args, scratch):
    return pl.pallas_call(
        kernel,
        out_shape=out_shape,
        in_specs=specs,
        out_specs=out_specs,
        scratch_shapes=scratch,
        compiler_params=pltpu.CompilerParams(
            collective_id=name, has_side_effects=True, vmem_limit_bytes=LIMIT
        ),
    )(*args)


def first_step(blocks, tally, species, heat, courant, spread, settings):
    nrxn = settings[0].shape[1]
    padded = -(-nrxn // 16) * 16
    brought = (tally, species, heat, courant, spread, *settings)

    def kernel(blocks_ref, *refs):
        anywhere, refs = refs[: len(brought)], refs[len(brought) :]
        out, lists, rates, sums, spread_out = refs[:5]
        near, refs = refs[5 : 5 + len(brought)], refs[5 + len(brought) :]
        fetch_sem, refs = refs[0], refs[1:]
        tally_ref, species_ref, heat_ref, courant_ref, spread_ref, *settings_refs = near
        grid, edge, halo, *sems = refs[: len(MOVE_SCRATCH)]
        refs = refs[len(MOVE_SCRATCH) :]
        first, second, third, *count_sems = refs[:5]
        codes, code_sem, table = refs[5:8]
        moved, *chem = refs[8:]

        met = greet(others("stream") + others("radial") + others("azim"))
        rows = [pl.ds(8 * i, 8) for i in range(8)]
        pairs = list(zip(anywhere, near))
        pairs[1:2] = [(anywhere[1].at[:, row], species_ref.at[:, row]) for row in rows]
        waits = fetch(pairs, fetch_sem)
        stream, radial, azim = (lax.axis_index(axis) for axis in AXES)
        me = (stream * 4 + radial) * 4 + azim
        waits[0]()
        own = jnp.sum(tally_ref[...], 1, keepdims=True)
        first[stream] = jnp.broadcast_to(own, (8, 128))
        stages = spread_counts(first, second, third, count_sems)
        met()
        waiting = [stages[0]()]
        waits[9]()
        for i, row in enumerate(rows):
            waits[1 + i]()
            cells = [species_ref[:, row], heat_ref[row][None], jnp.zeros((2, 8, 128), F32)]
            grid[i + 1, pl.ds(1, 8)] = jnp.swapaxes(jnp.concatenate(cells, 0), 0, 1)
        found = []

        def at_once():
            for wait in waits[10:]:
                wait()
            table[pl.ds(0, 1), pl.ds(0, 128)] = jnp.zeros((1, 128), F32)
            table[pl.ds(0, 1), pl.ds(0, 54)] = spread_ref[...].reshape(1, 54)
            row = lax.broadcasted_iota(jnp.int32, (ROWS, 128), 0)
            lane = lax.broadcasted_iota(jnp.int32, (ROWS, 128), 1)
            diagonal = jnp.where(row == lane, table[pl.ds(0, 1), pl.ds(0, 128)], 0.0)
            column = jnp.sum(diagonal, 1, keepdims=True)
            spread_out[...] = jnp.broadcast_to(column, (ROWS, 128))
            found.append(positions(blocks_ref))
            waiting[0]()
            waiting.append(stages[1]())
            prepare(*settings_refs, rates, sums, table)
            waiting[1]()
            waiting.append(stages[2]())

        def after_inner():
            waiting[2]()
            plan(me, stages[3](), found[0], blocks_ref, codes, lists, code_sem)

        nothing = lambda: None
        hooks = (at_once, after_inner)
        transport(nothing, courant_ref, spread_out, moved, grid, edge, halo, sems, hooks)
        chemistry(lists, moved, rates, sums, out, *chem[:5], chem[5:], lambda: None)

    smem, vmem = pl.BlockSpec(memory_space=pltpu.SMEM), pl.BlockSpec(memory_space=pltpu.VMEM)
    return communicating(
        kernel,
        0,
        [
            jax.ShapeDtypeStruct(STATE, F32),
            jax.ShapeDtypeStruct((8, 128), jnp.int32),
            jax.ShapeDtypeStruct((2 * padded, 4 * ROWS), BF16),
            jax.ShapeDtypeStruct((4 * ROWS, 2 * padded), BF16),
            jax.ShapeDtypeStruct((ROWS, 128), F32),
        ],
        [vmem, smem, vmem, vmem, vmem],
        [smem] + [pl.BlockSpec(memory_space=pl.ANY)] * len(brought),
        (blocks, *brought),
        [pltpu.VMEM(x.shape, x.dtype) for x in brought]
        + [pltpu.SemaphoreType.DMA((7 + len(brought),))]
        + MOVE_SCRATCH
        + COUNT_SCRATCH
        + [pltpu.VMEM(STATE, F32)]
        + CHEM_SCRATCH,
    )


def second_step(lists, state, courant, spread, rates, sums):
    brought = (courant, spread, rates, sums)

    def kernel(lists_ref, state_any, *refs):
        anywhere, refs = refs[: len(brought)], refs[len(brought) :]
        out, near, refs = refs[0], refs[1 : 1 + len(brought)], refs[1 + len(brought) :]
        fetch_sem, refs = refs[0], refs[1:]
        courant_ref, spread_ref, rates_ref, sums_ref = near
        grid, edge, halo, *sems = refs[: len(MOVE_SCRATCH)]
        moved, *chem = refs[len(MOVE_SCRATCH) :]
        met = greet(faces() + [shifted("stream", 2), shifted("stream", -2)])
        pairs = [
            (state_any.at[pl.ds(8 * i, 8)], grid.at[i + 1, pl.ds(1, 8)]) for i in range(8)
        ]
        waits = fetch(pairs + list(zip(anywhere, near)), fetch_sem)
        for wait in waits:
            wait()
        nothing = lambda: None
        hooks = (nothing, nothing)
        transport(met, courant_ref, spread_ref, moved, grid, edge, halo, sems, hooks)
        chemistry(lists_ref, moved, rates_ref, sums_ref, out, *chem[:5], chem[5:], nothing)

    smem, vmem = pl.BlockSpec(memory_space=pltpu.SMEM), pl.BlockSpec(memory_space=pltpu.VMEM)
    return communicating(
        kernel,
        1,
        jax.ShapeDtypeStruct(STATE, F32),
        vmem,
        [smem] + [pl.BlockSpec(memory_space=pl.ANY)] * 5,
        (lists, state, *brought),
        [pltpu.VMEM(x.shape, x.dtype) for x in brought]
        + [pltpu.SemaphoreType.DMA((8 + len(brought),))]
        + MOVE_SCRATCH
        + [pltpu.VMEM(STATE, F32)]
        + CHEM_SCRATCH,
    )


def shards(
    component_fractions,
    kilokelvin_field,
    axial_courant_number,
    spreading_number,
    arrhenius_multiplier_exponent,
    thermal_exponents,
    arrhenius_barrier,
    balance_constant_exponents,
    enthalpy_formation,
    consumed_stoich_matrix,
    yield_stoich_matrix,
    processor_tiles_burning,
    tile_transfer_tally,
):
    shape = component_fractions.shape
    settings = (
        consumed_stoich_matrix,
        yield_stoich_matrix,
        arrhenius_multiplier_exponent,
        thermal_exponents,
        arrhenius_barrier,
        balance_constant_exponents,
        enthalpy_formation,
    )
    species = component_fractions.reshape(53, 64, 128)
    heat = kilokelvin_field.reshape(64, 128)
    courant = axial_courant_number.reshape(64, 128)
    blocks, tally = processor_tiles_burning, tile_transfer_tally
    state, lists, rates, sums, spread = first_step(
        blocks, tally, species, heat, courant, spreading_number, settings
    )
    state = react_rest(lists, blocks, state, rates, sums)
    state = second_step(lists, state, courant, spread, rates, sums)
    species, heat = finish(lists, blocks, state, rates, sums)
    return species.reshape(shape), heat.reshape(shape[1:])


def solution(mesh):
    in_specs = (
        P(None, "stream", "radial", "azim"),
        P("stream", "radial", "azim"),
        P("stream", "radial", "azim"),
        P(),
        P(),
        P(),
        P(),
        P(),
        P(),
        P(),
        P(),
        P(AXES, None),
        P(AXES, None),
    )
    out_specs = (P(None, "stream", "radial", "azim"), P("stream", "radial", "azim"))
    return jax.shard_map(shards, mesh=mesh, in_specs=in_specs, out_specs=out_specs, check_vma=False)
```

```python
import functools

import jax
import jax.numpy as jnp
from jax import lax
from jax.experimental import pallas as pl
from jax.experimental.pallas import tpu as pltpu
from jax.sharding import PartitionSpec as P

NCYC = 4
ROWS = 56
GROUP = 8
chem_step = 0.02
mass_offset = 0.05
LOG2E = 1.4426950408889634
F32 = jnp.float32
BF16 = jnp.bfloat16
MESH = pl.DeviceIdType.MESH
AXES = ("stream", "radial", "azim")
LIMIT = 63 * 2**20
WORK = 32
EARLY = 8
LATE = 8
SPAN = WORK - EARLY - LATE
FLOOR = 24
SWEEPS = 3
PAIR = 10
SIDE = 5
SIZES = (PAIR,) + (SIDE,) * 6
BASES = tuple(sum(SIZES[:k]) for k in range(7))
SLOTS = sum(SIZES)
OPPOSITE = (0, 2, 1, 4, 3, 6, 5)
SEND, WORK_ROW, REPLY, FINAL, REST = range(5)


def prepare(consumed, made, exponent, thermal, barrier, balance, enthalpy, rates, sums, table):
    half = rates.shape[0] // 2
    exponent, thermal, barrier, balance, enthalpy = (
        vector[...].reshape(1, -1) for vector in (exponent, thermal, barrier, balance, enthalpy)
    )

    def put(side, row, value):
        rows, lanes = value.shape
        table[pl.ds(row, rows), pl.ds(side * half, lanes)] = value

    def halves(value):
        high = value.astype(BF16).astype(F32)
        return high, value - high

    table[...] = jnp.zeros_like(table)
    for side, change in enumerate((0.0, balance)):
        put(side, 0, (consumed, made)[side][...])
        put(side, 53, thermal)
        put(side, 54, -LOG2E * barrier)
        put(side, 55, LOG2E * (exponent - change))
    high, low = halves(table[:ROWS])
    stacked = jnp.concatenate([high, high, low, high], 0).T
    rates[...] = stacked[: 2 * half].astype(BF16)
    heat = LOG2E * lax.dot_general(
        enthalpy,
        made[...] - consumed[...],
        (((1,), (0,)), ((), ())),
        preferred_element_type=F32,
        precision=lax.Precision.HIGHEST,
    )
    table[...] = jnp.zeros_like(table)
    for side, (gain, loss, warm) in enumerate(((made, consumed, heat), (consumed, made, -heat))):
        put(side, 0, gain[...])
        put(side, 53, warm)
        put(side, ROWS, loss[...])
    high, low = halves(chem_step * table[...])
    sums[...] = jnp.concatenate([high, low], 0)[:, : 2 * half].astype(BF16)


def parted(value):
    high = value.astype(BF16)
    return high, value - high.astype(F32)


def product(a, b):
    return lax.dot_general(a, b, (((1,), (0,)), ((), ())), preferred_element_type=F32)


def cycle(state, rates, sums):
    row = lax.broadcasted_iota(jnp.int32, state.shape, 0)
    moved = state + jnp.where(row < 53, mass_offset, jnp.where(row == 53, 0.0, 1.0))
    heat = state[53:54]
    logs = jnp.log2(moved)
    logs = jnp.where(row == 54, 1.0 / heat, jnp.where(row == 55, 1.0, logs))
    first, rest = parted(logs)
    second, third = parted(rest)
    first, second = first.astype(F32), second.astype(F32)
    stacked = jnp.concatenate([first, second, first, third], 0).astype(BF16)
    flux = jnp.exp2(product(rates, stacked))
    high, low = parted(flux)
    half = sums.shape[0] // 2
    both = product(sums, high)
    total = both[:half] + both[half:] + product(sums[:half], low.astype(BF16))
    gain, loss = total[:ROWS], total[ROWS:]
    species = (state + gain) * moved / (moved + loss)
    return jnp.where(row == 53, heat * jnp.exp2(gain[53:54]), species)


def toward(value, k):
    lane = lax.broadcasted_iota(jnp.int32, value.shape, 1)
    azim, radial, core = lane & 3, (lane >> 2) & 3, (lane >> 4) & 1

    def ahead(step):
        return pltpu.roll(value, (128 - step) % 128, 1)

    return (
        lambda: jnp.where(core == 0, ahead(16), ahead(-16)),
        lambda: ahead(32),
        lambda: ahead(-32),
        lambda: jnp.where(radial < 3, ahead(4), ahead(-12)),
        lambda: jnp.where(radial > 0, ahead(-4), ahead(12)),
        lambda: jnp.where(azim < 3, ahead(1), ahead(-3)),
        lambda: jnp.where(azim > 0, ahead(-1), ahead(3)),
    )[k]()


def flows(counts):
    least = EARLY + LATE
    load, own = jnp.maximum(counts, least), counts
    given = [jnp.zeros_like(counts) for _ in SIZES]
    taken = [jnp.zeros_like(counts) for _ in SIZES]
    for sweep in range(SWEEPS):
        for axis in ((0,), (1, 2), (3, 4), (5, 6)):
            spare = jnp.minimum(jnp.maximum(own - least, 0), jnp.maximum(load - FLOOR, 0))
            gives = []
            for k in axis:
                other = toward(load, k)
                gap = load - other + (1 if sweep == SWEEPS - 1 else 0)
                room = jnp.maximum(WORK - other, 0)
                if len(axis) == 2:
                    room = (room + (1 if k == axis[0] else 0)) >> 1
                give = jnp.minimum(SIZES[k] - given[k], jnp.maximum(gap, 0) >> 1)
                give = jnp.minimum(jnp.minimum(give, room), spare)
                spare = spare - give
                gives.append(give)
            takes = [toward(give, OPPOSITE[k]) for k, give in zip(axis, gives)]
            for k, give, take in zip(axis, gives, takes):
                given[k], taken[k] = given[k] + give, taken[k] + take
            own = own - sum(gives)
            load = load - sum(gives) + sum(takes)
    return own, given, taken


def positions(blocks_ref):
    lane = lax.broadcasted_iota(jnp.int32, (8, 128), 1)
    found = jnp.zeros((8, 128), jnp.int32)
    for n in range(64):
        found = jnp.where(lane == blocks_ref[0, n], n, found)
    return found


def plan(me, counts, position, blocks_ref, codes, lists, sem):
    own, given, taken = flows(counts)
    row = lax.broadcasted_iota(jnp.int32, (8, 128), 0)
    lane = lax.broadcasted_iota(jnp.int32, (8, 128), 1)

    def mine(value):
        return jnp.sum(jnp.where(lane == me, value, 0), 1, keepdims=True)

    own, total = mine(own), mine(counts)
    given, taken = [mine(v) for v in given], [mine(v) for v in taken]
    received = sum(taken)
    kept = jnp.minimum(own, WORK - received)
    sent_before, taken_before = [kept], [jnp.zeros_like(kept)]
    for p in range(len(SIZES)):
        sent_before.append(sent_before[p] + given[p])
        taken_before.append(taken_before[p] + taken[p])

    late = WORK - LATE - EARLY + position
    middle = received + position - LATE
    slot = jnp.where(position < EARLY, position, jnp.where(position < EARLY + LATE, late, middle))
    final = jnp.where(position < kept, 128 + slot, lane)
    send, reply = jnp.zeros((8, 128), jnp.int32), jnp.zeros((8, 128), jnp.int32)
    step = lane - EARLY
    arrived = jnp.zeros((8, 128), jnp.int32)
    for p, (base, size) in enumerate(zip(BASES, SIZES)):
        inside = (position >= sent_before[p]) & (position < sent_before[p + 1])
        final = jnp.where(inside, 64 + base + position - sent_before[p], final)
        here = (lane >= base) & (lane < base + size)
        send = jnp.where(here, sent_before[p] + lane - base, send)
        reply = jnp.where(here, EARLY + taken_before[p] + lane - base, reply)
        inside = (step >= taken_before[p]) & (step < taken_before[p + 1])
        arrived = jnp.where(inside, 64 + base + step - taken_before[p], arrived)
    place = jnp.where(lane < EARLY, lane, EARLY + LATE + step - received)
    place = jnp.where(lane >= WORK - LATE, lane - (WORK - LATE - EARLY), place)
    wanted = jnp.clip(jnp.where(row == SEND, send, place), 0, 63)
    value = jnp.zeros((8, 128), jnp.int32)
    for n in range(64):
        value = jnp.where(wanted == n, blocks_ref[0, n], value)
    value = jnp.where((row == WORK_ROW) & (arrived > 0), arrived, value)
    value = jnp.where(row == REPLY, jnp.clip(reply, 0, WORK - 1), value)
    value = jnp.where(row == FINAL, final, value)
    value = jnp.where(row == REST, jnp.where(lane == 0, sent_before[-1], total), value)
    codes[...] = value
    copy = pltpu.make_async_copy(codes, lists, sem)
    copy.start()
    copy.wait()


def fetch(pairs, sem):
    copies = [pltpu.make_async_copy(*pair, sem.at[k]) for k, pair in enumerate(pairs)]
    for copy in copies:
        copy.start()
    return [copy.wait for copy in copies]


def subcycles(state, rates_ref, sums_ref):
    return lax.fori_loop(0, NCYC, lambda c, s: cycle(s, rates_ref[...], sums_ref[...]), state)


def rest_kernel(lists_ref, blocks_ref, state_ref, rates_any, sums_any, out_ref, rates, sums, held, sem):
    start, count = lists_ref[REST, 0], lists_ref[REST, 1]

    def bring(source, target):
        copy = pltpu.make_async_copy(source, target, sem)
        copy.start()
        copy.wait()

    @pl.when(start < count)
    def _():
        bring(rates_any, rates)
        bring(sums_any, sums)

        def group(g, carry):
            first = start + g * GROUP
            for k in range(GROUP):
                bring(out_ref.at[blocks_ref[0, jnp.minimum(first + k, 63)]], held.at[k])
            state = jnp.concatenate([held[k] for k in range(GROUP)], 1)
            state = subcycles(state, rates, sums)
            for k in range(GROUP):
                held[k] = state[:, k * 128 : (k + 1) * 128]

                @pl.when(first + k < count)
                def _():
                    bring(held.at[k], out_ref.at[blocks_ref[0, jnp.minimum(first + k, 63)]])

            return carry

        lax.fori_loop(0, (count - start + GROUP - 1) // GROUP, group, 0)


def react_rest(lists, blocks, state, rates, sums):
    smem, anywhere = pl.BlockSpec(memory_space=pltpu.SMEM), pl.BlockSpec(memory_space=pl.ANY)
    return pl.pallas_call(
        rest_kernel,
        out_shape=jax.ShapeDtypeStruct(state.shape, F32),
        in_specs=[smem, smem] + [anywhere] * 3,
        out_specs=anywhere,
        scratch_shapes=[
            pltpu.VMEM(rates.shape, BF16),
            pltpu.VMEM(sums.shape, BF16),
            pltpu.VMEM((GROUP, ROWS, 128), F32),
            pltpu.SemaphoreType.DMA(()),
        ],
        input_output_aliases={2: 0},
        compiler_params=pltpu.CompilerParams(vmem_limit_bytes=LIMIT),
    )(lists, blocks, state, rates, sums)


def last_kernel(
    lists_ref, blocks_ref, state_any, rates_any, sums_any, species_any, heat_any, *scratch
):
    state, species, heat, rates, sums, in_sem, out_sem, sem = scratch
    start, count = lists_ref[REST, 0], lists_ref[REST, 1]
    rows = [pl.ds(8 * i, 8) for i in range(8)]
    waits = fetch([(state_any.at[row], state.at[row]) for row in rows], in_sem)
    copies = []
    for i, row in enumerate(rows):
        waits[i]()
        turned = jnp.swapaxes(state[row], 0, 1)
        species[:, row] = turned[:53]
        heat[row] = turned[53]
        copies.append(
            pltpu.make_async_copy(species.at[:, row], species_any.at[:, row], out_sem.at[i])
        )
        copies[-1].start()
    copies.append(pltpu.make_async_copy(heat, heat_any, out_sem.at[8]))
    copies[-1].start()
    for copy in copies:
        copy.wait()

    def bring(source, target):
        copy = pltpu.make_async_copy(source, target, sem)
        copy.start()
        copy.wait()

    @pl.when(start < count)
    def _():
        bring(rates_any, rates)
        bring(sums_any, sums)

        def group(g, carry):
            first = start + g * GROUP
            at = [blocks_ref[0, jnp.minimum(first + k, 63)] for k in range(GROUP)]
            value = jnp.concatenate([state[at[k]] for k in range(GROUP)], 1)
            value = subcycles(value, rates, sums)
            for k in range(GROUP):

                @pl.when(first + k < count)
                def _():
                    state[at[k]] = value[:, k * 128 : (k + 1) * 128]

            return carry

        lax.fori_loop(0, (count - start + GROUP - 1) // GROUP, group, 0)
        for row in rows:
            turned = jnp.swapaxes(state[row], 0, 1)
            species[:, row] = turned[:53]
            heat[row] = turned[53]
        bring(species, species_any)
        bring(heat, heat_any)


def finish(lists, blocks, state, rates, sums):
    smem, anywhere = pl.BlockSpec(memory_space=pltpu.SMEM), pl.BlockSpec(memory_space=pl.ANY)
    return pl.pallas_call(
        last_kernel,
        out_shape=[jax.ShapeDtypeStruct((53, 64, 128), F32), jax.ShapeDtypeStruct((64, 128), F32)],
        in_specs=[smem, smem] + [anywhere] * 3,
        out_specs=[anywhere] * 2,
        scratch_shapes=[
            pltpu.VMEM(state.shape, F32),
            pltpu.VMEM((53, 64, 128), F32),
            pltpu.VMEM((64, 128), F32),
            pltpu.VMEM(rates.shape, BF16),
            pltpu.VMEM(sums.shape, BF16),
            pltpu.SemaphoreType.DMA((8,)),
            pltpu.SemaphoreType.DMA((9,)),
            pltpu.SemaphoreType.DMA(()),
        ],
        compiler_params=pltpu.CompilerParams(vmem_limit_bytes=LIMIT),
    )(lists, blocks, state, rates, sums)


def shifted(axis, step):
    n, me = lax.axis_size(axis), lax.axis_index(axis)
    return {axis: lax.rem(me + (n + step), n)}


def faces():
    return [shifted(axis, step) for axis in AXES for step in (-1, 1)]


def partners():
    me = lax.axis_index("stream")
    sides = [("stream", 2), ("stream", -2), ("radial", 1), ("radial", -1), ("azim", 1), ("azim", -1)]
    return [{"stream": me + 1 - 2 * lax.rem(me, 2)}] + [shifted(*side) for side in sides]


def greet(peers):
    barrier = pltpu.get_barrier_semaphore()
    for peer in peers:
        pl.semaphore_signal(barrier, inc=1, device_id=peer, device_id_type=MESH)
    return lambda: pl.semaphore_wait(barrier, len(peers))


def remote(source, target, sems, k, peer):
    return pltpu.make_async_remote_copy(
        src_ref=source,
        dst_ref=target,
        send_sem=sems[0].at[k],
        recv_sem=sems[1].at[k],
        device_id=peer,
        device_id_type=MESH,
    )


def transport(met, courant_ref, spread_ref, out, grid, edge, halo, sems, hooks):
    lane = lax.broadcasted_iota(jnp.int32, (ROWS, 128), 1)
    peers = faces()
    inner = pl.ds(1, 8)
    plans = [
        (grid.at[1, inner], grid.at[9, inner]),
        (grid.at[8, inner], grid.at[0, inner]),
        (grid.at[inner, 1], grid.at[inner, 9]),
        (grid.at[inner, 8], grid.at[inner, 0]),
        (edge, halo.at[1]),
        (edge, halo.at[0]),
    ]
    copies = [remote(*plans[k], sems, k, peers[k]) for k in range(6)]
    met()
    for k in (2, 3, 0, 1):
        copies[k].start()

    def ends(i, packed):
        for j in range(8):
            b = i * 8 + j
            turned = pltpu.roll(grid[i + 1, j + 1], 2 * b + 1, 1)
            packed = jnp.where((lane >> 1) == b, turned, packed)
        return packed

    edge[...] = lax.fori_loop(0, 8, ends, jnp.zeros((ROWS, 128), F32))
    copies[4].start()
    copies[5].start()
    hooks[0]()
    copies[4].wait()
    copies[5].wait()
    edge[...] = jnp.where((lane & 1) == 0, halo[0], halo[1])
    rate = spread_ref[...]
    keep = 1.0 - 6.0 * rate

    def cells(i, columns):
        for j in columns:
            b = i * 8 + j
            here = grid[i + 1, j + 1]
            behind = grid[i, j + 1]
            ends = pltpu.roll(edge[...], 127 - 2 * b, 1)
            left = pltpu.roll(jnp.where(lane == 127, ends, here), 1, 1)
            right = pltpu.roll(jnp.where(lane == 0, ends, here), 127, 1)
            around = (behind + grid[i + 2, j + 1]) + (grid[i + 1, j] + grid[i + 1, j + 2])
            around = around + (left + right)
            speed = courant_ref[pl.ds(b, 1), :]
            out[b] = (keep - speed) * here + rate * around + speed * behind

    def middle(i, carry):
        cells(i, range(1, 7))
        return carry

    lax.fori_loop(1, 7, middle, 0)
    hooks[1]()
    for k in range(4):
        copies[k].wait()
    blank = jnp.zeros((8, ROWS, 128), F32)
    stream, radial = lax.axis_index("stream"), lax.axis_index("radial")

    @pl.when(stream == 0)
    def _():
        grid[0, inner] = blank

    @pl.when(stream == lax.axis_size("stream") - 1)
    def _():
        grid[9, inner] = blank

    @pl.when(radial == 0)
    def _():
        grid[inner, 0] = blank

    @pl.when(radial == lax.axis_size("radial") - 1)
    def _():
        grid[inner, 9] = blank

    def sides(i, carry):
        cells(i, (0, 7))
        return carry

    def first_last(i, carry):
        cells(i * 7, range(1, 7))
        return carry

    lax.fori_loop(0, 8, sides, 0)
    lax.fori_loop(0, 2, first_last, 0)
    hooks[2]()


def chemistry(lists_ref, state, rates_ref, sums_ref, out, send, recv, reply, back, result, sems, met):
    def each(count, body):
        def four(g, carry):
            for k in range(4):
                body(4 * g + k)
            return carry

        lax.fori_loop(0, count // 4, four, 0)
        for k in range(count // 4 * 4, count):
            body(k)

    def pack(s):
        send[s] = state[lists_ref[SEND, s]]

    each(SLOTS, pack)
    met()
    peers = partners()

    def exchange(source, target, first, turned):
        found = []
        for k, (base, size) in enumerate(zip(BASES, SIZES)):
            area = pl.ds(base, size)
            peer = peers[OPPOSITE[k] if turned else k]
            found.append(remote(source.at[area], target.at[area], sems, first + k, peer))
            found[-1].start()
        return found

    def run(first, items):
        whole = subcycles(jnp.concatenate(items, 1), rates_ref, sums_ref)
        for k in range(len(items)):
            result[first + k] = whole[:, k * 128 : (k + 1) * 128]

    def own(first):
        run(first, [state[lists_ref[WORK_ROW, first + k]] for k in range(GROUP)])

    def any_item(slot):
        code = lists_ref[WORK_ROW, slot]
        there = recv[jnp.maximum(code - 64, 0)]
        return jnp.where(code < 64, state[jnp.minimum(code, 63)], there)

    def middle(g, carry):
        first = EARLY + g * GROUP
        run(first, [any_item(first + k) for k in range(GROUP)])
        return carry

    copies = exchange(send, recv, 0, False)
    own(0)
    for copy in copies:
        copy.wait()
    lax.fori_loop(0, SPAN // GROUP, middle, 0)

    def answer(s):
        reply[s] = result[lists_ref[REPLY, s]]

    each(SLOTS, answer)
    copies = exchange(reply, back, 7, True)
    own(WORK - LATE)
    for copy in copies:
        copy.wait()

    def settle(b):
        code = lists_ref[FINAL, b]
        here = state[jnp.minimum(code, 63)]
        there = back[jnp.clip(code - 64, 0, SLOTS - 1)]
        done = result[jnp.clip(code - 128, 0, WORK - 1)]
        out[b] = jnp.where(code < 64, here, jnp.where(code < 128, there, done))

    each(64, settle)


STATE = (64, ROWS, 128)
MOVE_SCRATCH = [
    pltpu.VMEM((10, 10, ROWS, 128), F32),
    pltpu.VMEM((ROWS, 128), F32),
    pltpu.VMEM((2, ROWS, 128), F32),
    pltpu.SemaphoreType.DMA((6,)),
    pltpu.SemaphoreType.DMA((6,)),
]
CHEM_SCRATCH = [pltpu.VMEM((SLOTS, ROWS, 128), F32)] * 4 + [
    pltpu.VMEM((WORK, ROWS, 128), F32),
    pltpu.SemaphoreType.DMA((14,)),
    pltpu.SemaphoreType.DMA((14,)),
]


COUNT_SCRATCH = [
    pltpu.VMEM((8, 8, 128), jnp.int32),
    pltpu.VMEM((4, 8, 128), jnp.int32),
    pltpu.VMEM((4, 4, 8, 128), jnp.int32),
    pltpu.SemaphoreType.DMA((13,)),
    pltpu.SemaphoreType.DMA((13,)),
    pltpu.VMEM((8, 128), jnp.int32),
    pltpu.SemaphoreType.DMA(()),
    pltpu.VMEM((2 * ROWS, 768), F32),
]


def others(axis):
    return [shifted(axis, step) for step in range(1, lax.axis_size(axis))]


def spread_counts(first, second, third, sems):
    stream, radial, azim = (lax.axis_index(axis) for axis in AXES)

    def stage(source, target, axis, start):
        copies = [remote(source, target, sems, start + k, p) for k, p in enumerate(others(axis))]
        for copy in copies:
            copy.start()

        def wait():
            for copy in copies:
                copy.wait()

        return wait

    def along_stream():
        return stage(first.at[stream], first.at[stream], "stream", 0)

    def along_radial():
        row = lax.broadcasted_iota(jnp.int32, (8, 128), 0)
        joined = first[0]
        for s in range(1, 8):
            joined = jnp.where(row == s, first[s], joined)
        second[radial] = joined
        return stage(second.at[radial], second.at[radial], "radial", 7)

    def along_azim():
        third[azim] = second[...]
        return stage(third.at[azim], third.at[azim], "azim", 10)

    def whole():
        row = lax.broadcasted_iota(jnp.int32, (8, 128), 0)
        lane = lax.broadcasted_iota(jnp.int32, (8, 128), 1)
        total = jnp.zeros((8, 128), jnp.int32)
        for a in range(4):
            for r in range(4):
                here = (lane & 15 == r * 4 + a) & (lane >> 4 == row)
                total = jnp.where(here, third[a, r], total)
        return jnp.broadcast_to(jnp.sum(total, 0, keepdims=True), (8, 128))

    return along_stream, along_radial, along_azim, whole


def communicating(kernel, name, out_shape, out_specs, specs, args, scratch):
    return pl.pallas_call(
        kernel,
        out_shape=out_shape,
        in_specs=specs,
        out_specs=out_specs,
        scratch_shapes=scratch,
        compiler_params=pltpu.CompilerParams(
            collective_id=name, has_side_effects=True, vmem_limit_bytes=LIMIT
        ),
    )(*args)


def first_step(blocks, tally, species, heat, courant, spread, settings):
    nrxn = settings[0].shape[1]
    padded = -(-nrxn // 16) * 16
    brought = (tally, species, heat, courant, spread, *settings)

    def kernel(blocks_ref, *refs):
        anywhere, refs = refs[: len(brought)], refs[len(brought) :]
        out, lists, rates, sums, spread_out = refs[:5]
        near, refs = refs[5 : 5 + len(brought)], refs[5 + len(brought) :]
        fetch_sem, refs = refs[0], refs[1:]
        tally_ref, species_ref, heat_ref, courant_ref, spread_ref, *settings_refs = near
        grid, edge, halo, *sems = refs[: len(MOVE_SCRATCH)]
        refs = refs[len(MOVE_SCRATCH) :]
        first, second, third, *count_sems = refs[:5]
        codes, code_sem, table = refs[5:8]
        moved, *chem = refs[8:]

        met = greet(others("stream") + others("radial") + others("azim"))
        rows = [pl.ds(8 * i, 8) for i in range(8)]
        pairs = list(zip(anywhere, near))
        pairs[1:2] = [(anywhere[1].at[:, row], species_ref.at[:, row]) for row in rows]
        waits = fetch(pairs, fetch_sem)
        stream, radial, azim = (lax.axis_index(axis) for axis in AXES)
        me = (stream * 4 + radial) * 4 + azim
        waits[0]()
        own = jnp.sum(tally_ref[...], 1, keepdims=True)
        first[stream] = jnp.broadcast_to(own, (8, 128))
        stages = spread_counts(first, second, third, count_sems)
        waits[9]()
        waiting = []
        for i, row in enumerate(rows):
            waits[1 + i]()
            cells = [species_ref[:, row], heat_ref[row][None], jnp.zeros((2, 8, 128), F32)]
            grid[i + 1, pl.ds(1, 8)] = jnp.swapaxes(jnp.concatenate(cells, 0), 0, 1)
            if i == 3:
                met()
                waiting.append(stages[0]())
        found = []

        def at_once():
            for wait in waits[10:]:
                wait()
            table[pl.ds(0, 1), pl.ds(0, 128)] = jnp.zeros((1, 128), F32)
            table[pl.ds(0, 1), pl.ds(0, 54)] = spread_ref[...].reshape(1, 54)
            row = lax.broadcasted_iota(jnp.int32, (ROWS, 128), 0)
            lane = lax.broadcasted_iota(jnp.int32, (ROWS, 128), 1)
            diagonal = jnp.where(row == lane, table[pl.ds(0, 1), pl.ds(0, 128)], 0.0)
            column = jnp.sum(diagonal, 1, keepdims=True)
            spread_out[...] = jnp.broadcast_to(column, (ROWS, 128))
            found.append(positions(blocks_ref))
            waiting[0]()
            waiting.append(stages[1]())
            prepare(*settings_refs, rates, sums, table)
            waiting[1]()
            waiting.append(stages[2]())

        def at_end():
            waiting[2]()
            plan(me, stages[3](), found[0], blocks_ref, codes, lists, code_sem)

        nothing = lambda: None
        hooks = (at_once, nothing, at_end)
        transport(nothing, courant_ref, spread_out, moved, grid, edge, halo, sems, hooks)
        chemistry(lists, moved, rates, sums, out, *chem[:5], chem[5:], lambda: None)

    smem, vmem = pl.BlockSpec(memory_space=pltpu.SMEM), pl.BlockSpec(memory_space=pltpu.VMEM)
    return communicating(
        kernel,
        0,
        [
            jax.ShapeDtypeStruct(STATE, F32),
            jax.ShapeDtypeStruct((8, 128), jnp.int32),
            jax.ShapeDtypeStruct((2 * padded, 4 * ROWS), BF16),
            jax.ShapeDtypeStruct((4 * ROWS, 2 * padded), BF16),
            jax.ShapeDtypeStruct((ROWS, 128), F32),
        ],
        [vmem, smem, vmem, vmem, vmem],
        [smem] + [pl.BlockSpec(memory_space=pl.ANY)] * len(brought),
        (blocks, *brought),
        [pltpu.VMEM(x.shape, x.dtype) for x in brought]
        + [pltpu.SemaphoreType.DMA((7 + len(brought),))]
        + MOVE_SCRATCH
        + COUNT_SCRATCH
        + [pltpu.VMEM(STATE, F32)]
        + CHEM_SCRATCH,
    )


def second_step(lists, state, courant, spread, rates, sums):
    brought = (courant, spread, rates, sums)

    def kernel(lists_ref, state_any, *refs):
        anywhere, refs = refs[: len(brought)], refs[len(brought) :]
        out, near, refs = refs[0], refs[1 : 1 + len(brought)], refs[1 + len(brought) :]
        fetch_sem, refs = refs[0], refs[1:]
        courant_ref, spread_ref, rates_ref, sums_ref = near
        grid, edge, halo, *sems = refs[: len(MOVE_SCRATCH)]
        moved, *chem = refs[len(MOVE_SCRATCH) :]
        met = greet(faces() + [shifted("stream", 2), shifted("stream", -2)])
        pairs = [
            (state_any.at[pl.ds(8 * i, 8)], grid.at[i + 1, pl.ds(1, 8)]) for i in range(8)
        ]
        waits = fetch(pairs + list(zip(anywhere, near)), fetch_sem)
        for wait in waits:
            wait()
        nothing = lambda: None
        hooks = (nothing, nothing, nothing)
        transport(met, courant_ref, spread_ref, moved, grid, edge, halo, sems, hooks)
        chemistry(lists_ref, moved, rates_ref, sums_ref, out, *chem[:5], chem[5:], nothing)

    smem, vmem = pl.BlockSpec(memory_space=pltpu.SMEM), pl.BlockSpec(memory_space=pltpu.VMEM)
    return communicating(
        kernel,
        1,
        jax.ShapeDtypeStruct(STATE, F32),
        vmem,
        [smem] + [pl.BlockSpec(memory_space=pl.ANY)] * 5,
        (lists, state, *brought),
        [pltpu.VMEM(x.shape, x.dtype) for x in brought]
        + [pltpu.SemaphoreType.DMA((8 + len(brought),))]
        + MOVE_SCRATCH
        + [pltpu.VMEM(STATE, F32)]
        + CHEM_SCRATCH,
    )


def shards(
    component_fractions,
    kilokelvin_field,
    axial_courant_number,
    spreading_number,
    arrhenius_multiplier_exponent,
    thermal_exponents,
    arrhenius_barrier,
    balance_constant_exponents,
    enthalpy_formation,
    consumed_stoich_matrix,
    yield_stoich_matrix,
    processor_tiles_burning,
    tile_transfer_tally,
):
    shape = component_fractions.shape
    settings = (
        consumed_stoich_matrix,
        yield_stoich_matrix,
        arrhenius_multiplier_exponent,
        thermal_exponents,
        arrhenius_barrier,
        balance_constant_exponents,
        enthalpy_formation,
    )
    species = component_fractions.reshape(53, 64, 128)
    heat = kilokelvin_field.reshape(64, 128)
    courant = axial_courant_number.reshape(64, 128)
    blocks, tally = processor_tiles_burning, tile_transfer_tally
    state, lists, rates, sums, spread = first_step(
        blocks, tally, species, heat, courant, spreading_number, settings
    )
    state = react_rest(lists, blocks, state, rates, sums)
    state = second_step(lists, state, courant, spread, rates, sums)
    species, heat = finish(lists, blocks, state, rates, sums)
    return species.reshape(shape), heat.reshape(shape[1:])


def solution(mesh):
    in_specs = (
        P(None, "stream", "radial", "azim"),
        P("stream", "radial", "azim"),
        P("stream", "radial", "azim"),
        P(),
        P(),
        P(),
        P(),
        P(),
        P(),
        P(),
        P(),
        P(AXES, None),
        P(AXES, None),
    )
    out_specs = (P(None, "stream", "radial", "azim"), P("stream", "radial", "azim"))
    return jax.shard_map(shards, mesh=mesh, in_specs=in_specs, out_specs=out_specs, check_vma=False)
```

```python
import functools

import jax
import jax.numpy as jnp
from jax import lax
from jax.experimental import pallas as pl
from jax.experimental.pallas import tpu as pltpu
from jax.sharding import PartitionSpec as P

NCYC = 4
ROWS = 56
GROUP = 8
chem_step = 0.02
mass_offset = 0.05
LOG2E = 1.4426950408889634
F32 = jnp.float32
BF16 = jnp.bfloat16
MESH = pl.DeviceIdType.MESH
AXES = ("stream", "radial", "azim")
LIMIT = 63 * 2**20
WORK = 32
EARLY = 8
LATE = 8
SPAN = WORK - EARLY - LATE
FLOOR = 24
SWEEPS = 3
PAIR = 10
SIDE = 5
SIZES = (PAIR,) + (SIDE,) * 6
BASES = tuple(sum(SIZES[:k]) for k in range(7))
SLOTS = sum(SIZES)
OPPOSITE = (0, 2, 1, 4, 3, 6, 5)
SEND, WORK_ROW, REPLY, FINAL, REST = range(5)


def prepare(consumed, made, exponent, thermal, barrier, balance, enthalpy, rates, sums, table):
    half = rates.shape[0] // 2
    exponent, thermal, barrier, balance, enthalpy = (
        vector[...].reshape(1, -1) for vector in (exponent, thermal, barrier, balance, enthalpy)
    )

    def put(side, row, value):
        rows, lanes = value.shape
        table[pl.ds(row, rows), pl.ds(side * half, lanes)] = value

    def halves(value):
        high = value.astype(BF16).astype(F32)
        return high, value - high

    table[...] = jnp.zeros_like(table)
    for side, change in enumerate((0.0, balance)):
        put(side, 0, (consumed, made)[side][...])
        put(side, 53, thermal)
        put(side, 54, -LOG2E * barrier)
        put(side, 55, LOG2E * (exponent - change))
    high, low = halves(table[:ROWS])
    stacked = jnp.concatenate([high, high, low, high], 0).T
    rates[...] = stacked[: 2 * half].astype(BF16)
    heat = LOG2E * lax.dot_general(
        enthalpy,
        made[...] - consumed[...],
        (((1,), (0,)), ((), ())),
        preferred_element_type=F32,
        precision=lax.Precision.HIGHEST,
    )
    table[...] = jnp.zeros_like(table)
    for side, (gain, loss, warm) in enumerate(((made, consumed, heat), (consumed, made, -heat))):
        put(side, 0, gain[...])
        put(side, 53, warm)
        put(side, ROWS, loss[...])
    high, low = halves(chem_step * table[...])
    sums[...] = jnp.concatenate([high, low], 0)[:, : 2 * half].astype(BF16)


def parted(value):
    high = value.astype(BF16)
    return high, value - high.astype(F32)


def product(a, b):
    return lax.dot_general(a, b, (((1,), (0,)), ((), ())), preferred_element_type=F32)


def cycle(state, rates, sums):
    row = lax.broadcasted_iota(jnp.int32, state.shape, 0)
    moved = state + jnp.where(row < 53, mass_offset, jnp.where(row == 53, 0.0, 1.0))
    heat = state[53:54]
    logs = jnp.log2(moved)
    logs = jnp.where(row == 54, 1.0 / heat, jnp.where(row == 55, 1.0, logs))
    first, rest = parted(logs)
    second, third = parted(rest)
    first, second = first.astype(F32), second.astype(F32)
    stacked = jnp.concatenate([first, second, first, third], 0).astype(BF16)
    flux = jnp.exp2(product(rates, stacked))
    high, low = parted(flux)
    half = sums.shape[0] // 2
    both = product(sums, high)
    total = both[:half] + both[half:] + product(sums[:half], low.astype(BF16))
    gain, loss = total[:ROWS], total[ROWS:]
    species = (state + gain) * moved / (moved + loss)
    return jnp.where(row == 53, heat * jnp.exp2(gain[53:54]), species)


def toward(value, k):
    lane = lax.broadcasted_iota(jnp.int32, value.shape, 1)
    azim, radial, core = lane & 3, (lane >> 2) & 3, (lane >> 4) & 1

    def ahead(step):
        return pltpu.roll(value, (128 - step) % 128, 1)

    return (
        lambda: jnp.where(core == 0, ahead(16), ahead(-16)),
        lambda: ahead(32),
        lambda: ahead(-32),
        lambda: jnp.where(radial < 3, ahead(4), ahead(-12)),
        lambda: jnp.where(radial > 0, ahead(-4), ahead(12)),
        lambda: jnp.where(azim < 3, ahead(1), ahead(-3)),
        lambda: jnp.where(azim > 0, ahead(-1), ahead(3)),
    )[k]()


def flows(counts):
    least = EARLY + LATE
    load, own = jnp.maximum(counts, least), counts
    given = [jnp.zeros_like(counts) for _ in SIZES]
    taken = [jnp.zeros_like(counts) for _ in SIZES]
    for sweep in range(SWEEPS):
        for axis in ((0,), (1, 2), (3, 4), (5, 6)):
            spare = jnp.minimum(jnp.maximum(own - least, 0), jnp.maximum(load - FLOOR, 0))
            gives = []
            for k in axis:
                other = toward(load, k)
                gap = load - other + (1 if sweep == SWEEPS - 1 else 0)
                room = jnp.maximum(WORK - other, 0)
                if len(axis) == 2:
                    room = (room + (1 if k == axis[0] else 0)) >> 1
                give = jnp.minimum(SIZES[k] - given[k], jnp.maximum(gap, 0) >> 1)
                give = jnp.minimum(jnp.minimum(give, room), spare)
                spare = spare - give
                gives.append(give)
            takes = [toward(give, OPPOSITE[k]) for k, give in zip(axis, gives)]
            for k, give, take in zip(axis, gives, takes):
                given[k], taken[k] = given[k] + give, taken[k] + take
            own = own - sum(gives)
            load = load - sum(gives) + sum(takes)
    return own, given, taken


def positions(blocks_ref):
    lane = lax.broadcasted_iota(jnp.int32, (8, 128), 1)
    found = jnp.zeros((8, 128), jnp.int32)
    for n in range(64):
        found = jnp.where(lane == blocks_ref[0, n], n, found)
    return found


def plan(me, counts, position, blocks_ref, codes, lists, sem):
    own, given, taken = flows(counts)
    row = lax.broadcasted_iota(jnp.int32, (8, 128), 0)
    lane = lax.broadcasted_iota(jnp.int32, (8, 128), 1)

    def mine(value):
        return jnp.sum(jnp.where(lane == me, value, 0), 1, keepdims=True)

    over = own - jnp.minimum(own, WORK - sum(taken))
    over = jnp.max(over, 1, keepdims=True)
    own, total = mine(own), mine(counts)
    given, taken = [mine(v) for v in given], [mine(v) for v in taken]
    received = sum(taken)
    kept = jnp.minimum(own, WORK - received)
    sent_before, taken_before = [kept], [jnp.zeros_like(kept)]
    for p in range(len(SIZES)):
        sent_before.append(sent_before[p] + given[p])
        taken_before.append(taken_before[p] + taken[p])

    late = WORK - LATE - EARLY + position
    middle = received + position - LATE
    slot = jnp.where(position < EARLY, position, jnp.where(position < EARLY + LATE, late, middle))
    final = jnp.where(position < kept, 128 + slot, lane)
    send, reply = jnp.zeros((8, 128), jnp.int32), jnp.zeros((8, 128), jnp.int32)
    step = lane - EARLY
    arrived = jnp.zeros((8, 128), jnp.int32)
    for p, (base, size) in enumerate(zip(BASES, SIZES)):
        inside = (position >= sent_before[p]) & (position < sent_before[p + 1])
        final = jnp.where(inside, 64 + base + position - sent_before[p], final)
        here = (lane >= base) & (lane < base + size)
        send = jnp.where(here, sent_before[p] + lane - base, send)
        reply = jnp.where(here, EARLY + taken_before[p] + lane - base, reply)
        inside = (step >= taken_before[p]) & (step < taken_before[p + 1])
        arrived = jnp.where(inside, 64 + base + step - taken_before[p], arrived)
    place = jnp.where(lane < EARLY, lane, EARLY + LATE + step - received)
    place = jnp.where(lane >= WORK - LATE, lane - (WORK - LATE - EARLY), place)
    wanted = jnp.clip(jnp.where(row == SEND, send, place), 0, 63)
    value = jnp.zeros((8, 128), jnp.int32)
    for n in range(64):
        value = jnp.where(wanted == n, blocks_ref[0, n], value)
    value = jnp.where((row == WORK_ROW) & (arrived > 0), arrived, value)
    value = jnp.where(row == REPLY, jnp.clip(reply, 0, WORK - 1), value)
    value = jnp.where(row == FINAL, final, value)
    rest = jnp.where(lane == 0, sent_before[-1], jnp.where(lane == 1, total, over))
    value = jnp.where(row == REST, rest, value)
    codes[...] = value
    copy = pltpu.make_async_copy(codes, lists, sem)
    copy.start()
    copy.wait()


def fetch(pairs, sem):
    copies = [pltpu.make_async_copy(*pair, sem.at[k]) for k, pair in enumerate(pairs)]
    for copy in copies:
        copy.start()
    return [copy.wait for copy in copies]


def subcycles(state, rates_ref, sums_ref):
    return lax.fori_loop(0, NCYC, lambda c, s: cycle(s, rates_ref[...], sums_ref[...]), state)


def rest_kernel(lists_ref, blocks_ref, state_ref, rates_any, sums_any, out_ref, rates, sums, held, sem):
    start, count = lists_ref[REST, 0], lists_ref[REST, 1]

    def bring(source, target):
        copy = pltpu.make_async_copy(source, target, sem)
        copy.start()
        copy.wait()

    @pl.when(start < count)
    def _():
        bring(rates_any, rates)
        bring(sums_any, sums)

        def group(g, carry):
            first = start + g * GROUP
            for k in range(GROUP):
                bring(out_ref.at[blocks_ref[0, jnp.minimum(first + k, 63)]], held.at[k])
            state = jnp.concatenate([held[k] for k in range(GROUP)], 1)
            state = subcycles(state, rates, sums)
            for k in range(GROUP):
                held[k] = state[:, k * 128 : (k + 1) * 128]

                @pl.when(first + k < count)
                def _():
                    bring(held.at[k], out_ref.at[blocks_ref[0, jnp.minimum(first + k, 63)]])

            return carry

        lax.fori_loop(0, (count - start + GROUP - 1) // GROUP, group, 0)


def react_rest(lists, blocks, state, rates, sums):
    smem, anywhere = pl.BlockSpec(memory_space=pltpu.SMEM), pl.BlockSpec(memory_space=pl.ANY)
    return pl.pallas_call(
        rest_kernel,
        out_shape=jax.ShapeDtypeStruct(state.shape, F32),
        in_specs=[smem, smem] + [anywhere] * 3,
        out_specs=anywhere,
        scratch_shapes=[
            pltpu.VMEM(rates.shape, BF16),
            pltpu.VMEM(sums.shape, BF16),
            pltpu.VMEM((GROUP, ROWS, 128), F32),
            pltpu.SemaphoreType.DMA(()),
        ],
        input_output_aliases={2: 0},
        compiler_params=pltpu.CompilerParams(vmem_limit_bytes=LIMIT),
    )(lists, blocks, state, rates, sums)


def last_kernel(
    lists_ref, blocks_ref, state_any, rates_any, sums_any, species_any, heat_any, *scratch
):
    state, species, heat, rates, sums, in_sem, out_sem, sem = scratch
    start, count = lists_ref[REST, 0], lists_ref[REST, 1]
    rows = [pl.ds(8 * i, 8) for i in range(8)]
    waits = fetch([(state_any.at[row], state.at[row]) for row in rows], in_sem)
    copies = []
    for i, row in enumerate(rows):
        waits[i]()
        turned = jnp.swapaxes(state[row], 0, 1)
        species[:, row] = turned[:53]
        heat[row] = turned[53]
        copies.append(
            pltpu.make_async_copy(species.at[:, row], species_any.at[:, row], out_sem.at[i])
        )
        copies[-1].start()
    copies.append(pltpu.make_async_copy(heat, heat_any, out_sem.at[8]))
    copies[-1].start()
    for copy in copies:
        copy.wait()

    def bring(source, target):
        copy = pltpu.make_async_copy(source, target, sem)
        copy.start()
        copy.wait()

    @pl.when(start < count)
    def _():
        bring(rates_any, rates)
        bring(sums_any, sums)

        def group(g, carry):
            first = start + g * GROUP
            at = [blocks_ref[0, jnp.minimum(first + k, 63)] for k in range(GROUP)]
            value = jnp.concatenate([state[at[k]] for k in range(GROUP)], 1)
            value = subcycles(value, rates, sums)
            for k in range(GROUP):

                @pl.when(first + k < count)
                def _():
                    state[at[k]] = value[:, k * 128 : (k + 1) * 128]

            return carry

        lax.fori_loop(0, (count - start + GROUP - 1) // GROUP, group, 0)
        for row in rows:
            turned = jnp.swapaxes(state[row], 0, 1)
            species[:, row] = turned[:53]
            heat[row] = turned[53]
        bring(species, species_any)
        bring(heat, heat_any)


def finish(lists, blocks, state, rates, sums):
    smem, anywhere = pl.BlockSpec(memory_space=pltpu.SMEM), pl.BlockSpec(memory_space=pl.ANY)
    return pl.pallas_call(
        last_kernel,
        out_shape=[jax.ShapeDtypeStruct((53, 64, 128), F32), jax.ShapeDtypeStruct((64, 128), F32)],
        in_specs=[smem, smem] + [anywhere] * 3,
        out_specs=[anywhere] * 2,
        scratch_shapes=[
            pltpu.VMEM(state.shape, F32),
            pltpu.VMEM((53, 64, 128), F32),
            pltpu.VMEM((64, 128), F32),
            pltpu.VMEM(rates.shape, BF16),
            pltpu.VMEM(sums.shape, BF16),
            pltpu.SemaphoreType.DMA((8,)),
            pltpu.SemaphoreType.DMA((9,)),
            pltpu.SemaphoreType.DMA(()),
        ],
        compiler_params=pltpu.CompilerParams(vmem_limit_bytes=LIMIT),
    )(lists, blocks, state, rates, sums)


def shifted(axis, step):
    n, me = lax.axis_size(axis), lax.axis_index(axis)
    return {axis: lax.rem(me + (n + step), n)}


def faces():
    return [shifted(axis, step) for axis in AXES for step in (-1, 1)]


def partners():
    me = lax.axis_index("stream")
    sides = [("stream", 2), ("stream", -2), ("radial", 1), ("radial", -1), ("azim", 1), ("azim", -1)]
    return [{"stream": me + 1 - 2 * lax.rem(me, 2)}] + [shifted(*side) for side in sides]


def greet(peers):
    barrier = pltpu.get_barrier_semaphore()
    for peer in peers:
        pl.semaphore_signal(barrier, inc=1, device_id=peer, device_id_type=MESH)
    return lambda: pl.semaphore_wait(barrier, len(peers))


def remote(source, target, sems, k, peer):
    return pltpu.make_async_remote_copy(
        src_ref=source,
        dst_ref=target,
        send_sem=sems[0].at[k],
        recv_sem=sems[1].at[k],
        device_id=peer,
        device_id_type=MESH,
    )


def transport(met, courant_ref, spread_ref, out, grid, edge, halo, sems, hooks):
    lane = lax.broadcasted_iota(jnp.int32, (ROWS, 128), 1)
    peers = faces()
    inner = pl.ds(1, 8)
    plans = [
        (grid.at[1, inner], grid.at[9, inner]),
        (grid.at[8, inner], grid.at[0, inner]),
        (grid.at[inner, 1], grid.at[inner, 9]),
        (grid.at[inner, 8], grid.at[inner, 0]),
        (edge, halo.at[1]),
        (edge, halo.at[0]),
    ]
    copies = [remote(*plans[k], sems, k, peers[k]) for k in range(6)]
    met()
    for k in (2, 3, 0, 1):
        copies[k].start()

    def ends(i, packed):
        for j in range(8):
            b = i * 8 + j
            turned = pltpu.roll(grid[i + 1, j + 1], 2 * b + 1, 1)
            packed = jnp.where((lane >> 1) == b, turned, packed)
        return packed

    edge[...] = lax.fori_loop(0, 8, ends, jnp.zeros((ROWS, 128), F32))
    copies[4].start()
    copies[5].start()
    hooks[0]()
    copies[4].wait()
    copies[5].wait()
    edge[...] = jnp.where((lane & 1) == 0, halo[0], halo[1])
    rate = spread_ref[...]
    keep = 1.0 - 6.0 * rate

    def cells(i, columns):
        for j in columns:
            b = i * 8 + j
            here = grid[i + 1, j + 1]
            behind = grid[i, j + 1]
            ends = pltpu.roll(edge[...], 127 - 2 * b, 1)
            left = pltpu.roll(jnp.where(lane == 127, ends, here), 1, 1)
            right = pltpu.roll(jnp.where(lane == 0, ends, here), 127, 1)
            around = (behind + grid[i + 2, j + 1]) + (grid[i + 1, j] + grid[i + 1, j + 2])
            around = around + (left + right)
            speed = courant_ref[pl.ds(b, 1), :]
            out[b] = (keep - speed) * here + rate * around + speed * behind

    def middle(i, carry):
        cells(i, range(1, 7))
        return carry

    lax.fori_loop(1, 7, middle, 0)
    hooks[1]()
    for k in range(4):
        copies[k].wait()
    blank = jnp.zeros((8, ROWS, 128), F32)
    stream, radial = lax.axis_index("stream"), lax.axis_index("radial")

    @pl.when(stream == 0)
    def _():
        grid[0, inner] = blank

    @pl.when(stream == lax.axis_size("stream") - 1)
    def _():
        grid[9, inner] = blank

    @pl.when(radial == 0)
    def _():
        grid[inner, 0] = blank

    @pl.when(radial == lax.axis_size("radial") - 1)
    def _():
        grid[inner, 9] = blank

    def sides(i, carry):
        cells(i, (0, 7))
        return carry

    def first_last(i, carry):
        cells(i * 7, range(1, 7))
        return carry

    lax.fori_loop(0, 8, sides, 0)
    lax.fori_loop(0, 2, first_last, 0)
    hooks[2]()


def chemistry(lists_ref, state, rates_ref, sums_ref, put, send, recv, reply, back, result, sems, met):
    def each(count, body):
        def four(g, carry):
            for k in range(4):
                body(4 * g + k)
            return carry

        lax.fori_loop(0, count // 4, four, 0)
        for k in range(count // 4 * 4, count):
            body(k)

    def pack(s):
        send[s] = state[lists_ref[SEND, s]]

    each(SLOTS, pack)
    met()
    peers = partners()

    def exchange(source, target, first, turned):
        found = []
        for k, (base, size) in enumerate(zip(BASES, SIZES)):
            area = pl.ds(base, size)
            peer = peers[OPPOSITE[k] if turned else k]
            found.append(remote(source.at[area], target.at[area], sems, first + k, peer))
            found[-1].start()
        return found

    def run(first, items):
        whole = subcycles(jnp.concatenate(items, 1), rates_ref, sums_ref)
        for k in range(len(items)):
            result[first + k] = whole[:, k * 128 : (k + 1) * 128]

    def own(first):
        run(first, [state[lists_ref[WORK_ROW, first + k]] for k in range(GROUP)])

    def any_item(slot):
        code = lists_ref[WORK_ROW, slot]
        there = recv[jnp.maximum(code - 64, 0)]
        return jnp.where(code < 64, state[jnp.minimum(code, 63)], there)

    def middle(g, carry):
        first = EARLY + g * GROUP
        run(first, [any_item(first + k) for k in range(GROUP)])
        return carry

    copies = exchange(send, recv, 0, False)
    own(0)
    for copy in copies:
        copy.wait()
    lax.fori_loop(0, SPAN // GROUP, middle, 0)

    def answer(s):
        reply[s] = result[lists_ref[REPLY, s]]

    each(SLOTS, answer)
    copies = exchange(reply, back, 7, True)
    own(WORK - LATE)
    for copy in copies:
        copy.wait()

    def settle(i, carry):
        for j in range(8):
            code = lists_ref[FINAL, i * 8 + j]
            here = state[jnp.minimum(code, 63)]
            there = back[jnp.clip(code - 64, 0, SLOTS - 1)]
            done = result[jnp.clip(code - 128, 0, WORK - 1)]
            put(i, j, jnp.where(code < 64, here, jnp.where(code < 128, there, done)))
        return carry

    lax.fori_loop(0, 8, settle, 0)


def into(out):
    def put(i, j, value):
        out[i * 8 + j] = value

    return put


STATE = (64, ROWS, 128)
MOVE_SCRATCH = [
    pltpu.VMEM((10, 10, ROWS, 128), F32),
    pltpu.VMEM((ROWS, 128), F32),
    pltpu.VMEM((2, ROWS, 128), F32),
    pltpu.SemaphoreType.DMA((6,)),
    pltpu.SemaphoreType.DMA((6,)),
]
CHEM_SCRATCH = [pltpu.VMEM((SLOTS, ROWS, 128), F32)] * 4 + [
    pltpu.VMEM((WORK, ROWS, 128), F32),
    pltpu.SemaphoreType.DMA((14,)),
    pltpu.SemaphoreType.DMA((14,)),
]


AGAIN_SCRATCH = [pltpu.VMEM((SLOTS, ROWS, 128), F32)] * 2 + [
    pltpu.SemaphoreType.DMA((14,)),
    pltpu.SemaphoreType.DMA((14,)),
]
COUNT_SCRATCH = [
    pltpu.VMEM((8, 8, 128), jnp.int32),
    pltpu.VMEM((4, 8, 128), jnp.int32),
    pltpu.VMEM((4, 4, 8, 128), jnp.int32),
    pltpu.SemaphoreType.DMA((13,)),
    pltpu.SemaphoreType.DMA((13,)),
    pltpu.VMEM((8, 128), jnp.int32),
    pltpu.SemaphoreType.DMA(()),
    pltpu.VMEM((2 * ROWS, 768), F32),
]


def others(axis):
    return [shifted(axis, step) for step in range(1, lax.axis_size(axis))]


def spread_counts(first, second, third, sems):
    stream, radial, azim = (lax.axis_index(axis) for axis in AXES)

    def stage(source, target, axis, start):
        copies = [remote(source, target, sems, start + k, p) for k, p in enumerate(others(axis))]
        for copy in copies:
            copy.start()

        def wait():
            for copy in copies:
                copy.wait()

        return wait

    def along_stream():
        return stage(first.at[stream], first.at[stream], "stream", 0)

    def along_radial():
        row = lax.broadcasted_iota(jnp.int32, (8, 128), 0)
        joined = first[0]
        for s in range(1, 8):
            joined = jnp.where(row == s, first[s], joined)
        second[radial] = joined
        return stage(second.at[radial], second.at[radial], "radial", 7)

    def along_azim():
        third[azim] = second[...]
        return stage(third.at[azim], third.at[azim], "azim", 10)

    def whole():
        row = lax.broadcasted_iota(jnp.int32, (8, 128), 0)
        lane = lax.broadcasted_iota(jnp.int32, (8, 128), 1)
        total = jnp.zeros((8, 128), jnp.int32)
        for a in range(4):
            for r in range(4):
                here = (lane & 15 == r * 4 + a) & (lane >> 4 == row)
                total = jnp.where(here, third[a, r], total)
        return jnp.broadcast_to(jnp.sum(total, 0, keepdims=True), (8, 128))

    return along_stream, along_radial, along_azim, whole


def communicating(kernel, name, out_shape, out_specs, specs, args, scratch):
    return pl.pallas_call(
        kernel,
        out_shape=out_shape,
        in_specs=specs,
        out_specs=out_specs,
        scratch_shapes=scratch,
        compiler_params=pltpu.CompilerParams(
            collective_id=name, has_side_effects=True, vmem_limit_bytes=LIMIT
        ),
    )(*args)


def first_steps(both, blocks, tally, species, heat, courant, spread, settings):
    nrxn = settings[0].shape[1]
    padded = -(-nrxn // 16) * 16
    brought = (tally, species, heat, courant, spread, *settings)

    def kernel(blocks_ref, *refs):
        anywhere, refs = refs[: len(brought)], refs[len(brought) :]
        out, lists, rates, sums, spread_out = refs[:5]
        near, refs = refs[5 : 5 + len(brought)], refs[5 + len(brought) :]
        fetch_sem, refs = refs[0], refs[1:]
        tally_ref, species_ref, heat_ref, courant_ref, spread_ref, *settings_refs = near
        grid, edge, halo, *sems = refs[: len(MOVE_SCRATCH)]
        refs = refs[len(MOVE_SCRATCH) :]
        first, second, third, *count_sems = refs[:5]
        codes, code_sem, table = refs[5:8]
        moved, *refs = refs[8:]
        chem, refs = refs[: len(CHEM_SCRATCH)], refs[len(CHEM_SCRATCH) :]

        met = greet(others("stream") + others("radial") + others("azim"))
        rows = [pl.ds(8 * i, 8) for i in range(8)]
        pairs = list(zip(anywhere, near))
        pairs[1:2] = [(anywhere[1].at[:, row], species_ref.at[:, row]) for row in rows]
        waits = fetch(pairs, fetch_sem)
        stream, radial, azim = (lax.axis_index(axis) for axis in AXES)
        me = (stream * 4 + radial) * 4 + azim
        waits[0]()
        own = jnp.sum(tally_ref[...], 1, keepdims=True)
        first[stream] = jnp.broadcast_to(own, (8, 128))
        stages = spread_counts(first, second, third, count_sems)
        waits[9]()
        waiting = []
        for i, row in enumerate(rows):
            waits[1 + i]()
            cells = [species_ref[:, row], heat_ref[row][None], jnp.zeros((2, 8, 128), F32)]
            grid[i + 1, pl.ds(1, 8)] = jnp.swapaxes(jnp.concatenate(cells, 0), 0, 1)
            if i == 3:
                met()
                waiting.append(stages[0]())
        found = []

        def at_once():
            for wait in waits[10:]:
                wait()
            table[pl.ds(0, 1), pl.ds(0, 128)] = jnp.zeros((1, 128), F32)
            table[pl.ds(0, 1), pl.ds(0, 54)] = spread_ref[...].reshape(1, 54)
            row = lax.broadcasted_iota(jnp.int32, (ROWS, 128), 0)
            lane = lax.broadcasted_iota(jnp.int32, (ROWS, 128), 1)
            diagonal = jnp.where(row == lane, table[pl.ds(0, 1), pl.ds(0, 128)], 0.0)
            column = jnp.sum(diagonal, 1, keepdims=True)
            spread_out[...] = jnp.broadcast_to(column, (ROWS, 128))
            found.append(positions(blocks_ref))
            waiting[0]()
            waiting.append(stages[1]())
            prepare(*settings_refs, rates, sums, table)
            waiting[1]()
            waiting.append(stages[2]())

        def at_end():
            waiting[2]()
            plan(me, stages[3](), found[0], blocks_ref, codes, lists, code_sem)

        nothing = lambda: None
        hooks = (at_once, nothing, at_end)
        transport(nothing, courant_ref, spread_out, moved, grid, edge, halo, sems, hooks)
        if not both:
            chemistry(lists, moved, rates, sums, into(out), *chem[:5], chem[5:], nothing)
            return
        grid, edge, halo, *sems = refs[: len(MOVE_SCRATCH)]
        recv, back, *again_sems = refs[len(MOVE_SCRATCH) :]

        def put(i, j, value):
            grid[i + 1, j + 1] = value

        chemistry(lists, moved, rates, sums, put, *chem[:5], chem[5:], nothing)
        hooks = (nothing, nothing, nothing)
        transport(nothing, courant_ref, spread_out, moved, grid, edge, halo, sems, hooks)
        send, _, reply, _, result = chem[:5]
        again = (send, recv, reply, back, result, again_sems)
        chemistry(lists, moved, rates, sums, into(out), *again, nothing)

    smem, vmem = pl.BlockSpec(memory_space=pltpu.SMEM), pl.BlockSpec(memory_space=pltpu.VMEM)
    return communicating(
        kernel,
        0 if both else 1,
        [
            jax.ShapeDtypeStruct(STATE, F32),
            jax.ShapeDtypeStruct((8, 128), jnp.int32),
            jax.ShapeDtypeStruct((2 * padded, 4 * ROWS), BF16),
            jax.ShapeDtypeStruct((4 * ROWS, 2 * padded), BF16),
            jax.ShapeDtypeStruct((ROWS, 128), F32),
        ],
        [vmem, smem, vmem, vmem, vmem],
        [smem] + [pl.BlockSpec(memory_space=pl.ANY)] * len(brought),
        (blocks, *brought),
        [pltpu.VMEM(x.shape, x.dtype) for x in brought]
        + [pltpu.SemaphoreType.DMA((7 + len(brought),))]
        + MOVE_SCRATCH
        + COUNT_SCRATCH
        + [pltpu.VMEM(STATE, F32)]
        + CHEM_SCRATCH
        + (MOVE_SCRATCH + AGAIN_SCRATCH if both else []),
    )


def second_step(lists, state, courant, spread, rates, sums):
    brought = (courant, spread, rates, sums)

    def kernel(lists_ref, state_any, *refs):
        anywhere, refs = refs[: len(brought)], refs[len(brought) :]
        out, near, refs = refs[0], refs[1 : 1 + len(brought)], refs[1 + len(brought) :]
        fetch_sem, refs = refs[0], refs[1:]
        courant_ref, spread_ref, rates_ref, sums_ref = near
        grid, edge, halo, *sems = refs[: len(MOVE_SCRATCH)]
        moved, *chem = refs[len(MOVE_SCRATCH) :]
        met = greet(faces() + [shifted("stream", 2), shifted("stream", -2)])
        pairs = [
            (state_any.at[pl.ds(8 * i, 8)], grid.at[i + 1, pl.ds(1, 8)]) for i in range(8)
        ]
        waits = fetch(pairs + list(zip(anywhere, near)), fetch_sem)
        for wait in waits:
            wait()
        nothing = lambda: None
        hooks = (nothing, nothing, nothing)
        transport(met, courant_ref, spread_ref, moved, grid, edge, halo, sems, hooks)
        chemistry(lists_ref, moved, rates_ref, sums_ref, into(out), *chem[:5], chem[5:], nothing)

    smem, vmem = pl.BlockSpec(memory_space=pltpu.SMEM), pl.BlockSpec(memory_space=pltpu.VMEM)
    return communicating(
        kernel,
        2,
        jax.ShapeDtypeStruct(STATE, F32),
        vmem,
        [smem] + [pl.BlockSpec(memory_space=pl.ANY)] * 5,
        (lists, state, *brought),
        [pltpu.VMEM(x.shape, x.dtype) for x in brought]
        + [pltpu.SemaphoreType.DMA((8 + len(brought),))]
        + MOVE_SCRATCH
        + [pltpu.VMEM(STATE, F32)]
        + CHEM_SCRATCH,
    )


def shards(
    component_fractions,
    kilokelvin_field,
    axial_courant_number,
    spreading_number,
    arrhenius_multiplier_exponent,
    thermal_exponents,
    arrhenius_barrier,
    balance_constant_exponents,
    enthalpy_formation,
    consumed_stoich_matrix,
    yield_stoich_matrix,
    processor_tiles_burning,
    tile_transfer_tally,
):
    shape = component_fractions.shape
    settings = (
        consumed_stoich_matrix,
        yield_stoich_matrix,
        arrhenius_multiplier_exponent,
        thermal_exponents,
        arrhenius_barrier,
        balance_constant_exponents,
        enthalpy_formation,
    )
    species = component_fractions.reshape(53, 64, 128)
    heat = kilokelvin_field.reshape(64, 128)
    courant = axial_courant_number.reshape(64, 128)
    blocks, tally = processor_tiles_burning, tile_transfer_tally
    inputs = (blocks, tally, species, heat, courant, spreading_number, settings)
    state, lists, rates, sums, _ = first_steps(True, *inputs)

    def balanced(state, lists, rates, sums):
        return finish(lists, blocks, state, rates, sums)

    def with_rest(state, lists, rates, sums):
        state, lists, rates, sums, spread = first_steps(False, *inputs)
        state = react_rest(lists, blocks, state, rates, sums)
        state = second_step(lists, state, courant, spread, rates, sums)
        return finish(lists, blocks, state, rates, sums)

    over = lists[REST, 2] > 0
    species, heat = lax.cond(over, with_rest, balanced, state, lists, rates, sums)
    return species.reshape(shape), heat.reshape(shape[1:])


def solution(mesh):
    in_specs = (
        P(None, "stream", "radial", "azim"),
        P("stream", "radial", "azim"),
        P("stream", "radial", "azim"),
        P(),
        P(),
        P(),
        P(),
        P(),
        P(),
        P(),
        P(),
        P(AXES, None),
        P(AXES, None),
    )
    out_specs = (P(None, "stream", "radial", "azim"), P("stream", "radial", "azim"))
    return jax.shard_map(shards, mesh=mesh, in_specs=in_specs, out_specs=out_specs, check_vma=False)
```

```python
import functools

import jax
import jax.numpy as jnp
from jax import lax
from jax.experimental import pallas as pl
from jax.experimental.pallas import tpu as pltpu
from jax.sharding import PartitionSpec as P

NCYC = 4
ROWS = 56
GROUP = 8
chem_step = 0.02
mass_offset = 0.05
LOG2E = 1.4426950408889634
F32 = jnp.float32
BF16 = jnp.bfloat16
MESH = pl.DeviceIdType.MESH
AXES = ("stream", "radial", "azim")
LIMIT = 63 * 2**20
WORK = 32
EARLY = 8
LATE = 8
SPAN = WORK - EARLY - LATE
FLOOR = 24
SWEEPS = 3
PAIR = 10
SIDE = 5
SIZES = (PAIR,) + (SIDE,) * 6
BASES = tuple(sum(SIZES[:k]) for k in range(7))
SLOTS = sum(SIZES)
OPPOSITE = (0, 2, 1, 4, 3, 6, 5)
SEND, WORK_ROW, REPLY, FINAL, REST = range(5)


def prepare(consumed, made, exponent, thermal, barrier, balance, enthalpy, rates, sums, table):
    half = rates.shape[0] // 2
    exponent, thermal, barrier, balance, enthalpy = (
        vector[...].reshape(1, -1) for vector in (exponent, thermal, barrier, balance, enthalpy)
    )

    def put(side, row, value):
        rows, lanes = value.shape
        table[pl.ds(row, rows), pl.ds(side * half, lanes)] = value

    def halves(value):
        high = value.astype(BF16).astype(F32)
        return high, value - high

    table[...] = jnp.zeros_like(table)
    for side, change in enumerate((0.0, balance)):
        put(side, 0, (consumed, made)[side][...])
        put(side, 53, thermal)
        put(side, 54, -LOG2E * barrier)
        put(side, 55, LOG2E * (exponent - change))
    high, low = halves(table[:ROWS])
    stacked = jnp.concatenate([high, high, low, high], 0).T
    rates[...] = stacked[: 2 * half].astype(BF16)
    heat = LOG2E * lax.dot_general(
        enthalpy,
        made[...] - consumed[...],
        (((1,), (0,)), ((), ())),
        preferred_element_type=F32,
        precision=lax.Precision.HIGHEST,
    )
    table[...] = jnp.zeros_like(table)
    for side, (gain, loss, warm) in enumerate(((made, consumed, heat), (consumed, made, -heat))):
        put(side, 0, gain[...])
        put(side, 53, warm)
        put(side, ROWS, loss[...])
    high, low = halves(chem_step * table[...])
    sums[...] = jnp.concatenate([high, low], 0)[:, : 2 * half].astype(BF16)


def parted(value):
    high = value.astype(BF16)
    return high, value - high.astype(F32)


def product(a, b):
    return lax.dot_general(a, b, (((1,), (0,)), ((), ())), preferred_element_type=F32)


def cycle(state, rates, sums):
    row = lax.broadcasted_iota(jnp.int32, state.shape, 0)
    moved = state + jnp.where(row < 53, mass_offset, jnp.where(row == 53, 0.0, 1.0))
    heat = state[53:54]
    logs = jnp.log2(moved)
    logs = jnp.where(row == 54, 1.0 / heat, jnp.where(row == 55, 1.0, logs))
    first, rest = parted(logs)
    second, third = parted(rest)
    first, second = first.astype(F32), second.astype(F32)
    stacked = jnp.concatenate([first, second, first, third], 0).astype(BF16)
    flux = jnp.exp2(product(rates, stacked))
    high, low = parted(flux)
    half = sums.shape[0] // 2
    both = product(sums, high)
    total = both[:half] + both[half:] + product(sums[:half], low.astype(BF16))
    gain, loss = total[:ROWS], total[ROWS:]
    species = (state + gain) * moved / (moved + loss)
    return jnp.where(row == 53, heat * jnp.exp2(gain[53:54]), species)


def toward(value, k):
    lane = lax.broadcasted_iota(jnp.int32, value.shape, 1)
    azim, radial, core = lane & 3, (lane >> 2) & 3, (lane >> 4) & 1

    def ahead(step):
        return pltpu.roll(value, (128 - step) % 128, 1)

    return (
        lambda: jnp.where(core == 0, ahead(16), ahead(-16)),
        lambda: ahead(32),
        lambda: ahead(-32),
        lambda: jnp.where(radial < 3, ahead(4), ahead(-12)),
        lambda: jnp.where(radial > 0, ahead(-4), ahead(12)),
        lambda: jnp.where(azim < 3, ahead(1), ahead(-3)),
        lambda: jnp.where(azim > 0, ahead(-1), ahead(3)),
    )[k]()


def flows(counts):
    least = EARLY + LATE
    load, own = jnp.maximum(counts, least), counts
    given = [jnp.zeros_like(counts) for _ in SIZES]
    taken = [jnp.zeros_like(counts) for _ in SIZES]
    for sweep in range(SWEEPS):
        for axis in ((0,), (1, 2), (3, 4), (5, 6)):
            spare = jnp.minimum(jnp.maximum(own - least, 0), jnp.maximum(load - FLOOR, 0))
            gives = []
            for k in axis:
                other = toward(load, k)
                gap = load - other + (1 if sweep == SWEEPS - 1 else 0)
                room = jnp.maximum(WORK - other, 0)
                if len(axis) == 2:
                    room = (room + (1 if k == axis[0] else 0)) >> 1
                give = jnp.minimum(SIZES[k] - given[k], jnp.maximum(gap, 0) >> 1)
                give = jnp.minimum(jnp.minimum(give, room), spare)
                spare = spare - give
                gives.append(give)
            takes = [toward(give, OPPOSITE[k]) for k, give in zip(axis, gives)]
            for k, give, take in zip(axis, gives, takes):
                given[k], taken[k] = given[k] + give, taken[k] + take
            own = own - sum(gives)
            load = load - sum(gives) + sum(takes)
    return own, given, taken


def positions(blocks_ref):
    lane = lax.broadcasted_iota(jnp.int32, (8, 128), 1)
    found = jnp.zeros((8, 128), jnp.int32)
    for n in range(64):
        found = jnp.where(lane == blocks_ref[0, n], n, found)
    return found


def plan(me, counts, position, blocks_ref, codes, lists, sem):
    own, given, taken = flows(counts)
    row = lax.broadcasted_iota(jnp.int32, (8, 128), 0)
    lane = lax.broadcasted_iota(jnp.int32, (8, 128), 1)

    def mine(value):
        return jnp.sum(jnp.where(lane == me, value, 0), 1, keepdims=True)

    over = own - jnp.minimum(own, WORK - sum(taken))
    over = jnp.max(over, 1, keepdims=True)
    own, total = mine(own), mine(counts)
    given, taken = [mine(v) for v in given], [mine(v) for v in taken]
    received = sum(taken)
    kept = jnp.minimum(own, WORK - received)
    sent_before, taken_before = [kept], [jnp.zeros_like(kept)]
    for p in range(len(SIZES)):
        sent_before.append(sent_before[p] + given[p])
        taken_before.append(taken_before[p] + taken[p])

    late = WORK - LATE - EARLY + position
    middle = received + position - LATE
    slot = jnp.where(position < EARLY, position, jnp.where(position < EARLY + LATE, late, middle))
    final = jnp.where(position < kept, 128 + slot, lane)
    send, reply = jnp.zeros((8, 128), jnp.int32), jnp.zeros((8, 128), jnp.int32)
    step = lane - EARLY
    arrived = jnp.zeros((8, 128), jnp.int32)
    for p, (base, size) in enumerate(zip(BASES, SIZES)):
        inside = (position >= sent_before[p]) & (position < sent_before[p + 1])
        final = jnp.where(inside, 64 + base + position - sent_before[p], final)
        here = (lane >= base) & (lane < base + size)
        send = jnp.where(here, sent_before[p] + lane - base, send)
        reply = jnp.where(here, EARLY + taken_before[p] + lane - base, reply)
        inside = (step >= taken_before[p]) & (step < taken_before[p + 1])
        arrived = jnp.where(inside, 64 + base + step - taken_before[p], arrived)
    place = jnp.where(lane < EARLY, lane, EARLY + LATE + step - received)
    place = jnp.where(lane >= WORK - LATE, lane - (WORK - LATE - EARLY), place)
    wanted = jnp.clip(jnp.where(row == SEND, send, place), 0, 63)
    value = jnp.zeros((8, 128), jnp.int32)
    for n in range(64):
        value = jnp.where(wanted == n, blocks_ref[0, n], value)
    value = jnp.where((row == WORK_ROW) & (arrived > 0), arrived, value)
    value = jnp.where(row == REPLY, jnp.clip(reply, 0, WORK - 1), value)
    value = jnp.where(row == FINAL, final, value)
    rest = jnp.where(lane == 0, sent_before[-1], jnp.where(lane == 1, total, over))
    value = jnp.where(row == REST, rest, value)
    codes[...] = value
    copy = pltpu.make_async_copy(codes, lists, sem)
    copy.start()
    copy.wait()


def fetch(pairs, sem):
    copies = [pltpu.make_async_copy(*pair, sem.at[k]) for k, pair in enumerate(pairs)]
    for copy in copies:
        copy.start()
    return [copy.wait for copy in copies]


def subcycles(state, rates_ref, sums_ref):
    return lax.fori_loop(0, NCYC, lambda c, s: cycle(s, rates_ref[...], sums_ref[...]), state)


def rest_kernel(lists_ref, blocks_ref, state_ref, rates_any, sums_any, out_ref, rates, sums, held, sem):
    start, count = lists_ref[REST, 0], lists_ref[REST, 1]

    def bring(source, target):
        copy = pltpu.make_async_copy(source, target, sem)
        copy.start()
        copy.wait()

    @pl.when(start < count)
    def _():
        bring(rates_any, rates)
        bring(sums_any, sums)

        def group(g, carry):
            first = start + g * GROUP
            for k in range(GROUP):
                bring(out_ref.at[blocks_ref[0, jnp.minimum(first + k, 63)]], held.at[k])
            state = jnp.concatenate([held[k] for k in range(GROUP)], 1)
            state = subcycles(state, rates, sums)
            for k in range(GROUP):
                held[k] = state[:, k * 128 : (k + 1) * 128]

                @pl.when(first + k < count)
                def _():
                    bring(held.at[k], out_ref.at[blocks_ref[0, jnp.minimum(first + k, 63)]])

            return carry

        lax.fori_loop(0, (count - start + GROUP - 1) // GROUP, group, 0)


def react_rest(lists, blocks, state, rates, sums):
    smem, anywhere = pl.BlockSpec(memory_space=pltpu.SMEM), pl.BlockSpec(memory_space=pl.ANY)
    return pl.pallas_call(
        rest_kernel,
        out_shape=jax.ShapeDtypeStruct(state.shape, F32),
        in_specs=[smem, smem] + [anywhere] * 3,
        out_specs=anywhere,
        scratch_shapes=[
            pltpu.VMEM(rates.shape, BF16),
            pltpu.VMEM(sums.shape, BF16),
            pltpu.VMEM((GROUP, ROWS, 128), F32),
            pltpu.SemaphoreType.DMA(()),
        ],
        input_output_aliases={2: 0},
        compiler_params=pltpu.CompilerParams(vmem_limit_bytes=LIMIT),
    )(lists, blocks, state, rates, sums)


def last_kernel(
    lists_ref, blocks_ref, state_any, rates_any, sums_any, species_any, heat_any, *scratch
):
    state, species, heat, rates, sums, in_sem, out_sem, sem = scratch
    start, count = lists_ref[REST, 0], lists_ref[REST, 1]
    rows = [pl.ds(8 * i, 8) for i in range(8)]
    waits = fetch([(state_any.at[row], state.at[row]) for row in rows], in_sem)
    copies = []
    for i, row in enumerate(rows):
        waits[i]()
        turned = jnp.swapaxes(state[row], 0, 1)
        species[:, row] = turned[:53]
        heat[row] = turned[53]
        copies.append(
            pltpu.make_async_copy(species.at[:, row], species_any.at[:, row], out_sem.at[i])
        )
        copies[-1].start()
    copies.append(pltpu.make_async_copy(heat, heat_any, out_sem.at[8]))
    copies[-1].start()
    for copy in copies:
        copy.wait()

    def bring(source, target):
        copy = pltpu.make_async_copy(source, target, sem)
        copy.start()
        copy.wait()

    @pl.when(start < count)
    def _():
        bring(rates_any, rates)
        bring(sums_any, sums)

        def group(g, carry):
            first = start + g * GROUP
            at = [blocks_ref[0, jnp.minimum(first + k, 63)] for k in range(GROUP)]
            value = jnp.concatenate([state[at[k]] for k in range(GROUP)], 1)
            value = subcycles(value, rates, sums)
            for k in range(GROUP):

                @pl.when(first + k < count)
                def _():
                    state[at[k]] = value[:, k * 128 : (k + 1) * 128]

            return carry

        lax.fori_loop(0, (count - start + GROUP - 1) // GROUP, group, 0)
        for row in rows:
            turned = jnp.swapaxes(state[row], 0, 1)
            species[:, row] = turned[:53]
            heat[row] = turned[53]
        bring(species, species_any)
        bring(heat, heat_any)


def finish(lists, blocks, state, rates, sums):
    smem, anywhere = pl.BlockSpec(memory_space=pltpu.SMEM), pl.BlockSpec(memory_space=pl.ANY)
    return pl.pallas_call(
        last_kernel,
        out_shape=[jax.ShapeDtypeStruct((53, 64, 128), F32), jax.ShapeDtypeStruct((64, 128), F32)],
        in_specs=[smem, smem] + [anywhere] * 3,
        out_specs=[anywhere] * 2,
        scratch_shapes=[
            pltpu.VMEM(state.shape, F32),
            pltpu.VMEM((53, 64, 128), F32),
            pltpu.VMEM((64, 128), F32),
            pltpu.VMEM(rates.shape, BF16),
            pltpu.VMEM(sums.shape, BF16),
            pltpu.SemaphoreType.DMA((8,)),
            pltpu.SemaphoreType.DMA((9,)),
            pltpu.SemaphoreType.DMA(()),
        ],
        compiler_params=pltpu.CompilerParams(vmem_limit_bytes=LIMIT),
    )(lists, blocks, state, rates, sums)


def shifted(axis, step):
    n, me = lax.axis_size(axis), lax.axis_index(axis)
    return {axis: lax.rem(me + (n + step), n)}


def faces():
    return [shifted(axis, step) for axis in AXES for step in (-1, 1)]


def partners():
    me = lax.axis_index("stream")
    sides = [("stream", 2), ("stream", -2), ("radial", 1), ("radial", -1), ("azim", 1), ("azim", -1)]
    return [{"stream": me + 1 - 2 * lax.rem(me, 2)}] + [shifted(*side) for side in sides]


def greet(peers):
    barrier = pltpu.get_barrier_semaphore()
    for peer in peers:
        pl.semaphore_signal(barrier, inc=1, device_id=peer, device_id_type=MESH)
    return lambda: pl.semaphore_wait(barrier, len(peers))


def remote(source, target, sems, k, peer):
    return pltpu.make_async_remote_copy(
        src_ref=source,
        dst_ref=target,
        send_sem=sems[0].at[k],
        recv_sem=sems[1].at[k],
        device_id=peer,
        device_id_type=MESH,
    )


def transport(met, courant_ref, spread_ref, out, grid, edge, halo, sems, hooks):
    lane = lax.broadcasted_iota(jnp.int32, (ROWS, 128), 1)
    peers = faces()
    inner = pl.ds(1, 8)
    plans = [
        (grid.at[1, inner], grid.at[9, inner]),
        (grid.at[8, inner], grid.at[0, inner]),
        (grid.at[inner, 1], grid.at[inner, 9]),
        (grid.at[inner, 8], grid.at[inner, 0]),
        (edge, halo.at[1]),
        (edge, halo.at[0]),
    ]
    copies = [remote(*plans[k], sems, k, peers[k]) for k in range(6)]
    met()
    for k in (2, 3, 0, 1):
        copies[k].start()

    def ends(i, packed):
        for j in range(8):
            b = i * 8 + j
            turned = pltpu.roll(grid[i + 1, j + 1], 2 * b + 1, 1)
            packed = jnp.where((lane >> 1) == b, turned, packed)
        return packed

    edge[...] = lax.fori_loop(0, 8, ends, jnp.zeros((ROWS, 128), F32))
    copies[4].start()
    copies[5].start()
    hooks[0]()
    copies[4].wait()
    copies[5].wait()
    edge[...] = jnp.where((lane & 1) == 0, halo[0], halo[1])
    rate = spread_ref[...]
    keep = 1.0 - 6.0 * rate

    def cells(i, columns):
        for j in columns:
            b = i * 8 + j
            here = grid[i + 1, j + 1]
            behind = grid[i, j + 1]
            ends = pltpu.roll(edge[...], 127 - 2 * b, 1)
            left = pltpu.roll(jnp.where(lane == 127, ends, here), 1, 1)
            right = pltpu.roll(jnp.where(lane == 0, ends, here), 127, 1)
            around = (behind + grid[i + 2, j + 1]) + (grid[i + 1, j] + grid[i + 1, j + 2])
            around = around + (left + right)
            speed = courant_ref[pl.ds(b, 1), :]
            out[b] = (keep - speed) * here + rate * around + speed * behind

    def middle(i, carry):
        cells(i, range(1, 7))
        return carry

    lax.fori_loop(1, 7, middle, 0)
    hooks[1]()
    for k in range(4):
        copies[k].wait()
    blank = jnp.zeros((8, ROWS, 128), F32)
    stream, radial = lax.axis_index("stream"), lax.axis_index("radial")

    @pl.when(stream == 0)
    def _():
        grid[0, inner] = blank

    @pl.when(stream == lax.axis_size("stream") - 1)
    def _():
        grid[9, inner] = blank

    @pl.when(radial == 0)
    def _():
        grid[inner, 0] = blank

    @pl.when(radial == lax.axis_size("radial") - 1)
    def _():
        grid[inner, 9] = blank

    def sides(i, carry):
        cells(i, (0, 7))
        return carry

    def first_last(i, carry):
        cells(i * 7, range(1, 7))
        return carry

    lax.fori_loop(0, 8, sides, 0)
    lax.fori_loop(0, 2, first_last, 0)
    hooks[2]()


def chemistry(lists_ref, state, rates_ref, sums_ref, put, send, recv, reply, back, result, sems, met):
    def each(count, body):
        def four(g, carry):
            for k in range(4):
                body(4 * g + k)
            return carry

        lax.fori_loop(0, count // 4, four, 0)
        for k in range(count // 4 * 4, count):
            body(k)

    def pack(s):
        send[s] = state[lists_ref[SEND, s]]

    each(SLOTS, pack)
    met()
    peers = partners()

    def exchange(source, target, first, turned):
        found = []
        for k, (base, size) in enumerate(zip(BASES, SIZES)):
            area = pl.ds(base, size)
            peer = peers[OPPOSITE[k] if turned else k]
            found.append(remote(source.at[area], target.at[area], sems, first + k, peer))
            found[-1].start()
        return found

    def run(first, items):
        whole = subcycles(jnp.concatenate(items, 1), rates_ref, sums_ref)
        for k in range(len(items)):
            result[first + k] = whole[:, k * 128 : (k + 1) * 128]

    def own(first):
        run(first, [state[lists_ref[WORK_ROW, first + k]] for k in range(GROUP)])

    def any_item(slot):
        code = lists_ref[WORK_ROW, slot]
        there = recv[jnp.maximum(code - 64, 0)]
        return jnp.where(code < 64, state[jnp.minimum(code, 63)], there)

    def middle(g, carry):
        first = EARLY + g * GROUP
        run(first, [any_item(first + k) for k in range(GROUP)])
        return carry

    copies = exchange(send, recv, 0, False)
    own(0)
    for copy in copies:
        copy.wait()
    lax.fori_loop(0, SPAN // GROUP, middle, 0)

    def answer(s):
        reply[s] = result[lists_ref[REPLY, s]]

    each(SLOTS, answer)
    copies = exchange(reply, back, 7, True)
    own(WORK - LATE)
    for copy in copies:
        copy.wait()

    def settle(i, carry):
        for j in range(8):
            code = lists_ref[FINAL, i * 8 + j]
            here = state[jnp.minimum(code, 63)]
            there = back[jnp.clip(code - 64, 0, SLOTS - 1)]
            done = result[jnp.clip(code - 128, 0, WORK - 1)]
            put(i, j, jnp.where(code < 64, here, jnp.where(code < 128, there, done)))
        return carry

    lax.fori_loop(0, 8, settle, 0)


def into(out):
    def put(i, j, value):
        out[i * 8 + j] = value

    return put


STATE = (64, ROWS, 128)
MOVE_SCRATCH = [
    pltpu.VMEM((10, 10, ROWS, 128), F32),
    pltpu.VMEM((ROWS, 128), F32),
    pltpu.VMEM((2, ROWS, 128), F32),
    pltpu.SemaphoreType.DMA((6,)),
    pltpu.SemaphoreType.DMA((6,)),
]
CHEM_SCRATCH = [pltpu.VMEM((SLOTS, ROWS, 128), F32)] * 4 + [
    pltpu.VMEM((WORK, ROWS, 128), F32),
    pltpu.SemaphoreType.DMA((14,)),
    pltpu.SemaphoreType.DMA((14,)),
]


AGAIN_SCRATCH = [pltpu.VMEM((SLOTS, ROWS, 128), F32)] * 2 + [
    pltpu.SemaphoreType.DMA((14,)),
    pltpu.SemaphoreType.DMA((14,)),
]
COUNT_SCRATCH = [
    pltpu.VMEM((8, 8, 128), jnp.int32),
    pltpu.VMEM((16, 8, 128), jnp.int32),
    pltpu.SemaphoreType.DMA((22,)),
    pltpu.SemaphoreType.DMA((22,)),
    pltpu.VMEM((8, 128), jnp.int32),
    pltpu.SemaphoreType.DMA(()),
    pltpu.VMEM((2 * ROWS, 768), F32),
]


def others(axis):
    n = lax.axis_size(axis)
    return [shifted(axis, step) for step in sorted(range(1, n), key=lambda step: -min(step, n - step))]


def plane():
    far = (0, 1, 2, 1)
    steps = sorted(range(1, 16), key=lambda step: -far[step // 4] - far[step % 4])
    return [{**shifted("radial", step // 4), **shifted("azim", step % 4)} for step in steps]


def spread_counts(first, second, sems):
    stream, radial, azim = (lax.axis_index(axis) for axis in AXES)

    def stage(buffer, peers, start):
        copies = [remote(buffer, buffer, sems, start + k, p) for k, p in enumerate(peers)]
        for copy in copies:
            copy.start()

        def wait():
            for copy in copies:
                copy.wait()

        return wait

    def along_stream():
        return stage(first.at[stream], others("stream"), 0)

    def in_plane():
        row = lax.broadcasted_iota(jnp.int32, (8, 128), 0)
        joined = first[0]
        for s in range(1, 8):
            joined = jnp.where(row == s, first[s], joined)
        second[radial * 4 + azim] = joined
        return stage(second.at[radial * 4 + azim], plane(), 7)

    def whole():
        row = lax.broadcasted_iota(jnp.int32, (8, 128), 0)
        lane = lax.broadcasted_iota(jnp.int32, (8, 128), 1)
        total = jnp.zeros((8, 128), jnp.int32)
        for place in range(16):
            here = (lane & 15 == place) & (lane >> 4 == row)
            total = jnp.where(here, second[place], total)
        return jnp.broadcast_to(jnp.sum(total, 0, keepdims=True), (8, 128))

    return along_stream, in_plane, whole


def communicating(kernel, name, out_shape, out_specs, specs, args, scratch):
    return pl.pallas_call(
        kernel,
        out_shape=out_shape,
        in_specs=specs,
        out_specs=out_specs,
        scratch_shapes=scratch,
        compiler_params=pltpu.CompilerParams(
            collective_id=name, has_side_effects=True, vmem_limit_bytes=LIMIT
        ),
    )(*args)


def first_steps(both, blocks, tally, species, heat, courant, spread, settings):
    nrxn = settings[0].shape[1]
    padded = -(-nrxn // 16) * 16
    brought = (tally, species, heat, courant, spread, *settings)

    def kernel(blocks_ref, *refs):
        anywhere, refs = refs[: len(brought)], refs[len(brought) :]
        out, lists, rates, sums, spread_out = refs[:5]
        near, refs = refs[5 : 5 + len(brought)], refs[5 + len(brought) :]
        fetch_sem, refs = refs[0], refs[1:]
        tally_ref, species_ref, heat_ref, courant_ref, spread_ref, *settings_refs = near
        grid, edge, halo, *sems = refs[: len(MOVE_SCRATCH)]
        refs = refs[len(MOVE_SCRATCH) :]
        first, second, *count_sems = refs[:4]
        codes, code_sem, table = refs[4:7]
        moved, *refs = refs[7:]
        chem, refs = refs[: len(CHEM_SCRATCH)], refs[len(CHEM_SCRATCH) :]

        rows = [pl.ds(8 * i, 8) for i in range(8)]
        pairs = list(zip(anywhere, near))
        pairs[1:2] = [(anywhere[1].at[:, row], species_ref.at[:, row]) for row in rows]
        waits = fetch(pairs, fetch_sem)
        met = greet(others("stream") + plane())
        stream, radial, azim = (lax.axis_index(axis) for axis in AXES)
        me = (stream * 4 + radial) * 4 + azim
        waits[0]()
        own = jnp.sum(tally_ref[...], 1, keepdims=True)
        first[stream] = jnp.broadcast_to(own, (8, 128))
        stages = spread_counts(first, second, count_sems)
        met()
        waiting = [stages[0]()]
        waits[9]()
        for i, row in enumerate(rows):
            waits[1 + i]()
            cells = [species_ref[:, row], heat_ref[row][None], jnp.zeros((2, 8, 128), F32)]
            grid[i + 1, pl.ds(1, 8)] = jnp.swapaxes(jnp.concatenate(cells, 0), 0, 1)
        found = []

        def at_once():
            for wait in waits[10:]:
                wait()
            table[pl.ds(0, 1), pl.ds(0, 128)] = jnp.zeros((1, 128), F32)
            table[pl.ds(0, 1), pl.ds(0, 54)] = spread_ref[...].reshape(1, 54)
            row = lax.broadcasted_iota(jnp.int32, (ROWS, 128), 0)
            lane = lax.broadcasted_iota(jnp.int32, (ROWS, 128), 1)
            diagonal = jnp.where(row == lane, table[pl.ds(0, 1), pl.ds(0, 128)], 0.0)
            column = jnp.sum(diagonal, 1, keepdims=True)
            spread_out[...] = jnp.broadcast_to(column, (ROWS, 128))
            found.append(positions(blocks_ref))
            waiting[0]()
            waiting.append(stages[1]())
            prepare(*settings_refs, rates, sums, table)

        def at_end():
            waiting[1]()
            plan(me, stages[2](), found[0], blocks_ref, codes, lists, code_sem)

        nothing = lambda: None
        hooks = (at_once, nothing, at_end)
        transport(nothing, courant_ref, spread_out, moved, grid, edge, halo, sems, hooks)
        if not both:
            chemistry(lists, moved, rates, sums, into(out), *chem[:5], chem[5:], nothing)
            return
        grid, edge, halo, *sems = refs[: len(MOVE_SCRATCH)]
        recv, back, *again_sems = refs[len(MOVE_SCRATCH) :]

        def put(i, j, value):
            grid[i + 1, j + 1] = value

        chemistry(lists, moved, rates, sums, put, *chem[:5], chem[5:], nothing)
        hooks = (nothing, nothing, nothing)
        transport(nothing, courant_ref, spread_out, moved, grid, edge, halo, sems, hooks)
        send, _, reply, _, result = chem[:5]
        again = (send, recv, reply, back, result, again_sems)
        chemistry(lists, moved, rates, sums, into(out), *again, nothing)

    smem, vmem = pl.BlockSpec(memory_space=pltpu.SMEM), pl.BlockSpec(memory_space=pltpu.VMEM)
    return communicating(
        kernel,
        0 if both else 1,
        [
            jax.ShapeDtypeStruct(STATE, F32),
            jax.ShapeDtypeStruct((8, 128), jnp.int32),
            jax.ShapeDtypeStruct((2 * padded, 4 * ROWS), BF16),
            jax.ShapeDtypeStruct((4 * ROWS, 2 * padded), BF16),
            jax.ShapeDtypeStruct((ROWS, 128), F32),
        ],
        [vmem, smem, vmem, vmem, vmem],
        [smem] + [pl.BlockSpec(memory_space=pl.ANY)] * len(brought),
        (blocks, *brought),
        [pltpu.VMEM(x.shape, x.dtype) for x in brought]
        + [pltpu.SemaphoreType.DMA((7 + len(brought),))]
        + MOVE_SCRATCH
        + COUNT_SCRATCH
        + [pltpu.VMEM(STATE, F32)]
        + CHEM_SCRATCH
        + (MOVE_SCRATCH + AGAIN_SCRATCH if both else []),
    )


def second_step(lists, state, courant, spread, rates, sums):
    brought = (courant, spread, rates, sums)

    def kernel(lists_ref, state_any, *refs):
        anywhere, refs = refs[: len(brought)], refs[len(brought) :]
        out, near, refs = refs[0], refs[1 : 1 + len(brought)], refs[1 + len(brought) :]
        fetch_sem, refs = refs[0], refs[1:]
        courant_ref, spread_ref, rates_ref, sums_ref = near
        grid, edge, halo, *sems = refs[: len(MOVE_SCRATCH)]
        moved, *chem = refs[len(MOVE_SCRATCH) :]
        met = greet(faces() + [shifted("stream", 2), shifted("stream", -2)])
        pairs = [
            (state_any.at[pl.ds(8 * i, 8)], grid.at[i + 1, pl.ds(1, 8)]) for i in range(8)
        ]
        waits = fetch(pairs + list(zip(anywhere, near)), fetch_sem)
        for wait in waits:
            wait()
        nothing = lambda: None
        hooks = (nothing, nothing, nothing)
        transport(met, courant_ref, spread_ref, moved, grid, edge, halo, sems, hooks)
        chemistry(lists_ref, moved, rates_ref, sums_ref, into(out), *chem[:5], chem[5:], nothing)

    smem, vmem = pl.BlockSpec(memory_space=pltpu.SMEM), pl.BlockSpec(memory_space=pltpu.VMEM)
    return communicating(
        kernel,
        2,
        jax.ShapeDtypeStruct(STATE, F32),
        vmem,
        [smem] + [pl.BlockSpec(memory_space=pl.ANY)] * 5,
        (lists, state, *brought),
        [pltpu.VMEM(x.shape, x.dtype) for x in brought]
        + [pltpu.SemaphoreType.DMA((8 + len(brought),))]
        + MOVE_SCRATCH
        + [pltpu.VMEM(STATE, F32)]
        + CHEM_SCRATCH,
    )


def shards(
    component_fractions,
    kilokelvin_field,
    axial_courant_number,
    spreading_number,
    arrhenius_multiplier_exponent,
    thermal_exponents,
    arrhenius_barrier,
    balance_constant_exponents,
    enthalpy_formation,
    consumed_stoich_matrix,
    yield_stoich_matrix,
    processor_tiles_burning,
    tile_transfer_tally,
):
    shape = component_fractions.shape
    settings = (
        consumed_stoich_matrix,
        yield_stoich_matrix,
        arrhenius_multiplier_exponent,
        thermal_exponents,
        arrhenius_barrier,
        balance_constant_exponents,
        enthalpy_formation,
    )
    species = component_fractions.reshape(53, 64, 128)
    heat = kilokelvin_field.reshape(64, 128)
    courant = axial_courant_number.reshape(64, 128)
    blocks, tally = processor_tiles_burning, tile_transfer_tally
    inputs = (blocks, tally, species, heat, courant, spreading_number, settings)
    state, lists, rates, sums, _ = first_steps(True, *inputs)

    def balanced(state, lists, rates, sums):
        return finish(lists, blocks, state, rates, sums)

    def with_rest(state, lists, rates, sums):
        state, lists, rates, sums, spread = first_steps(False, *inputs)
        state = react_rest(lists, blocks, state, rates, sums)
        state = second_step(lists, state, courant, spread, rates, sums)
        return finish(lists, blocks, state, rates, sums)

    over = lists[REST, 2] > 0
    species, heat = lax.cond(over, with_rest, balanced, state, lists, rates, sums)
    return species.reshape(shape), heat.reshape(shape[1:])


def solution(mesh):
    in_specs = (
        P(None, "stream", "radial", "azim"),
        P("stream", "radial", "azim"),
        P("stream", "radial", "azim"),
        P(),
        P(),
        P(),
        P(),
        P(),
        P(),
        P(),
        P(),
        P(AXES, None),
        P(AXES, None),
    )
    out_specs = (P(None, "stream", "radial", "azim"), P("stream", "radial", "azim"))
    return jax.shard_map(shards, mesh=mesh, in_specs=in_specs, out_specs=out_specs, check_vma=False)
```

```python
import functools

import jax
import jax.numpy as jnp
from jax import lax
from jax.experimental import pallas as pl
from jax.experimental.pallas import tpu as pltpu
from jax.sharding import PartitionSpec as P

NCYC = 4
ROWS = 56
GROUP = 8
chem_step = 0.02
mass_offset = 0.05
LOG2E = 1.4426950408889634
F32 = jnp.float32
BF16 = jnp.bfloat16
MESH = pl.DeviceIdType.MESH
AXES = ("stream", "radial", "azim")
LIMIT = 63 * 2**20
WORK = 32
EARLY = 8
LATE = 8
SPAN = WORK - EARLY - LATE
FLOOR = 24
SWEEPS = 3
PAIR = 10
SIDE = 5
SIZES = (PAIR,) + (SIDE,) * 6
BASES = tuple(sum(SIZES[:k]) for k in range(7))
SLOTS = sum(SIZES)
OPPOSITE = (0, 2, 1, 4, 3, 6, 5)
SEND, WORK_ROW, REPLY, FINAL, REST = range(5)


def prepare(consumed, made, exponent, thermal, barrier, balance, enthalpy, rates, sums, table):
    half = rates.shape[0] // 2
    exponent, thermal, barrier, balance, enthalpy = (
        vector[...].reshape(1, -1) for vector in (exponent, thermal, barrier, balance, enthalpy)
    )

    def put(side, row, value):
        rows, lanes = value.shape
        table[pl.ds(row, rows), pl.ds(side * half, lanes)] = value

    def halves(value):
        high = value.astype(BF16).astype(F32)
        return high, value - high

    table[...] = jnp.zeros_like(table)
    for side, change in enumerate((0.0, balance)):
        put(side, 0, (consumed, made)[side][...])
        put(side, 53, thermal)
        put(side, 54, -LOG2E * barrier)
        put(side, 55, LOG2E * (exponent - change))
    high, low = halves(table[:ROWS])
    stacked = jnp.concatenate([high, high, low, high], 0).T
    rates[...] = stacked[: 2 * half].astype(BF16)
    heat = LOG2E * lax.dot_general(
        enthalpy,
        made[...] - consumed[...],
        (((1,), (0,)), ((), ())),
        preferred_element_type=F32,
        precision=lax.Precision.HIGHEST,
    )
    table[...] = jnp.zeros_like(table)
    for side, (gain, loss, warm) in enumerate(((made, consumed, heat), (consumed, made, -heat))):
        put(side, 0, gain[...])
        put(side, 53, warm)
        put(side, ROWS, loss[...])
    high, low = halves(chem_step * table[...])
    sums[...] = jnp.concatenate([high, low], 0)[:, : 2 * half].astype(BF16)


def parted(value):
    high = value.astype(BF16)
    return high, value - high.astype(F32)


def product(a, b):
    return lax.dot_general(a, b, (((1,), (0,)), ((), ())), preferred_element_type=F32)


def cycle(state, rates, sums):
    row = lax.broadcasted_iota(jnp.int32, state.shape, 0)
    moved = state + jnp.where(row < 53, mass_offset, jnp.where(row == 53, 0.0, 1.0))
    heat = state[53:54]
    logs = jnp.log2(moved)
    logs = jnp.where(row == 54, 1.0 / heat, jnp.where(row == 55, 1.0, logs))
    first, rest = parted(logs)
    second, third = parted(rest)
    first, second = first.astype(F32), second.astype(F32)
    stacked = jnp.concatenate([first, second, first, third], 0).astype(BF16)
    count, half = rates.shape[0], sums.shape[0] // 2
    size = count if state.shape[1] <= GROUP * 128 else 256
    total = None
    for start in range(0, count, size):
        stop = min(start + size, count)
        flux = jnp.exp2(product(rates[start:stop], stacked))
        high, low = parted(flux)
        both = product(sums[:, start:stop], high)
        part = both[:half] + both[half:] + product(sums[:half, start:stop], low.astype(BF16))
        total = part if total is None else total + part
    gain, loss = total[:ROWS], total[ROWS:]
    species = (state + gain) * moved / (moved + loss)
    return jnp.where(row == 53, heat * jnp.exp2(gain[53:54]), species)


def toward(value, k):
    lane = lax.broadcasted_iota(jnp.int32, value.shape, 1)
    azim, radial, core = lane & 3, (lane >> 2) & 3, (lane >> 4) & 1

    def ahead(step):
        return pltpu.roll(value, (128 - step) % 128, 1)

    return (
        lambda: jnp.where(core == 0, ahead(16), ahead(-16)),
        lambda: ahead(32),
        lambda: ahead(-32),
        lambda: jnp.where(radial < 3, ahead(4), ahead(-12)),
        lambda: jnp.where(radial > 0, ahead(-4), ahead(12)),
        lambda: jnp.where(azim < 3, ahead(1), ahead(-3)),
        lambda: jnp.where(azim > 0, ahead(-1), ahead(3)),
    )[k]()


def flows(counts):
    least = EARLY + LATE
    load, own = jnp.maximum(counts, least), counts
    given = [jnp.zeros_like(counts) for _ in SIZES]
    taken = [jnp.zeros_like(counts) for _ in SIZES]
    for sweep in range(SWEEPS):
        for axis in ((0,), (1, 2), (3, 4), (5, 6)):
            spare = jnp.minimum(jnp.maximum(own - least, 0), jnp.maximum(load - FLOOR, 0))
            gives = []
            for k in axis:
                other = toward(load, k)
                gap = load - other + (1 if sweep == SWEEPS - 1 else 0)
                room = jnp.maximum(WORK - other, 0)
                if len(axis) == 2:
                    room = (room + (1 if k == axis[0] else 0)) >> 1
                give = jnp.minimum(SIZES[k] - given[k], jnp.maximum(gap, 0) >> 1)
                give = jnp.minimum(jnp.minimum(give, room), spare)
                spare = spare - give
                gives.append(give)
            takes = [toward(give, OPPOSITE[k]) for k, give in zip(axis, gives)]
            for k, give, take in zip(axis, gives, takes):
                given[k], taken[k] = given[k] + give, taken[k] + take
            own = own - sum(gives)
            load = load - sum(gives) + sum(takes)
    return own, given, taken


def positions(blocks_ref):
    lane = lax.broadcasted_iota(jnp.int32, (8, 128), 1)
    found = jnp.zeros((8, 128), jnp.int32)
    for n in range(64):
        found = jnp.where(lane == blocks_ref[0, n], n, found)
    return found


def plan(me, counts, position, blocks_ref, codes, lists, sem):
    own, given, taken = flows(counts)
    row = lax.broadcasted_iota(jnp.int32, (8, 128), 0)
    lane = lax.broadcasted_iota(jnp.int32, (8, 128), 1)

    def mine(value):
        return jnp.sum(jnp.where(lane == me, value, 0), 1, keepdims=True)

    over = own - jnp.minimum(own, WORK - sum(taken))
    over = jnp.max(over, 1, keepdims=True)
    own, total = mine(own), mine(counts)
    given, taken = [mine(v) for v in given], [mine(v) for v in taken]
    received = sum(taken)
    kept = jnp.minimum(own, WORK - received)
    sent_before, taken_before = [kept], [jnp.zeros_like(kept)]
    for p in range(len(SIZES)):
        sent_before.append(sent_before[p] + given[p])
        taken_before.append(taken_before[p] + taken[p])

    late = WORK - LATE - EARLY + position
    middle = received + position - LATE
    slot = jnp.where(position < EARLY, position, jnp.where(position < EARLY + LATE, late, middle))
    final = jnp.where(position < kept, 128 + slot, lane)
    send, reply = jnp.zeros((8, 128), jnp.int32), jnp.zeros((8, 128), jnp.int32)
    step = lane - EARLY
    arrived = jnp.zeros((8, 128), jnp.int32)
    for p, (base, size) in enumerate(zip(BASES, SIZES)):
        inside = (position >= sent_before[p]) & (position < sent_before[p + 1])
        final = jnp.where(inside, 64 + base + position - sent_before[p], final)
        here = (lane >= base) & (lane < base + size)
        send = jnp.where(here, sent_before[p] + lane - base, send)
        reply = jnp.where(here, EARLY + taken_before[p] + lane - base, reply)
        inside = (step >= taken_before[p]) & (step < taken_before[p + 1])
        arrived = jnp.where(inside, 64 + base + step - taken_before[p], arrived)
    place = jnp.where(lane < EARLY, lane, EARLY + LATE + step - received)
    place = jnp.where(lane >= WORK - LATE, lane - (WORK - LATE - EARLY), place)
    wanted = jnp.clip(jnp.where(row == SEND, send, place), 0, 63)
    value = jnp.zeros((8, 128), jnp.int32)
    for n in range(64):
        value = jnp.where(wanted == n, blocks_ref[0, n], value)
    value = jnp.where((row == WORK_ROW) & (arrived > 0), arrived, value)
    value = jnp.where(row == REPLY, jnp.clip(reply, 0, WORK - 1), value)
    value = jnp.where(row == FINAL, final, value)
    rest = jnp.where(lane == 0, sent_before[-1], jnp.where(lane == 1, total, over))
    value = jnp.where(row == REST, rest, value)
    codes[...] = value
    copy = pltpu.make_async_copy(codes, lists, sem)
    copy.start()
    copy.wait()


def fetch(pairs, sem):
    copies = [pltpu.make_async_copy(*pair, sem.at[k]) for k, pair in enumerate(pairs)]
    for copy in copies:
        copy.start()
    return [copy.wait for copy in copies]


def subcycles(state, rates_ref, sums_ref):
    return lax.fori_loop(0, NCYC, lambda c, s: cycle(s, rates_ref[...], sums_ref[...]), state)


def rest_kernel(lists_ref, blocks_ref, state_ref, rates_any, sums_any, out_ref, rates, sums, held, sem):
    start, count = lists_ref[REST, 0], lists_ref[REST, 1]

    def bring(source, target):
        copy = pltpu.make_async_copy(source, target, sem)
        copy.start()
        copy.wait()

    @pl.when(start < count)
    def _():
        bring(rates_any, rates)
        bring(sums_any, sums)

        def group(g, carry):
            first = start + g * GROUP
            for k in range(GROUP):
                bring(out_ref.at[blocks_ref[0, jnp.minimum(first + k, 63)]], held.at[k])
            state = jnp.concatenate([held[k] for k in range(GROUP)], 1)
            state = subcycles(state, rates, sums)
            for k in range(GROUP):
                held[k] = state[:, k * 128 : (k + 1) * 128]

                @pl.when(first + k < count)
                def _():
                    bring(held.at[k], out_ref.at[blocks_ref[0, jnp.minimum(first + k, 63)]])

            return carry

        lax.fori_loop(0, (count - start + GROUP - 1) // GROUP, group, 0)


def react_rest(lists, blocks, state, rates, sums):
    smem, anywhere = pl.BlockSpec(memory_space=pltpu.SMEM), pl.BlockSpec(memory_space=pl.ANY)
    return pl.pallas_call(
        rest_kernel,
        out_shape=jax.ShapeDtypeStruct(state.shape, F32),
        in_specs=[smem, smem] + [anywhere] * 3,
        out_specs=anywhere,
        scratch_shapes=[
            pltpu.VMEM(rates.shape, BF16),
            pltpu.VMEM(sums.shape, BF16),
            pltpu.VMEM((GROUP, ROWS, 128), F32),
            pltpu.SemaphoreType.DMA(()),
        ],
        input_output_aliases={2: 0},
        compiler_params=pltpu.CompilerParams(vmem_limit_bytes=LIMIT),
    )(lists, blocks, state, rates, sums)


def last_kernel(
    lists_ref, blocks_ref, state_any, rates_any, sums_any, species_any, heat_any, *scratch
):
    state, species, heat, rates, sums, in_sem, out_sem, sem = scratch
    start, count = lists_ref[REST, 0], lists_ref[REST, 1]
    rows = [pl.ds(8 * i, 8) for i in range(8)]
    waits = fetch([(state_any.at[row], state.at[row]) for row in rows], in_sem)
    copies = []
    for i, row in enumerate(rows):
        waits[i]()
        turned = jnp.swapaxes(state[row], 0, 1)
        species[:, row] = turned[:53]
        heat[row] = turned[53]
        copies.append(
            pltpu.make_async_copy(species.at[:, row], species_any.at[:, row], out_sem.at[i])
        )
        copies[-1].start()
    copies.append(pltpu.make_async_copy(heat, heat_any, out_sem.at[8]))
    copies[-1].start()
    for copy in copies:
        copy.wait()

    def bring(source, target):
        copy = pltpu.make_async_copy(source, target, sem)
        copy.start()
        copy.wait()

    @pl.when(start < count)
    def _():
        bring(rates_any, rates)
        bring(sums_any, sums)

        def group(g, carry):
            first = start + g * GROUP
            at = [blocks_ref[0, jnp.minimum(first + k, 63)] for k in range(GROUP)]
            value = jnp.concatenate([state[at[k]] for k in range(GROUP)], 1)
            value = subcycles(value, rates, sums)
            for k in range(GROUP):

                @pl.when(first + k < count)
                def _():
                    state[at[k]] = value[:, k * 128 : (k + 1) * 128]

            return carry

        lax.fori_loop(0, (count - start + GROUP - 1) // GROUP, group, 0)
        for row in rows:
            turned = jnp.swapaxes(state[row], 0, 1)
            species[:, row] = turned[:53]
            heat[row] = turned[53]
        bring(species, species_any)
        bring(heat, heat_any)


def finish(lists, blocks, state, rates, sums):
    smem, anywhere = pl.BlockSpec(memory_space=pltpu.SMEM), pl.BlockSpec(memory_space=pl.ANY)
    return pl.pallas_call(
        last_kernel,
        out_shape=[jax.ShapeDtypeStruct((53, 64, 128), F32), jax.ShapeDtypeStruct((64, 128), F32)],
        in_specs=[smem, smem] + [anywhere] * 3,
        out_specs=[anywhere] * 2,
        scratch_shapes=[
            pltpu.VMEM(state.shape, F32),
            pltpu.VMEM((53, 64, 128), F32),
            pltpu.VMEM((64, 128), F32),
            pltpu.VMEM(rates.shape, BF16),
            pltpu.VMEM(sums.shape, BF16),
            pltpu.SemaphoreType.DMA((8,)),
            pltpu.SemaphoreType.DMA((9,)),
            pltpu.SemaphoreType.DMA(()),
        ],
        compiler_params=pltpu.CompilerParams(vmem_limit_bytes=LIMIT),
    )(lists, blocks, state, rates, sums)


def shifted(axis, step):
    n, me = lax.axis_size(axis), lax.axis_index(axis)
    return {axis: lax.rem(me + (n + step), n)}


def faces():
    return [shifted(axis, step) for axis in AXES for step in (-1, 1)]


def partners():
    me = lax.axis_index("stream")
    sides = [("stream", 2), ("stream", -2), ("radial", 1), ("radial", -1), ("azim", 1), ("azim", -1)]
    return [{"stream": me + 1 - 2 * lax.rem(me, 2)}] + [shifted(*side) for side in sides]


def greet(peers):
    barrier = pltpu.get_barrier_semaphore()
    for peer in peers:
        pl.semaphore_signal(barrier, inc=1, device_id=peer, device_id_type=MESH)
    return lambda: pl.semaphore_wait(barrier, len(peers))


def remote(source, target, sems, k, peer):
    return pltpu.make_async_remote_copy(
        src_ref=source,
        dst_ref=target,
        send_sem=sems[0].at[k],
        recv_sem=sems[1].at[k],
        device_id=peer,
        device_id_type=MESH,
    )


def face_copies(grid, edge, halo, sems):
    peers = faces()
    inner = pl.ds(1, 8)
    plans = [
        (grid.at[1, inner], grid.at[9, inner]),
        (grid.at[8, inner], grid.at[0, inner]),
        (grid.at[inner, 1], grid.at[inner, 9]),
        (grid.at[inner, 8], grid.at[inner, 0]),
        (edge, halo.at[1]),
        (edge, halo.at[0]),
    ]
    return [remote(*plans[k], sems, k, peers[k]) for k in range(6)]


def send_faces(copies):
    for k in (2, 3, 0, 1):
        copies[k].start()


def transport(copies, courant_ref, spread_ref, out, grid, edge, halo, hooks):
    lane = lax.broadcasted_iota(jnp.int32, (ROWS, 128), 1)
    inner = pl.ds(1, 8)

    def ends(i, packed):
        for j in range(8):
            b = i * 8 + j
            turned = pltpu.roll(grid[i + 1, j + 1], 2 * b + 1, 1)
            packed = jnp.where((lane >> 1) == b, turned, packed)
        return packed

    edge[...] = lax.fori_loop(0, 8, ends, jnp.zeros((ROWS, 128), F32))
    copies[4].start()
    copies[5].start()
    hooks[0]()
    copies[4].wait()
    copies[5].wait()
    edge[...] = jnp.where((lane & 1) == 0, halo[0], halo[1])
    rate = spread_ref[...]
    keep = 1.0 - 6.0 * rate

    def cells(i, columns):
        for j in columns:
            b = i * 8 + j
            here = grid[i + 1, j + 1]
            behind = grid[i, j + 1]
            ends = pltpu.roll(edge[...], 127 - 2 * b, 1)
            left = pltpu.roll(jnp.where(lane == 127, ends, here), 1, 1)
            right = pltpu.roll(jnp.where(lane == 0, ends, here), 127, 1)
            around = (behind + grid[i + 2, j + 1]) + (grid[i + 1, j] + grid[i + 1, j + 2])
            around = around + (left + right)
            speed = courant_ref[pl.ds(b, 1), :]
            out[b] = (keep - speed) * here + rate * around + speed * behind

    def middle(i, carry):
        cells(i, range(1, 7))
        return carry

    lax.fori_loop(1, 7, middle, 0)
    hooks[1]()
    for k in range(4):
        copies[k].wait()
    blank = jnp.zeros((8, ROWS, 128), F32)
    stream, radial = lax.axis_index("stream"), lax.axis_index("radial")

    @pl.when(stream == 0)
    def _():
        grid[0, inner] = blank

    @pl.when(stream == lax.axis_size("stream") - 1)
    def _():
        grid[9, inner] = blank

    @pl.when(radial == 0)
    def _():
        grid[inner, 0] = blank

    @pl.when(radial == lax.axis_size("radial") - 1)
    def _():
        grid[inner, 9] = blank

    def sides(i, carry):
        cells(i, (0, 7))
        return carry

    def first_last(i, carry):
        cells(i * 7, range(1, 7))
        return carry

    lax.fori_loop(0, 8, sides, 0)
    lax.fori_loop(0, 2, first_last, 0)
    hooks[2]()


def chemistry(lists_ref, state, rates_ref, sums_ref, places, send, recv, reply, back, result, sems, met):
    put, border, row = places

    def each(count, body):
        def four(g, carry):
            for k in range(4):
                body(4 * g + k)
            return carry

        lax.fori_loop(0, count // 4, four, 0)
        for k in range(count // 4 * 4, count):
            body(k)

    def pack(s):
        send[s] = state[lists_ref[SEND, s]]

    each(SLOTS, pack)
    met()
    peers = partners()

    def exchange(source, target, first, turned):
        found = []
        for k, (base, size) in enumerate(zip(BASES, SIZES)):
            area = pl.ds(base, size)
            peer = peers[OPPOSITE[k] if turned else k]
            found.append(remote(source.at[area], target.at[area], sems, first + k, peer))
            found[-1].start()
        return found

    def run(first, items):
        whole = subcycles(jnp.concatenate(items, 1), rates_ref, sums_ref)
        for k in range(len(items)):
            result[first + k] = whole[:, k * 128 : (k + 1) * 128]

    def own(first):
        run(first, [state[lists_ref[WORK_ROW, first + k]] for k in range(GROUP)])

    def any_item(slot):
        code = lists_ref[WORK_ROW, slot]
        there = recv[jnp.maximum(code - 64, 0)]
        return jnp.where(code < 64, state[jnp.minimum(code, 63)], there)

    copies = exchange(send, recv, 0, False)
    own(0)
    for copy in copies:
        copy.wait()
    run(EARLY, [any_item(EARLY + k) for k in range(SPAN)])

    def answer(s):
        reply[s] = result[lists_ref[REPLY, s]]

    each(SLOTS, answer)
    copies = exchange(reply, back, 7, True)
    own(WORK - LATE)
    for copy in copies:
        copy.wait()

    def settle(i, columns):
        for j in columns:
            code = lists_ref[FINAL, i * 8 + j]
            here = state[jnp.minimum(code, 63)]
            there = back[jnp.clip(code - 64, 0, SLOTS - 1)]
            done = result[jnp.clip(code - 128, 0, WORK - 1)]
            put(i, j, jnp.where(code < 64, here, jnp.where(code < 128, there, done)))

    def sides(i, carry):
        settle(i, (0, 7))
        return carry

    def first_last(i, carry):
        settle(i * 7, range(1, 7))
        return carry

    def middle_rows(i, carry):
        settle(i, range(1, 7))
        row(i)
        return carry

    lax.fori_loop(0, 8, sides, 0)
    lax.fori_loop(0, 2, first_last, 0)
    border()
    lax.fori_loop(1, 7, middle_rows, 0)


def nothing(*_):
    return None


def into(out):
    def put(i, j, value):
        out[i * 8 + j] = value

    return put, nothing, nothing


STATE = (64, ROWS, 128)
MOVE_SCRATCH = [
    pltpu.VMEM((10, 10, ROWS, 128), F32),
    pltpu.VMEM((ROWS, 128), F32),
    pltpu.VMEM((2, ROWS, 128), F32),
    pltpu.SemaphoreType.DMA((6,)),
    pltpu.SemaphoreType.DMA((6,)),
]
CHEM_SCRATCH = [pltpu.VMEM((SLOTS, ROWS, 128), F32)] * 4 + [
    pltpu.VMEM((WORK, ROWS, 128), F32),
    pltpu.SemaphoreType.DMA((14,)),
    pltpu.SemaphoreType.DMA((14,)),
]


AGAIN_SCRATCH = [pltpu.VMEM((SLOTS, ROWS, 128), F32)] * 2 + [
    pltpu.SemaphoreType.DMA((14,)),
    pltpu.SemaphoreType.DMA((14,)),
]
FINAL_SCRATCH = [pltpu.VMEM(STATE, F32), pltpu.SemaphoreType.DMA((8,))]
COUNT_SCRATCH = [
    pltpu.VMEM((8, 8, 128), jnp.int32),
    pltpu.VMEM((16, 8, 128), jnp.int32),
    pltpu.SemaphoreType.DMA((22,)),
    pltpu.SemaphoreType.DMA((22,)),
    pltpu.VMEM((8, 128), jnp.int32),
    pltpu.SemaphoreType.DMA(()),
    pltpu.VMEM((2 * ROWS, 768), F32),
]


def others(axis):
    n = lax.axis_size(axis)
    return [shifted(axis, step) for step in sorted(range(1, n), key=lambda step: -min(step, n - step))]


def plane():
    far = (0, 1, 2, 1)
    steps = sorted(range(1, 16), key=lambda step: -far[step // 4] - far[step % 4])
    return [{**shifted("radial", step // 4), **shifted("azim", step % 4)} for step in steps]


def spread_counts(first, second, sems):
    stream, radial, azim = (lax.axis_index(axis) for axis in AXES)

    def stage(buffer, peers, start):
        copies = [remote(buffer, buffer, sems, start + k, p) for k, p in enumerate(peers)]
        for copy in copies:
            copy.start()

        def wait():
            for copy in copies:
                copy.wait()

        return wait

    def along_stream():
        return stage(first.at[stream], others("stream"), 0)

    def in_plane():
        row = lax.broadcasted_iota(jnp.int32, (8, 128), 0)
        joined = first[0]
        for s in range(1, 8):
            joined = jnp.where(row == s, first[s], joined)
        second[radial * 4 + azim] = joined
        return stage(second.at[radial * 4 + azim], plane(), 7)

    def whole():
        row = lax.broadcasted_iota(jnp.int32, (8, 128), 0)
        lane = lax.broadcasted_iota(jnp.int32, (8, 128), 1)
        total = jnp.zeros((8, 128), jnp.int32)
        for place in range(16):
            here = (lane & 15 == place) & (lane >> 4 == row)
            total = jnp.where(here, second[place], total)
        return jnp.broadcast_to(jnp.sum(total, 0, keepdims=True), (8, 128))

    return along_stream, in_plane, whole


def communicating(kernel, name, out_shape, out_specs, specs, args, scratch):
    return pl.pallas_call(
        kernel,
        out_shape=out_shape,
        in_specs=specs,
        out_specs=out_specs,
        scratch_shapes=scratch,
        compiler_params=pltpu.CompilerParams(
            collective_id=name, has_side_effects=True, vmem_limit_bytes=LIMIT
        ),
    )(*args)


def first_steps(both, blocks, tally, species, heat, courant, spread, settings):
    nrxn = settings[0].shape[1]
    padded = -(-nrxn // 16) * 16
    brought = (tally, species, heat, courant, spread, *settings, blocks)

    def kernel(*refs):
        anywhere, refs = refs[: len(brought)], refs[len(brought) :]
        out, lists, rates, sums, spread_out, flag = refs[:6]
        near, refs = refs[6 : 6 + len(brought)], refs[6 + len(brought) :]
        fetch_sem, refs = refs[0], refs[1:]
        tally_ref, species_ref, heat_ref, courant_ref, spread_ref, *settings_refs = near
        blocks_ref = settings_refs.pop()
        grid, edge, halo, *sems = refs[: len(MOVE_SCRATCH)]
        refs = refs[len(MOVE_SCRATCH) :]
        first, second, *count_sems = refs[:4]
        codes, code_sem, table = refs[4:7]
        moved, *refs = refs[7:]
        chem, refs = refs[: len(CHEM_SCRATCH)], refs[len(CHEM_SCRATCH) :]

        rows = [pl.ds(8 * i, 8) for i in range(8)]
        pairs = list(zip(anywhere, near))
        pairs[1:2] = [(anywhere[1].at[:, row], species_ref.at[:, row]) for row in rows]
        waits = fetch(pairs, fetch_sem)
        met = greet(others("stream") + plane())
        stream, radial, azim = (lax.axis_index(axis) for axis in AXES)
        me = (stream * 4 + radial) * 4 + azim
        waits[0]()
        own = jnp.sum(tally_ref[...], 1, keepdims=True)
        first[stream] = jnp.broadcast_to(own, (8, 128))
        stages = spread_counts(first, second, count_sems)
        met()
        waiting = [stages[0]()]
        waits[9]()
        for i, row in enumerate(rows):
            waits[1 + i]()
            cells = [species_ref[:, row], heat_ref[row][None], jnp.zeros((2, 8, 128), F32)]
            grid[i + 1, pl.ds(1, 8)] = jnp.swapaxes(jnp.concatenate(cells, 0), 0, 1)
        found = []

        def at_once():
            for wait in waits[10:]:
                wait()
            table[pl.ds(0, 1), pl.ds(0, 128)] = jnp.zeros((1, 128), F32)
            table[pl.ds(0, 1), pl.ds(0, 54)] = spread_ref[...].reshape(1, 54)
            row = lax.broadcasted_iota(jnp.int32, (ROWS, 128), 0)
            lane = lax.broadcasted_iota(jnp.int32, (ROWS, 128), 1)
            diagonal = jnp.where(row == lane, table[pl.ds(0, 1), pl.ds(0, 128)], 0.0)
            column = jnp.sum(diagonal, 1, keepdims=True)
            spread_out[...] = jnp.broadcast_to(column, (ROWS, 128))
            found.append(positions(blocks_ref))
            waiting[0]()
            waiting.append(stages[1]())
            prepare(*settings_refs, rates, sums, table)

        def at_end():
            waiting[1]()
            plan(me, stages[2](), found[0], blocks_ref, codes, lists, code_sem)
            flag[0] = lists[REST, 2]

        copies = face_copies(grid, edge, halo, sems)
        send_faces(copies)
        hooks = (at_once, nothing, at_end)
        transport(copies, courant_ref, spread_out, moved, grid, edge, halo, hooks)
        if not both:
            chemistry(lists, moved, rates, sums, into(out), *chem[:5], chem[5:], nothing)
            return
        grid, edge, halo, *sems = refs[: len(MOVE_SCRATCH)]
        refs = refs[len(MOVE_SCRATCH) :]
        recv, back, *again_sems = refs[: len(AGAIN_SCRATCH)]
        last, last_sem = refs[len(AGAIN_SCRATCH) :]
        copies = face_copies(grid, edge, halo, sems)

        def put(i, j, value):
            grid[i + 1, j + 1] = value

        places = (put, lambda: send_faces(copies), nothing)
        chemistry(lists, moved, rates, sums, places, *chem[:5], chem[5:], nothing)
        hooks = (nothing, nothing, nothing)
        transport(copies, courant_ref, spread_out, moved, grid, edge, halo, hooks)
        send, _, reply, _, result = chem[:5]
        again = (send, recv, reply, back, result, again_sems)

        def leave(i):
            row = pl.ds(8 * i, 8)
            return pltpu.make_async_copy(last.at[row], out.at[row], last_sem.at[i])

        def outer():
            leave(0).start()
            leave(7).start()

        places = (into(last)[0], outer, lambda i: leave(i).start())
        chemistry(lists, moved, rates, sums, places, *again, nothing)
        for i in range(8):
            leave(i).wait()

    smem, vmem = pl.BlockSpec(memory_space=pltpu.SMEM), pl.BlockSpec(memory_space=pltpu.VMEM)
    anywhere = pl.BlockSpec(memory_space=pl.ANY)
    return communicating(
        kernel,
        0 if both else 1,
        [
            jax.ShapeDtypeStruct(STATE, F32),
            jax.ShapeDtypeStruct((8, 128), jnp.int32),
            jax.ShapeDtypeStruct((2 * padded, 4 * ROWS), BF16),
            jax.ShapeDtypeStruct((4 * ROWS, 2 * padded), BF16),
            jax.ShapeDtypeStruct((ROWS, 128), F32),
            jax.ShapeDtypeStruct((1,), jnp.int32),
        ],
        [anywhere if both else vmem, smem, vmem, vmem, vmem, smem],
        [anywhere] * len(brought),
        brought,
        [pltpu.VMEM(x.shape, x.dtype) for x in brought[:-1]]
        + [pltpu.SMEM(blocks.shape, blocks.dtype)]
        + [pltpu.SemaphoreType.DMA((7 + len(brought),))]
        + MOVE_SCRATCH
        + COUNT_SCRATCH
        + [pltpu.VMEM(STATE, F32)]
        + CHEM_SCRATCH
        + (MOVE_SCRATCH + AGAIN_SCRATCH + FINAL_SCRATCH if both else []),
    )


def second_step(lists, state, courant, spread, rates, sums):
    brought = (courant, spread, rates, sums)

    def kernel(lists_ref, state_any, *refs):
        anywhere, refs = refs[: len(brought)], refs[len(brought) :]
        out, near, refs = refs[0], refs[1 : 1 + len(brought)], refs[1 + len(brought) :]
        fetch_sem, refs = refs[0], refs[1:]
        courant_ref, spread_ref, rates_ref, sums_ref = near
        grid, edge, halo, *sems = refs[: len(MOVE_SCRATCH)]
        moved, *chem = refs[len(MOVE_SCRATCH) :]
        met = greet(faces() + [shifted("stream", 2), shifted("stream", -2)])
        pairs = [
            (state_any.at[pl.ds(8 * i, 8)], grid.at[i + 1, pl.ds(1, 8)]) for i in range(8)
        ]
        waits = fetch(pairs + list(zip(anywhere, near)), fetch_sem)
        for wait in waits:
            wait()
        met()
        copies = face_copies(grid, edge, halo, sems)
        send_faces(copies)
        hooks = (nothing, nothing, nothing)
        transport(copies, courant_ref, spread_ref, moved, grid, edge, halo, hooks)
        chemistry(lists_ref, moved, rates_ref, sums_ref, into(out), *chem[:5], chem[5:], nothing)

    smem, vmem = pl.BlockSpec(memory_space=pltpu.SMEM), pl.BlockSpec(memory_space=pltpu.VMEM)
    return communicating(
        kernel,
        2,
        jax.ShapeDtypeStruct(STATE, F32),
        vmem,
        [smem] + [pl.BlockSpec(memory_space=pl.ANY)] * 5,
        (lists, state, *brought),
        [pltpu.VMEM(x.shape, x.dtype) for x in brought]
        + [pltpu.SemaphoreType.DMA((8 + len(brought),))]
        + MOVE_SCRATCH
        + [pltpu.VMEM(STATE, F32)]
        + CHEM_SCRATCH,
    )


def shards(
    component_fractions,
    kilokelvin_field,
    axial_courant_number,
    spreading_number,
    arrhenius_multiplier_exponent,
    thermal_exponents,
    arrhenius_barrier,
    balance_constant_exponents,
    enthalpy_formation,
    consumed_stoich_matrix,
    yield_stoich_matrix,
    processor_tiles_burning,
    tile_transfer_tally,
):
    shape = component_fractions.shape
    settings = (
        consumed_stoich_matrix,
        yield_stoich_matrix,
        arrhenius_multiplier_exponent,
        thermal_exponents,
        arrhenius_barrier,
        balance_constant_exponents,
        enthalpy_formation,
    )
    species = component_fractions.reshape(53, 64, 128)
    heat = kilokelvin_field.reshape(64, 128)
    courant = axial_courant_number.reshape(64, 128)
    blocks, tally = processor_tiles_burning, tile_transfer_tally
    inputs = (blocks, tally, species, heat, courant, spreading_number, settings)
    state, lists, rates, sums, _, flag = first_steps(True, *inputs)

    def balanced(state, lists, rates, sums):
        return finish(lists, blocks, state, rates, sums)

    def with_rest(state, lists, rates, sums):
        state, lists, rates, sums, spread, _ = first_steps(False, *inputs)
        state = react_rest(lists, blocks, state, rates, sums)
        state = second_step(lists, state, courant, spread, rates, sums)
        return finish(lists, blocks, state, rates, sums)

    over = flag.reshape(()) > 0
    species, heat = lax.cond(over, with_rest, balanced, state, lists, rates, sums)
    return species.reshape(shape), heat.reshape(shape[1:])


def solution(mesh):
    in_specs = (
        P(None, "stream", "radial", "azim"),
        P("stream", "radial", "azim"),
        P("stream", "radial", "azim"),
        P(),
        P(),
        P(),
        P(),
        P(),
        P(),
        P(),
        P(),
        P(AXES, None),
        P(AXES, None),
    )
    out_specs = (P(None, "stream", "radial", "azim"), P("stream", "radial", "azim"))
    return jax.shard_map(shards, mesh=mesh, in_specs=in_specs, out_specs=out_specs, check_vma=False)
```
